128 devices in a mesh: ctx: 16 (over z, y), fsdp: 8 (over x, core).
Axes of the slice: x: 4, y: 4, z: 4, core: 2. Of those that a mesh axis runs over, the one named last changes fastest.
Arguments:
- tokens: bfloat16 [8, 2048, 1536], P('fsdp', 'ctx'), may hold values from -6 to 6
- cotangent: bfloat16 [8, 2048, 1536], P('fsdp', 'ctx'), may hold values from -6 to 6
- lengths: int32 [8], P('fsdp'), may hold values from 512 to 2048, as said below
- block_map: int32 [32], replicated, may hold values from 0 to 31, each once
- norm_gain: bfloat16 [1536], P('fsdp'), may hold values from 0.5 to 1.5
- w_query: bfloat16 [1536, 1536], P('fsdp'), may hold values from -0.15625 to 0.15625
- w_key: bfloat16 [1536, 1536], P('fsdp'), may hold values from -0.15625 to 0.15625
- w_value: bfloat16 [1536, 1536], P('fsdp'), may hold values from -0.15625 to 0.15625
- w_forget: bfloat16 [1536, 24], P('fsdp'), may hold values from -0.15625 to 0.15625
- forget_bias: bfloat16 [24], P('fsdp'), may hold values from 2 to 8
- w_outgate: bfloat16 [1536, 1536], P('fsdp'), may hold values from -0.15625 to 0.15625
- w_output: bfloat16 [1536, 1536], P('fsdp'), may hold values from -0.625 to 0.625
- ffn_gain: bfloat16 [1536], P('fsdp'), may hold values from 0.5 to 1.5
- w_gate: bfloat16 [1536, 4096], P('fsdp'), may hold values from -0.15625 to 0.15625
- w_up: bfloat16 [1536, 4096], P('fsdp'), may hold values from -0.15625 to 0.15625
- w_down: bfloat16 [4096, 1536], P('fsdp'), may hold values from -0.09375 to 0.09375
Outputs:
- mixed: bfloat16 [8, 2048, 1536], P('fsdp', 'ctx')
- tokens_grad: bfloat16 [8, 2048, 1536], P('fsdp', 'ctx')
- norm_gain_grad: float32 [1536], P('fsdp')
- w_query_grad: float32 [1536, 1536], P('fsdp')
- w_key_grad: float32 [1536, 1536], P('fsdp')
- w_value_grad: float32 [1536, 1536], P('fsdp')
- w_forget_grad: float32 [1536, 24], P('fsdp')
- forget_bias_grad: float32 [24], P('fsdp')
- w_outgate_grad: float32 [1536, 1536], P('fsdp')
- w_output_grad: float32 [1536, 1536], P('fsdp')
- ffn_gain_grad: float32 [1536], P('fsdp')
- w_gate_grad: float32 [1536, 4096], P('fsdp')
- w_up_grad: float32 [1536, 4096], P('fsdp')
- w_down_grad: float32 [4096, 1536], P('fsdp')
The draws below stay inside these ranges and needn't reach their ends.
Inputs may be any that keep to these rules, and one draw needn't show every extreme that they name: `lengths`: each slot's sequence fills its first global positions; some slot is exactly 2048 long and another a quarter of 2048. A permutation: storage block b of every slot holds global block block_map[b].
All inputs are finite; a program needn't handle non-finite values.
Results may differ from the reference program's by a relative error of at most 0.023.
Values may be sent and summed in bfloat16 or wider, within the bound.
No kernel may reach another device: no remote copies, remote signals or barrier semaphores. Data moves between devices by JAX's collectives and lax.ppermute only.
A program may use at most 320 MiB of HBM per device.

```python
import math
import jax
import jax.numpy as jnp
from jax import lax

D = 1536
H = 24
HD = 64
FF = 4096
BLK = 64
NBLK = 32
SLOT_LEN = 2048
SLOTS = 8


def draw_lengths(key, part):
    order = jax.random.permutation(jax.random.fold_in(key, 11), SLOTS)
    spread = jax.random.randint(jax.random.fold_in(key, 12), (SLOTS,), SLOT_LEN // 4, SLOT_LEN + 1)
    spread = jnp.where(order == 0, SLOT_LEN, spread)
    spread = jnp.where(order == 1, SLOT_LEN // 4, spread)
    return spread.astype(jnp.int32)


def levels(own_key, shape, cuts, smallest, top_value):
    level = 1.0
    for dim, blocks in cuts:
        draws = jax.random.uniform(jax.random.fold_in(jax.random.fold_in(own_key, 6), dim), (blocks,), jnp.float32, smallest / len(cuts), top_value / len(cuts))
        level = level * jnp.repeat(jnp.exp(draws), shape[dim] // blocks).reshape((-1,) + (1,) * (len(shape) - 1 - dim))
    return level


def normal_values(key, dims, scale, limit, pieces=(), held_as=jnp.bfloat16):
    values = scale * jax.random.normal(key, dims, jnp.float32)
    if pieces:
        values = values * levels(key, dims, pieces, -0.22, 0.18)
    return jnp.clip(values, -limit, limit).astype(held_as)


def setup_inputs(seed: int = 0) -> dict:
    seeds = jax.random.split(jax.random.key(seed), 17)
    tokens = normal_values(seeds[0], (SLOTS, SLOT_LEN, D), 1.0, 6.0, ((0, 8), (1, 16)))
    cotangent = normal_values(seeds[1], (SLOTS, SLOT_LEN, D), 1.0, 6.0, ((0, 8), (1, 16)))
    lengths = draw_lengths(jax.random.fold_in(seeds[16], 71), 0)
    block_map = jax.random.permutation(seeds[3], NBLK).astype(jnp.int32)
    norm_gain = jnp.clip(1.0 + 0.1 * jax.random.normal(seeds[4], (D,), jnp.float32), 0.5, 1.5).astype(jnp.bfloat16)
    w_query = normal_values(seeds[5], (D, D), D ** -0.5, 0.15625, ((0, 8),))
    w_key = normal_values(seeds[6], (D, D), D ** -0.5, 0.15625, ((0, 8),))
    w_value = normal_values(seeds[7], (D, D), D ** -0.5, 0.15625, ((0, 8),))
    w_forget = normal_values(seeds[8], (D, H), D ** -0.5, 0.15625, ((0, 8),))
    forget_bias = jnp.clip(2.0 + 6.0 * jax.random.uniform(seeds[9], (H,), jnp.float32) ** levels(seeds[9], (H,), ((0, 8),), -0.2, 0.2), 2.0, 8.0).astype(jnp.bfloat16)
    w_outgate = normal_values(seeds[10], (D, D), D ** -0.5, 0.15625, ((0, 8),))
    w_output = normal_values(seeds[11], (D, D), (D // 16) ** -0.5, 0.625, ((0, 8),))
    ffn_gain = jnp.clip(1.0 + 0.1 * jax.random.normal(seeds[12], (D,), jnp.float32), 0.5, 1.5).astype(jnp.bfloat16)
    w_gate = normal_values(seeds[13], (D, FF), D ** -0.5, 0.15625, ((0, 8),))
    w_up = normal_values(seeds[14], (D, FF), D ** -0.5, 0.15625, ((0, 8),))
    w_down = normal_values(seeds[15], (FF, D), FF ** -0.5, 0.09375, ((0, 8),))
    return {"tokens": tokens, "cotangent": cotangent, "lengths": lengths, "block_map": block_map, "norm_gain": norm_gain, "w_query": w_query, "w_key": w_key, "w_value": w_value, "w_forget": w_forget, "forget_bias": forget_bias, "w_outgate": w_outgate, "w_output": w_output, "ffn_gain": ffn_gain, "w_gate": w_gate, "w_up": w_up, "w_down": w_down}


@jax.custom_vjp
def low(v):
    return lax.optimization_barrier(v.astype(jnp.bfloat16)).astype(jnp.float32)

@jax.custom_vjp
def low_back(v):
    return v

def low_keep(v):
    return (low(v), None)

def low_pass(kept, grad):
    return (grad,)

def back_keep(v):
    return (v, None)

def back_low(kept, grad):
    return (low(grad),)
low.defvjp(low_keep, low_pass)
low_back.defvjp(back_keep, back_low)
EPS = 1e-06
NEG = -1e+30
HIGH = lax.Precision.HIGHEST

def matmul(left, right):
    return jnp.dot(left, right, precision=HIGH)

def rms_norm(values, gain):
    return values * lax.rsqrt(lax.optimization_barrier(jnp.mean(values * values, -1, keepdims=True)) + EPS) * gain[None, :]

def attend(queries, keys, values, decay):
    span = queries.shape[0]
    width = math.gcd(span, 512)
    count = span // width
    scale = 1.0 / math.sqrt(HD)
    key_heads = keys.reshape(span, H, HD)
    value_heads = values.reshape(span, H, HD)
    positions = jnp.arange(span, dtype=jnp.int32)

    def portion(items):
        query_block, decay_block, pos_block = items
        scored = jnp.einsum('qhd,khd->hqk', query_block, key_heads, precision=HIGH) * scale
        scored = scored + decay_block.T[:, :, None] - decay.T[:, None, :]
        scored = low_back(scored)
        scored = jnp.where((pos_block[:, None] >= positions[None, :])[None], scored, NEG)
        probs = low(jax.nn.softmax(scored, -1))
        return low_back(jnp.einsum('hqk,khd->qhd', probs, value_heads, precision=HIGH))
    result = lax.map(jax.checkpoint(portion), (queries.reshape(count, width, H, HD), decay.reshape(count, width, H), positions.reshape(count, width)))
    return result.reshape(span, H * HD)

def forward(inputs, weights, live):
    gain_first, w_q, w_k, w_v, w_f, b_f, w_g, w_o, gain_second, w_gt, w_u, w_d = weights
    normed = low(rms_norm(inputs, gain_first))
    queries = low_back(low(matmul(normed, w_q)))
    keys = low_back(low(matmul(normed, w_k)))
    values = low_back(low(matmul(normed, w_v)))
    forget_pre = low_back(matmul(normed, w_f) + b_f[None, :])
    log_keep = low(jax.nn.log_sigmoid(forget_pre))
    decay = jnp.cumsum(log_keep, 0)
    gate_logit = low_back(matmul(normed, w_g))
    attended = attend(queries, keys, values, decay)
    mixed_in = low(attended * jax.nn.sigmoid(gate_logit))
    residual = inputs + low_back(matmul(mixed_in, w_o))
    normed_two = low(rms_norm(residual, gain_second))
    gate_pre = low_back(matmul(normed_two, w_gt))
    up_pre = low_back(matmul(normed_two, w_u))
    hidden = low(jax.nn.silu(gate_pre) * up_pre)
    ffn_out = low_back(matmul(hidden, w_d))
    return live[:, None] * (residual + ffn_out)

def reference(tokens, cotangent, lengths, block_map, norm_gain, w_query, w_key, w_value, w_forget, forget_bias, w_outgate, w_output, ffn_gain, w_gate, w_up, w_down):
    weights = tuple((w.astype(jnp.float32) for w in (norm_gain, w_query, w_key, w_value, w_forget, forget_bias, w_outgate, w_output, ffn_gain, w_gate, w_up, w_down)))
    block_count = block_map.shape[0]
    inverse = jnp.argsort(block_map).astype(jnp.int32)
    order = block_map.astype(jnp.int32)

    def to_global(array):
        return jnp.take(array.reshape(block_count, BLK, -1), inverse, axis=0).reshape(SLOT_LEN, -1)

    def to_store(array):
        return jnp.take(array.reshape(block_count, BLK, -1), order, axis=0).reshape(SLOT_LEN, -1)
    zero_grads = tuple((jnp.zeros(w.shape, jnp.float32) for w in weights))

    def per_slot(running, items):
        slot_tokens, slot_cot, length = items
        inputs = to_global(slot_tokens.astype(jnp.float32))
        upstream = to_global(slot_cot.astype(jnp.float32))
        live = (jnp.arange(SLOT_LEN, dtype=jnp.int32) < length).astype(jnp.float32)
        result, pull = jax.vjp(lambda values, params: forward(values, params, live), inputs, weights)
        input_grad, weight_grads = pull(upstream)
        running = tuple((a + b for a, b in zip(running, weight_grads)))
        return (running, (to_store(result).astype(jnp.bfloat16), to_store(input_grad).astype(jnp.bfloat16)))
    grads, (mixed, tokens_grad) = lax.scan(per_slot, zero_grads, (tokens, cotangent, lengths))
    return (mixed, tokens_grad, grads[0], grads[1], grads[2], grads[3], grads[4], grads[5], grads[6], grads[7], grads[8], grads[9], grads[10], grads[11])
```

```python
import jax
import jax.numpy as jnp
from jax import lax
from jax.experimental import pallas as pl
from jax.experimental.pallas import tpu as pltpu
from jax.sharding import PartitionSpec as P

EPS = 1e-06
NEG = -1e30
HD = 64
QB = 256
SPAN = 2048
SHARED = ((0, 3, 4, 7), (1, 2, 5, 6))
F32 = jnp.float32
BF16 = jnp.bfloat16
HIGH = lax.Precision.HIGHEST
NN = (((1,), (0,)), ((), ()))
NT = (((1,), (1,)), ((), ()))
TN = (((0,), (0,)), ((), ()))
MIB = 2**20
SMEM = pl.BlockSpec(memory_space=pltpu.SMEM)
VMEM = pl.BlockSpec(memory_space=pltpu.VMEM)
ANY = pl.BlockSpec(memory_space=pl.ANY)
BOTH = ("ctx", "fsdp")


def dot(a, b, dims=NN):
    return lax.dot_general(a, b, dims, preferred_element_type=F32)


def shape(*dims, dtype=BF16):
    return jax.ShapeDtypeStruct(dims, dtype)


def call(kernel, outs, name, args, scratch=(), ins=None, flops=10**9, moved=10**7, limit=60):
    return pl.pallas_call(
        kernel,
        grid=(1,),
        out_shape=outs,
        in_specs=ins or [VMEM] * len(args),
        out_specs=jax.tree.map(lambda _: VMEM, outs),
        scratch_shapes=list(scratch),
        compiler_params=pltpu.CompilerParams(vmem_limit_bytes=limit * MIB),
        cost_estimate=pl.CostEstimate(flops=flops, bytes_accessed=moved, transcendentals=0),
        name=name,
    )(*args)


def pack_kernel(wq, wk, wv, wf, g1, g2, out):
    lane = lax.broadcasted_iota(jnp.int32, (192, 64), 1)
    rows = jnp.concatenate(
        [g1[...].astype(F32), g2[...].astype(F32), jnp.zeros((6, 192), F32)], 0
    ).T
    base = jnp.where(lane == 3, rows[:, 0:1], jnp.where(lane == 4, rows[:, 1:2], 0.0))
    forget = wf[...].astype(F32)
    for d in range(8):
        parts = []
        for h in range(3):
            at = d * 192 + h * 64
            parts += [wq[:, at : at + 64], wk[:, at : at + 64], wv[:, at : at + 64]]
        ext = base
        for h in range(3):
            ext = jnp.where(lane == h, forget[:, 3 * d + h : 3 * d + h + 1], ext)
        parts.append(ext.astype(BF16))
        for m in range(5):
            out[d, :, m * 128 : (m + 1) * 128] = jnp.concatenate(
                [parts[2 * m], parts[2 * m + 1]], 1
            )


def pack_two_kernel(f_ref, wg, wu, wo, *refs):
    outs, all_s = refs[:8], refs[8]
    for d in range(8):
        all_s[d, :, 0:512] = wg[:, d * 512 : (d + 1) * 512]
        all_s[d, :, 512:1024] = wu[:, d * 512 : (d + 1) * 512]
        at = d * 192
        heads = [wo[:, at + h * 64 : at + h * 64 + 64] for h in range(3)]
        all_s[d, :, 1024:1152] = jnp.concatenate([heads[0], heads[1]], 1)
        all_s[d, :, 1152:1280] = jnp.concatenate([heads[1], heads[2]], 1)
    for k in range(8):
        outs[k][...] = all_s[lax.rem(f_ref[0] + k, 8)]


def place_kernel(f_ref, n1, *refs):
    ins, w2, sig = refs[:8], refs[8], refs[9]
    for k in range(8):
        at = pl.multiple_of(lax.rem(f_ref[0] + 8 - k, 8) * 192, 64)
        w2[pl.ds(at, 192), :] = ins[k][...]
    sig[...] = jax.nn.sigmoid(dot(n1[...], w2[:, 1024:1280]))


def mask_kernel(live, c, _n1, out):
    keep = live[:, 0:1] > 0.5
    out[...] = jnp.where(keep, c[...].astype(F32), 0.0).astype(BF16)


def proj_kernel(x, w1, bias, _part, n1, send, fpre, gains):
    gains[...] = w1[:, 512:640].astype(F32).T[64:72]
    x32 = x[...].astype(F32)
    r1 = lax.rsqrt(jnp.mean(x32 * x32, -1, keepdims=True) + EPS)
    normed = (x32 * r1 * gains[3:4]).astype(BF16)
    n1[...] = normed
    proj = dot(normed, w1[...])
    rows = proj[:, 512:640].T[64:72] + bias[...]
    fpre[...] = rows
    logs = jnp.minimum(rows, 0.0) - jnp.log1p(jnp.exp(-jnp.abs(rows)))
    low = proj[:, 0:576].astype(BF16)
    for s in range(4):
        for j in range(2):
            send[2 * s + j, 0:128, :] = low[s * 128 : (s + 1) * 128, j * 192 : j * 192 + 384]
            line = jnp.concatenate(
                [
                    logs[j : j + 1, s * 128 : (s + 1) * 128],
                    logs[j + 1 : j + 2, s * 128 : (s + 1) * 128],
                    jnp.zeros((1, 128), F32),
                ],
                1,
            )
            send[2 * s + j, 128:144, :] = jnp.broadcast_to(line, (16, 384)).astype(BF16)


def project(x_all, w1, bias, after):
    def fixed(*dims):
        return pl.BlockSpec(dims, lambda i: (0,) * len(dims))

    return pl.pallas_call(
        proj_kernel,
        grid=(2,),
        out_shape=(
            shape(1024, 1536),
            shape(16, 144, 384),
            shape(8, 1024, dtype=F32),
            shape(8, 1536, dtype=F32),
        ),
        in_specs=[
            pl.BlockSpec((512, 1536), lambda i: (i, 0)),
            fixed(1536, 640),
            fixed(8, 1),
            ANY,
        ],
        out_specs=(
            pl.BlockSpec((512, 1536), lambda i: (i, 0)),
            pl.BlockSpec((8, 144, 384), lambda i: (i, 0, 0)),
            pl.BlockSpec((8, 512), lambda i: (0, i)),
            fixed(8, 1536),
        ),
        compiler_params=pltpu.CompilerParams(vmem_limit_bytes=40 * MIB),
        cost_estimate=pl.CostEstimate(
            flops=2 * 10**9, bytes_accessed=10**7, transcendentals=0
        ),
        name="project",
    )(x_all, w1, bias, after)


def score_cols(hs, b, q_s, k_s, fc_s, fr):
    n = (b + 1) * QB
    q0 = b * QB
    qq = q_s[hs, q0 : q0 + QB, :]
    cols = dot(k_s[hs, 0:n, :], qq, NT)
    bias = fr[hs, :, q0 : q0 + 1] - fc_s[hs, 0:n, :]
    cols = cols + bias
    keep = lax.broadcasted_iota(jnp.int32, (QB, QB), 0) <= lax.broadcasted_iota(
        jnp.int32, (QB, QB), 1
    )
    tail = jnp.where(keep, cols[n - QB : n], NEG)
    if b:
        cols = jnp.concatenate([cols[: n - QB], tail], 0)
    else:
        cols = tail
    return cols, qq, n, q0


def run_units(j, unit):
    for b in range(SPAN // QB):
        unit(j, b)
    for half in range(2):

        @pl.when(j == half)
        def _():
            for b in SHARED[half]:
                unit(1 - half, b)


def load_heads(bm_ref, r1, q_s, k_s, v_s):
    for blk in range(32):
        at = pl.multiple_of(bm_ref[blk] * 64, 64)
        c, r = divmod(blk, 2)
        for hs in range(2):
            part = r1[c, r * 64 : (r + 1) * 64, hs * 192 : (hs + 1) * 192]
            q_s[hs, pl.ds(at, 64), :] = (part[:, 0:64].astype(F32) * 0.125).astype(BF16)
            k_s[hs, pl.ds(at, 64), :] = part[:, 64:128]
            v_s[hs, pl.ds(at, 64), :] = part[:, 128:192]


def column_decay(fr, fc_s):
    both = jnp.concatenate([fr[0], fr[1], jnp.zeros((6, SPAN), F32)], 0).T
    fc_s[0] = both[:, 0:1]
    fc_s[1] = both[:, 1:2]


def fwd_kernel(bm_ref, j_ref, r1, fr, _a, _b, _c, o_ref, attn_ref, l_ref, q_s, k_s, v_s, vt_s, fc_s, o_s):
    j = j_ref[0]
    load_heads(bm_ref, r1, q_s, k_s, v_s)
    column_decay(fr, fc_s)
    for hs in range(2):
        vt_s[hs, 0:64, :] = v_s[hs].astype(F32).T.astype(BF16)
        vt_s[hs, 64:80, :] = jnp.ones((16, SPAN), BF16)
        o_s[hs] = jnp.zeros((SPAN, HD), BF16)

    def unit(hs, b):
        cols, _, n, q0 = score_cols(hs, b, q_s, k_s, fc_s, fr)
        top = jnp.max(cols, 0, keepdims=True)
        probs = jnp.exp(cols - top).astype(BF16)
        acc = dot(vt_s[hs, :, 0:n], probs)
        total = acc[64:65]
        rows = (acc[0:64] / total).T
        attn_ref[hs, q0 : q0 + QB, :] = rows
        l_ref[hs, :, q0 : q0 + QB] = top + jnp.log(total)
        o_s[hs, q0 : q0 + QB, :] = rows.astype(BF16)

    run_units(j, unit)
    for blk in range(32):
        at = pl.multiple_of(bm_ref[blk] * 64, 64)
        c, r = divmod(blk, 2)
        o_ref[c, r * 64 : (r + 1) * 64, :] = jnp.concatenate(
            [o_s[0, pl.ds(at, 64), :], o_s[1, pl.ds(at, 64), :]], 1
        )


def suffix_sums(row, dl_s, hs):
    grid = jnp.concatenate([row[:, b * 64 : (b + 1) * 64] for b in range(32)], 0)
    tri = lax.broadcasted_iota(jnp.int32, (64, 64), 0) >= lax.broadcasted_iota(
        jnp.int32, (64, 64), 1
    )
    within = jnp.dot(grid, tri.astype(F32), precision=HIGH, preferred_element_type=F32)
    total = jnp.broadcast_to(within[:, 0:1], (32, 64))
    later = lax.broadcasted_iota(jnp.int32, (32, 32), 0) < lax.broadcasted_iota(
        jnp.int32, (32, 32), 1
    )
    dl_s[hs] = within + jnp.dot(
        later.astype(F32), total, precision=HIGH, preferred_element_type=F32
    )


def bwd_kernel(
    bm_ref, j_ref, r1, da_r, attn_ref, l_ref, fr, go,
    ds_ref,
    q_s, k_s, v_s, da_s, kt_s, fc_s, dk_s, dv_s, out_s, rs_ref, dl_s,
):
    j = j_ref[0]
    for c in range(16):
        ds_ref[c, 144:192, :] = go[c]
    load_heads(bm_ref, r1, q_s, k_s, v_s)
    column_decay(fr, fc_s)
    for blk in range(32):
        at = pl.multiple_of(bm_ref[blk] * 64, 64)
        c, r = divmod(blk, 2)
        part = da_r[c, r * 64 : (r + 1) * 64, :]
        for hs in range(2):
            da_s[hs, pl.ds(at, 64), :] = part[:, hs * 64 : (hs + 1) * 64]
    for hs in range(2):
        kt_s[hs, 0:64, :] = k_s[hs].astype(F32).T.astype(BF16)
        kt_s[hs, 64:80, :] = jnp.ones((16, SPAN), BF16)
        dk_s[hs] = jnp.zeros((SPAN, 128), F32)
        dv_s[hs] = jnp.zeros((SPAN, HD), F32)
        out_s[hs] = jnp.zeros((SPAN, 192), BF16)
        rs_ref[hs] = jnp.zeros((1, SPAN), F32)

    def unit(hs, b):
        cols, qq, n, q0 = score_cols(hs, b, q_s, k_s, fc_s, fr)
        datt = da_s[hs, q0 : q0 + QB, :]
        attn = attn_ref[hs, q0 : q0 + QB, :]
        delta = jnp.sum((datt.astype(F32) * attn).T, 0, keepdims=True)
        probs = jnp.exp(cols - l_ref[hs, :, q0 : q0 + QB])
        dv_s[hs, 0:n, :] += dot(probs.astype(BF16), datt)
        back = dot(v_s[hs, 0:n, :], datt, NT)
        dscore = (probs * (back - delta)).astype(BF16)
        wide = jnp.concatenate([qq, jnp.ones((QB, HD), BF16)], 1)
        dk_s[hs, 0:n, :] += dot(dscore, wide)
        dq = dot(kt_s[hs, :, 0:n], dscore)
        rs_ref[hs, :, q0 : q0 + QB] = dq[64:65]
        out_s[hs, q0 : q0 + QB, 0:64] = (dq[0:64].T * 0.125).astype(BF16)

    run_units(j, unit)
    for hs in range(2):
        both = dk_s[hs]
        suffix_sums(rs_ref[hs] - both.T[64:65], dl_s, hs)
        out_s[hs, :, 64:128] = both[:, 0:64].astype(BF16)
        out_s[hs, :, 128:192] = dv_s[hs].astype(BF16)
    for blk in range(32):
        at = pl.multiple_of(bm_ref[blk] * 64, 64)
        c, r = divmod(blk, 2)
        ds_ref[c, r * 64 : (r + 1) * 64, :] = jnp.concatenate(
            [out_s[0, pl.ds(at, 64), :], out_s[1, pl.ds(at, 64), :]], 1
        )
    for c in range(16):
        lines = [
            dl_s[hs, pl.ds(bm_ref[2 * c + r], 1), :] for hs in range(2) for r in range(2)
        ]
        line = jnp.concatenate(lines + [jnp.zeros((1, 128), F32)], 1)
        ds_ref[c, 128:144, :] = jnp.broadcast_to(line, (16, 384)).astype(BF16)


HEADS = [pltpu.VMEM((2, SPAN, HD), BF16)] * 3


def attend(block_map, j, r1, decay, after):
    return call(
        fwd_kernel,
        (shape(16, 128, 128), shape(2, SPAN, HD, dtype=F32), shape(2, 1, SPAN, dtype=F32)),
        "attend",
        (block_map, j, r1, decay, *after),
        HEADS
        + [
            pltpu.VMEM((2, 80, SPAN), BF16),
            pltpu.VMEM((2, SPAN, 1), F32),
            pltpu.VMEM((2, SPAN, HD), BF16),
        ],
        [SMEM, SMEM, VMEM, VMEM, ANY, ANY, ANY],
        flops=4 * 10**9,
    )


def attend_back(block_map, j, r1, upstream, attn, logs, decay, go):
    return call(
        bwd_kernel,
        shape(16, 192, 384),
        "attend_back",
        (block_map, j, r1, upstream, attn, logs, decay, go),
        HEADS
        + [
            pltpu.VMEM((2, SPAN, HD), BF16),
            pltpu.VMEM((2, 80, SPAN), BF16),
            pltpu.VMEM((2, SPAN, 1), F32),
            pltpu.VMEM((2, SPAN, 128), F32),
            pltpu.VMEM((2, SPAN, HD), F32),
            pltpu.VMEM((2, SPAN, 192), BF16),
            pltpu.VMEM((2, 1, SPAN), F32),
            pltpu.VMEM((2, 32, 64), F32),
        ],
        [SMEM, SMEM] + [VMEM] * 6,
        flops=10**10,
    )


def mid_kernel(o_r, wo, x, gains, h_ref, n2_ref, r2_ref):
    acc = x[...].astype(F32)
    for f in range(8):
        at = f * 192
        acc += dot(o_r[f, :, 0:128], wo[at : at + 128, :])
        acc += dot(o_r[f, :, 128:256], wo[at + 64 : at + 192, :])
    h_ref[...] = acc
    r2 = lax.rsqrt(jnp.mean(acc * acc, -1, keepdims=True) + EPS)
    r2_ref[...] = jnp.broadcast_to(r2, (128, 128))
    n2_ref[...] = (acc * r2 * gains[4:5]).astype(BF16)


def mid_back_kernel(
    dn2_r, h_ref, r2_ref, c_ref, gains, wo, _a, _b, _c, _d,
    dh_ref, da_ref, do_ref, g2_ref,
):
    h = h_ref[...]
    r2 = r2_ref[:, 0:1]
    dn2 = dn2_r[...].astype(F32)
    g2_ref[...] = jnp.sum(dn2 * h * r2, 0, keepdims=True)
    scaled = dn2 * gains[4:5]
    dh = (
        c_ref[...].astype(F32)
        + r2 * scaled
        - h * (r2 * r2 * r2) * jnp.mean(scaled * h, -1, keepdims=True)
    )
    dh_ref[...] = dh
    da = dh.astype(BF16)
    da_ref[...] = da
    for f in range(8):
        at = f * 192
        do_ref[f, :, 0:128] = dot(da, wo[at : at + 128, :], NT).astype(BF16)
        do_ref[f, :, 128:256] = dot(da, wo[at + 64 : at + 192, :], NT).astype(BF16)


def ffn_kernel(n2, c, w2, wd, dn2_ref, ffo_ref, u_ref, dpre_ref):
    pre = dot(n2[...], w2[:, 0:1024])
    gate, up = pre[:, 0:512], pre[:, 512:1024]
    sig = jax.nn.sigmoid(gate)
    act = gate * sig
    u = (act * up).astype(BF16)
    u_ref[...] = u
    du = dot(c[...], wd[...], NT)
    dgate = (du * up * (sig * (1.0 + gate * (1.0 - sig)))).astype(BF16)
    dup = (du * act).astype(BF16)
    dpre = jnp.concatenate([dgate, dup], 1)
    dpre_ref[...] = dpre
    dn2_ref[...] = dot(dpre, w2[:, 0:1024], NT).astype(BF16)
    ffo_ref[...] = dot(u, wd[...]).astype(BF16)


def feed_forward(n2, c_all, w2, wd):
    rows = 256
    return pl.pallas_call(
        ffn_kernel,
        grid=(1024 // rows,),
        out_shape=(
            shape(1024, 1536),
            shape(1024, 1536),
            shape(1024, 512),
            shape(1024, 1024),
        ),
        in_specs=[
            pl.BlockSpec((rows, 1536), lambda i: (i, 0)),
            pl.BlockSpec((rows, 1536), lambda i: (i, 0)),
            pl.BlockSpec((1536, 1280), lambda i: (0, 0)),
            pl.BlockSpec((512, 1536), lambda i: (0, 0)),
        ],
        out_specs=(
            pl.BlockSpec((rows, 1536), lambda i: (i, 0)),
            pl.BlockSpec((rows, 1536), lambda i: (i, 0)),
            pl.BlockSpec((rows, 512), lambda i: (i, 0)),
            pl.BlockSpec((rows, 1024), lambda i: (i, 0)),
        ),
        compiler_params=pltpu.CompilerParams(vmem_limit_bytes=48 * MIB),
        cost_estimate=pl.CostEstimate(
            flops=10**10, bytes_accessed=2 * 10**7, transcendentals=0
        ),
        name="feed_forward",
    )(n2, c_all, w2, wd)


HALF = 576


def ffn_grad_kernel(zy_ref, n2, dpre, u, c, *refs):
    outs, all_s = refs[:8], refs[8]
    for part in range(4):
        g = dot(n2[:, part * 384 : (part + 1) * 384], dpre[...], TN).astype(BF16)
        for sub in range(2):
            f = 2 * part + sub
            for cr in range(4):
                for col in range(8):
                    cc, half = divmod(col, 2)
                    at = f * 96 + half * 48
                    all_s[cr * 4 + cc, at : at + 48, :] = g[
                        sub * 192 + cr * 48 : sub * 192 + cr * 48 + 48,
                        col * 128 : (col + 1) * 128,
                    ]
    for part in range(4):
        g = dot(u[:, part * 128 : (part + 1) * 128], c[...], TN).astype(BF16)
        for sub in range(4):
            for col in range(12):
                at = 768 + col * 32
                all_s[4 * part + sub, at : at + 32, :] = g[
                    sub * 32 : sub * 32 + 32, col * 128 : (col + 1) * 128
                ]
    for k in range(4):
        y = lax.rem(zy_ref[1] + k, 4)
        z = lax.rem(zy_ref[0] + k, 4)
        for i in range(4):
            outs[k][i] = all_s[i * 4 + y, 0:HALF, :]
            outs[4 + k][i] = all_s[z * 4 + i, HALF:1152, :]


def first_sum_kernel(zy_ref, *refs):
    ins, outs, acc_s = refs[:8], refs[8:16], refs[16]
    for half in range(2):
        for i in range(4):
            acc = ins[4 * half][i].astype(F32)
            for k in range(1, 4):
                acc += ins[4 * half + k][i].astype(F32)
            acc_s[half, i] = acc.astype(BF16)
        for k in range(4):
            outs[4 * half + k][...] = acc_s[half, lax.rem(zy_ref[half] + k, 4)]


def second_sum_kernel(*refs):
    ins, cols, down = refs[:8], refs[8], refs[9]
    sums = []
    for half in range(2):
        acc = ins[4 * half][...].astype(F32)
        for k in range(1, 4):
            acc += ins[4 * half + k][...].astype(F32)
        sums.append(acc.astype(BF16))
    full = jnp.concatenate(sums, 0)
    cols[...] = full[0:768].reshape(8, 96, 128)
    down[...] = full[768:1152]


def shift(arrays, axis):
    out = [arrays[0]]
    for k in range(1, 4):
        pairs = []
        for z in range(4):
            for y in range(4):
                to = ((z + k) % 4, y) if axis == 0 else (z, (y + k) % 4)
                pairs.append((z * 4 + y, to[0] * 4 + to[1]))
        out.append(lax.ppermute(arrays[k], "ctx", pairs))
    return out


def out_grad_kernel(f_ref, o, *refs):
    pieces, out, o_s, da_s = refs[:8], refs[8], refs[9], refs[10]
    fi = f_ref[0]
    for k in range(8):
        first = fi if k < 4 else fi + 1 - 2 * lax.rem(fi, 2)
        slot = lax.rem(first + 8 - 2 * (k % 4), 8)
        at = pl.multiple_of(slot * 128, 128)
        o_s[k * 128 : (k + 1) * 128, :] = o[pl.ds(at, 128), :]
        da_s[k * 128 : (k + 1) * 128, :] = pieces[k][...]
    t = dot(o_s[...], da_s[...], TN)
    t = jnp.concatenate([t[0:64], t[64:128] + t[128:192], t[192:256]], 0).astype(BF16)
    for c in range(16):
        cr, cc = divmod(c, 4)
        out[c] = t[cr * 48 : (cr + 1) * 48, cc * 384 : (cc + 1) * 384]


def head_grad_kernel(n1, dback, dlog2, out, dproj):
    for s in range(8):
        d0, d1 = dback[2 * s], dback[2 * s + 1]
        dproj[s * 128 : (s + 1) * 128, :] = jnp.concatenate(
            [d0[0:128, 0:192], d0[0:128, 192:384] + d1[0:128, 0:192], d1[0:128, 192:384]], 1
        )
    for c in (14, 15):
        out[c] = jnp.zeros((8, 80, 128), BF16)
    for part in range(2):
        left = n1[:, part * 768 : (part + 1) * 768]
        heads = dot(left, dproj[...], TN)
        gate = dot(left, dlog2[...], TN)
        mid = gate[:, 64:128] + gate[:, 128:192]
        g = jnp.concatenate([heads, gate[:, 0:64], mid, gate[:, 192:256]], 1).astype(BF16)
        for sub in range(4):
            f = 4 * part + sub
            for t in range(72):
                rt, lt = divmod(t, 6)
                c, slot = divmod(t, 5)
                row = sub * 192 + rt * 16
                out[c, f, slot * 16 : (slot + 1) * 16, :] = g[
                    row : row + 16, lt * 128 : (lt + 1) * 128
                ]


def input_grad_kernel(
    f_ref, dproj, dlog2, dl, fpre, w1, w2, gains, n1, gain2, out
):
    fi = f_ref[0]
    rows = [[], [], []]
    for s in range(8):
        d0 = dl[2 * s : 2 * s + 1].astype(F32)
        d1 = dl[2 * s + 1 : 2 * s + 2].astype(F32)
        rows[0].append(d0[:, 0:128])
        rows[1].append(d0[:, 128:256] + d1[:, 0:128])
        rows[2].append(d1[:, 128:256])
    dlf = jnp.concatenate(
        [jnp.concatenate(r, 1) for r in rows] + [jnp.zeros((5, 1024), F32)], 0
    )
    is_head = lax.broadcasted_iota(jnp.int32, (8, 1024), 0) < 3
    dfpre = jnp.where(is_head, dlf * jax.nn.sigmoid(-fpre[...]), 0.0).astype(BF16)
    w_forget = gains[...].astype(BF16)
    gain1 = jnp.zeros((1, 1536), F32)
    for p in range(4):
        at = p * 256
        part = (
            dot(dproj[at : at + 256, :], w1[:, 0:576], NT)
            + dot(dlog2[at : at + 256, :], w2[:, 1024:1280], NT)
            + dot(dfpre[:, at : at + 256], w_forget, TN)
        )
        gain1 += jnp.sum(part * n1[at : at + 256, :].astype(F32), 0, keepdims=True)
        out[2 * p : 2 * p + 2, 0:128, :] = part.astype(BF16).reshape(2, 128, 1536)
    gain1 = gain1 / gains[3:4]
    forget = dot(dfpre, n1[...])
    bias = jnp.sum(dfpre.astype(F32), 1, keepdims=True)
    lane = lax.broadcasted_iota(jnp.int32, (8, 1536), 1)
    mine = (lane >= fi * 192) & (lane < fi * 192 + 192)
    for d in range(8):
        at = d * 192
        top = jnp.concatenate([forget[:, at : at + 192]] * 8, 1)
        top = jnp.where(mine, top, 0.0)
        own = jnp.broadcast_to(bias[0:3], (3, 1536)) * (fi == d).astype(F32)
        low = jnp.concatenate(
            [
                jnp.concatenate([gain1[:, at : at + 192]] * 8, 1),
                jnp.concatenate([gain2[:, at : at + 192]] * 8, 1),
                own,
                jnp.zeros((3, 1536), F32),
            ],
            0,
        )
        out[d, 128:144, :] = jnp.concatenate([top, low], 0).astype(BF16)


def head_sum_kernel(r, go, out):
    for f in range(8):
        acc = r[0, f].astype(F32)
        for c in range(1, 16):
            acc += r[c, f].astype(F32)
        out[f * 80 : (f + 1) * 80, :] = acc.astype(BF16)
    acc = go[0].astype(F32)
    for c in range(1, 16):
        acc += go[c].astype(F32)
    for lt in range(3):
        out[640 + lt * 48 : 688 + lt * 48, :] = acc[:, lt * 128 : (lt + 1) * 128].astype(BF16)


def unpack_ffn_kernel(r, gate, up, down):
    for cc in range(4):
        to = gate if cc < 2 else up
        for f in range(8):
            for half in range(2):
                at = f * 96 + half * 48
                col = f * 512 + (cc % 2) * 256 + half * 128
                to[:, col : col + 128] = r[cc, at : at + 48, :].astype(F32)
        for col in range(12):
            at = 768 + col * 32
            down[cc * 32 : (cc + 1) * 32, col * 128 : (col + 1) * 128] = r[
                cc, at : at + 32, :
            ].astype(F32)


def unpack_ffn(gathered):
    return pl.pallas_call(
        unpack_ffn_kernel,
        grid=(4,),
        out_shape=(
            shape(192, 4096, dtype=F32),
            shape(192, 4096, dtype=F32),
            shape(512, 1536, dtype=F32),
        ),
        in_specs=[pl.BlockSpec((4, 1152, 128), lambda i: (i, 0, 0))],
        out_specs=(
            pl.BlockSpec((48, 4096), lambda i: (i, 0)),
            pl.BlockSpec((48, 4096), lambda i: (i, 0)),
            pl.BlockSpec((128, 1536), lambda i: (i, 0)),
        ),
        compiler_params=pltpu.CompilerParams(vmem_limit_bytes=40 * MIB),
        cost_estimate=pl.CostEstimate(flops=0, bytes_accessed=2 * 10**7, transcendentals=0),
        name="unpack_ffn",
    )(gathered)


def unpack_kernel(r, q, k, v, g, o):
    for rt in range(12):
        rows = [[], [], [], []]
        for f in range(8):
            tiles = []
            for lt in range(6):
                c, slot = divmod(rt * 6 + lt, 5)
                at = f * 80 + slot * 16
                tiles.append(r[c, at : at + 16, :].astype(F32))
            line = jnp.concatenate(tiles, 1)
            for h in range(3):
                for w in range(3):
                    at = h * 192 + w * 64
                    rows[w].append(line[:, at : at + 64])
            rows[3].append(line[:, 576:768])
        for w, to in enumerate((q, k, v, g)):
            to[rt * 16 : (rt + 1) * 16, :] = jnp.concatenate(rows[w], 1)
    for c in range(16):
        cr, cc = divmod(c, 4)
        for lt in range(3):
            col = cc * 384 + lt * 128
            o[cr * 48 : (cr + 1) * 48, col : col + 128] = r[
                c, 640 + lt * 48 : 688 + lt * 48, :
            ].astype(F32)


def swap(array, axis):
    return lax.all_to_all(array, axis, 0, 0, tiled=True)


def gather(array, axis):
    return lax.all_gather(array, axis, axis=0, tiled=True)


def tie(*arrays):
    return lax.optimization_barrier(arrays)


def per_device(
    tokens, cotangent, lengths, block_map, norm_gain, w_query, w_key, w_value, w_forget,
    forget_bias, w_outgate, w_output, ffn_gain, w_gate, w_up, w_down,
):
    ci = lax.axis_index("ctx").astype(jnp.int32)
    fi = lax.axis_index("fsdp").astype(jnp.int32)
    j = lax.rem(ci, 2)[None]
    zy = jnp.stack([ci // 4, lax.rem(ci, 4)])
    offsets = jnp.arange(64, dtype=jnp.int32)
    own_blocks = lax.dynamic_slice_in_dim(block_map, 2 * ci, 2)
    live = ((own_blocks[:, None] * 64 + offsets[None, :]).reshape(128) < lengths[0])[:, None]
    x_own = tokens[0]
    live32 = jnp.broadcast_to(live.astype(F32), (128, 128))

    w1 = call(
        pack_kernel,
        shape(8, 192, 640),
        "pack",
        (w_query, w_key, w_value, w_forget, norm_gain[None], ffn_gain[None]),
    )
    x_own, w1 = tie(x_own, w1)
    x_all = gather(x_own, "fsdp")
    w1 = swap(w1, "fsdp").reshape(1536, 640)
    parts = call(
        pack_two_kernel,
        (shape(192, 1280),) * 8,
        "pack_two",
        (fi[None], w_gate, w_up, w_outgate),
        [pltpu.VMEM((8, 192, 1280), BF16)],
        [SMEM] + [VMEM] * 3,
    )
    parts = [parts[0]] + [
        lax.ppermute(parts[k], "fsdp", [(f, (f + k) % 8) for f in range(8)]) for k in range(1, 8)
    ]
    w_output, x_all = tie(w_output, x_all)
    wo_all = gather(w_output, "fsdp")

    bias = jnp.pad(forget_bias.astype(F32), (0, 5))[:, None]
    n1, send, fpre, gains = project(x_all, w1, bias, parts[0])
    c_own = call(
        mask_kernel, shape(128, 1536), "mask", (live32, cotangent[0], n1), ins=[VMEM, VMEM, ANY]
    )
    c_all = gather(c_own, "fsdp")
    recv = swap(send, "ctx")
    w2, sig2 = call(
        place_kernel,
        (shape(1536, 1280), shape(1024, 256, dtype=F32)),
        "place",
        (fi[None], n1, *parts),
        ins=[SMEM] + [VMEM] * 9,
    )

    tri = (offsets[:, None] <= offsets[None, :]).astype(BF16)
    blocks = jnp.arange(32, dtype=jnp.int32)
    pick = (block_map[None, :] == blocks[:, None]).astype(BF16)
    logs = recv[:, 128, 0:256].reshape(16, 2, 2, 64).transpose(0, 2, 1, 3).reshape(32, 128)
    logs = dot(pick, logs).astype(BF16).reshape(32, 2, 64)
    within = jnp.einsum("bht,tu->hbu", logs, tri, preferred_element_type=F32)
    before = (blocks[None, :] < blocks[:, None]).astype(F32)
    starts = jnp.sum(before[None, :, :] * within[:, None, :, 63], -1)
    decay = (within + starts[:, :, None]).reshape(2, 1, SPAN)

    attn_own, attn, log_total = attend(block_map, j, recv, decay, parts[1:4])
    attn2 = swap(attn_own, "ctx").reshape(8, 2, 128, 128).transpose(0, 2, 1, 3)
    attn2 = attn2.reshape(1024, 256)
    o2 = (attn2.astype(F32) * sig2).astype(BF16)
    o_own = swap(o2.reshape(8, 128, 256), "fsdp")
    o_own, c_all = tie(o_own, c_all)
    h, n2_own, inv2 = call(
        mid_kernel,
        (shape(128, 1536, dtype=F32), shape(128, 1536), shape(128, 128, dtype=F32)),
        "mid",
        (o_own, wo_all, x_own, gains),
    )
    n2 = gather(n2_own, "fsdp")
    dn2, ffo, u, dpre = feed_forward(n2, c_all, w2, w_down)
    dn2 = lax.psum_scatter(dn2, "fsdp", scatter_dimension=0, tiled=True)

    fg = call(
        ffn_grad_kernel,
        (shape(4, HALF, 128),) * 8,
        "ffn_grad",
        (zy, n2, dpre, u, c_all),
        [pltpu.VMEM((16, 1152, 128), BF16)],
        [SMEM] + [VMEM] * 4,
        flops=5 * 10**9,
    )
    fg = shift(fg[:4], 1) + shift(fg[4:], 0)

    dh, da_own, do_own, gain2_part = call(
        mid_back_kernel,
        (
            shape(128, 1536, dtype=F32),
            shape(128, 1536),
            shape(8, 128, 256),
            shape(1, 1536, dtype=F32),
        ),
        "mid_back",
        (dn2, h, inv2, c_own, gains, wo_all, fg[1], fg[5], fg[2], fg[6]),
        ins=[VMEM] * 6 + [ANY] * 4,
    )
    do2 = swap(do_own, "fsdp").reshape(1024, 256)
    near = [da_own] + [
        lax.ppermute(da_own, "fsdp", [(f, (f + 2 * k) % 8) for f in range(8)]) for k in range(1, 4)
    ]
    da = near + [lax.ppermute(piece, "fsdp", [(f, f ^ 1) for f in range(8)]) for piece in near]
    fg = call(
        first_sum_kernel,
        (shape(HALF, 128),) * 8,
        "first_sum",
        (zy, *fg),
        [pltpu.VMEM((2, 4, HALF, 128), BF16)],
        [SMEM] + [VMEM] * 8,
    )
    fg = shift(fg[:4], 0) + shift(fg[4:], 1)
    do2 = do2.astype(F32)
    datt2 = (do2 * sig2).astype(BF16)
    dlog2 = (do2 * attn2.astype(F32) * sig2 * (1.0 - sig2)).astype(BF16)
    datt = swap(datt2.reshape(8, 128, 2, 128).transpose(0, 2, 1, 3).reshape(16, 128, 128), "ctx")
    datt, *fg = tie(datt, *fg)
    cols_g, down_g = call(second_sum_kernel, (shape(8, 96, 128), shape(384, 128)), "second_sum", fg)
    ffo, da_own = tie(ffo, da_own)
    ffo = lax.psum_scatter(ffo, "fsdp", scatter_dimension=0, tiled=True)
    go = call(
        out_grad_kernel,
        shape(16, 48, 384),
        "out_grad",
        (fi[None], o2, *da),
        [pltpu.VMEM((1024, 256), BF16), pltpu.VMEM((1024, 1536), BF16)],
        [SMEM] + [VMEM] * 9,
    )
    cols_g = swap(cols_g, "fsdp").reshape(768, 128)
    dheads = attend_back(block_map, j, recv, datt, attn, log_total, decay, go)
    dheads, cols_g, ffo = tie(dheads, cols_g, ffo)
    ffn = gather(jnp.concatenate([cols_g, down_g], 0), "ctx").reshape(16, 1152, 128)
    dback = swap(dheads, "ctx")
    mixed = jnp.where(live, h + ffo.astype(F32), 0.0).astype(BF16)

    g1, dproj = call(
        head_grad_kernel,
        (shape(16, 8, 80, 128), shape(1024, 576)),
        "head_grad",
        (n1, dback, dlog2),
        flops=3 * 10**9,
    )
    g1 = swap(g1.reshape(128, 80, 128), BOTH).reshape(16, 8, 80, 128)

    dn1 = call(
        input_grad_kernel,
        shape(8, 144, 1536),
        "input_grad",
        (fi[None], dproj, dlog2, dback[:, 128, 0:256], fpre, w1, w2, gains, n1, gain2_part),
        ins=[SMEM] + [VMEM] * 9,
        flops=3 * 10**9,
    )
    dn1 = lax.psum_scatter(
        dn1.reshape(1152, 1536), "fsdp", scatter_dimension=0, tiled=True
    )
    g1, ffn = tie(g1, ffn)
    att = call(head_sum_kernel, shape(784, 128), "head_sum", (g1, dback[:, 144:192]))
    att, dn1 = tie(att, dn1)
    att = gather(att, "ctx").reshape(16, 784, 128)

    small = jnp.concatenate([dn1[128:131], dn1[136:141]], 0)
    small = swap(jnp.broadcast_to(small[None], (16, 8, 1536)), "ctx")
    small = jnp.sum(small.astype(F32), 0)
    forget_g = small[0:3].reshape(3, 8, 192).transpose(2, 1, 0).reshape(192, 24)

    dn1 = dn1[0:128].astype(F32)
    gain1 = gains[3:4]
    x_own32 = x_own.astype(F32)
    r1_own = lax.rsqrt(jnp.mean(x_own32 * x_own32, -1, keepdims=True) + EPS)
    scaled1 = dn1 * gain1
    tokens_grad = (
        dh
        + r1_own * scaled1
        - x_own32 * (r1_own * r1_own * r1_own) * jnp.mean(scaled1 * x_own32, -1, keepdims=True)
    ).astype(BF16)

    gate_g, up_g, down_g = unpack_ffn(ffn)
    mat = shape(192, 1536, dtype=F32)
    query_g, key_g, value_g, outgate_g, output_g = call(
        unpack_kernel, (mat,) * 5, "unpack_heads", (att,)
    )
    return (
        mixed[None], tokens_grad[None], small[3, 0:192], query_g, key_g, value_g, forget_g,
        small[5:8, 0], outgate_g, output_g, small[4, 0:192], gate_g, up_g, down_g,
    )


def solution(mesh):
    act = P("fsdp", "ctx", None)
    vec, mat = P("fsdp"), P("fsdp", None)
    return jax.shard_map(
        per_device,
        mesh=mesh,
        in_specs=(act, act, vec, P(), vec, mat, mat, mat, mat, vec, mat, mat, vec, mat, mat, mat),
        out_specs=(act, act, vec, mat, mat, mat, mat, vec, mat, mat, vec, mat, mat, mat),
        check_vma=False,
    )
```

```python
import jax
import jax.numpy as jnp
from jax import lax
from jax.experimental import pallas as pl
from jax.experimental.pallas import tpu as pltpu
from jax.sharding import PartitionSpec as P

EPS = 1e-06
NEG = -1e30
HD = 64
QB = 256
SPAN = 2048
SHARED = ((0, 3, 4, 7), (1, 2, 5, 6))
F32 = jnp.float32
BF16 = jnp.bfloat16
HIGH = lax.Precision.HIGHEST
NN = (((1,), (0,)), ((), ()))
NT = (((1,), (1,)), ((), ()))
TN = (((0,), (0,)), ((), ()))
MIB = 2**20
SMEM = pl.BlockSpec(memory_space=pltpu.SMEM)
VMEM = pl.BlockSpec(memory_space=pltpu.VMEM)
ANY = pl.BlockSpec(memory_space=pl.ANY)
BOTH = ("ctx", "fsdp")


def dot(a, b, dims=NN):
    return lax.dot_general(a, b, dims, preferred_element_type=F32)


def shape(*dims, dtype=BF16):
    return jax.ShapeDtypeStruct(dims, dtype)


def call(kernel, outs, name, args, scratch=(), ins=None, flops=10**9, moved=10**7, limit=60):
    return pl.pallas_call(
        kernel,
        grid=(1,),
        out_shape=outs,
        in_specs=ins or [VMEM] * len(args),
        out_specs=jax.tree.map(lambda _: VMEM, outs),
        scratch_shapes=list(scratch),
        compiler_params=pltpu.CompilerParams(vmem_limit_bytes=limit * MIB),
        cost_estimate=pl.CostEstimate(flops=flops, bytes_accessed=moved, transcendentals=0),
        name=name,
    )(*args)


def pack_kernel(ids, bm_ref, len_ref, x, cot, wq, wk, wv, wf, gain, wo, wg, wu, out, x_out, c_out):
    row = lax.broadcasted_iota(jnp.int32, (128, 128), 0)
    first, second = bm_ref[2 * ids[4]] * 64, bm_ref[2 * ids[4] + 1] * 64
    pos = row + jnp.where(row < 64, first, second - 64)
    live = jnp.where(pos < len_ref[0], 1.0, 0.0)[:, 0:1]
    x_out[...] = x[...]
    c_out[...] = jnp.where(live > 0.5, cot[...].astype(F32), 0.0).astype(BF16)
    lane = lax.broadcasted_iota(jnp.int32, (192, 64), 1)
    rows = jnp.concatenate(
        [wf[...].astype(F32), gain[...].astype(F32), jnp.zeros((6, 192), F32)], 0
    ).T
    base = jnp.where(lane == 3, rows[:, 24:25], jnp.where(lane == 4, rows[:, 25:26], 0.0))
    for d in range(8):
        parts = []
        for h in range(3):
            at = d * 192 + h * 64
            parts += [wq[:, at : at + 64], wk[:, at : at + 64], wv[:, at : at + 64]]
        ext = base
        for h in range(3):
            ext = jnp.where(lane == h, rows[:, 3 * d + h : 3 * d + h + 1], ext)
        parts.append(ext.astype(BF16))
        heads = [wo[:, d * 192 + h * 64 : d * 192 + h * 64 + 64] for h in range(3)]
        parts += [heads[0], heads[1], heads[1], heads[2]]
        for m in range(7):
            out[d, 0:192, m * 128 : (m + 1) * 128] = jnp.concatenate(
                [parts[2 * m], parts[2 * m + 1]], 1
            )
        out[d, 192:208, 768:896] = jnp.zeros((16, 128), BF16)
    for half in range(2):

        @pl.when(ids[1] // 2 == half)
        def _():
            w = (wg, wu)[half]
            for d in range(8):
                for b in range(6):
                    lt, part = divmod(b, 3)
                    at = pl.multiple_of(ids[0] * 48 + part * 16, 16)
                    col = pl.multiple_of(lax.rem(ids[1], 2) * 256 + (d * 512 + lt * 128), 128)
                    out[d, 192:208, b * 128 : (b + 1) * 128] = w[pl.ds(at, 16), pl.ds(col, 128)]


def open_kernel(n1, w1, _a, sig):
    sig[...] = jax.nn.sigmoid(dot(n1[...], w1[:, 640:896]))


def proj_kernel(x, w1r, bias, wo, n1, send, fpre, gains, w1, w2, wo_out):
    @pl.when(pl.program_id(0) == 0)
    def _():
        for f in range(8):
            w1[f * 192 : (f + 1) * 192, :] = w1r[f, 0:192, :]
            for b in range(6):
                at = f * 96 + b * 16
                w2[at : at + 16, :] = w1r[f, 192:208, b * 128 : (b + 1) * 128]
        wo_out[...] = wo[...]
        gains[...] = w1[:, 512:640].astype(F32).T[64:72]

    x32 = x[...].astype(F32)
    r1 = lax.rsqrt(jnp.mean(x32 * x32, -1, keepdims=True) + EPS)
    normed = (x32 * r1 * gains[3:4]).astype(BF16)
    n1[...] = normed
    proj = dot(normed, w1[:, 0:640])
    rows = proj[:, 512:640].T[64:72] + bias[...]
    fpre[...] = rows
    logs = jnp.minimum(rows, 0.0) - jnp.log1p(jnp.exp(-jnp.abs(rows)))
    low = proj[:, 0:576].astype(BF16)
    for s in range(4):
        for j in range(2):
            send[2 * s + j, 0:128, :] = low[s * 128 : (s + 1) * 128, j * 192 : j * 192 + 384]
            line = jnp.concatenate(
                [
                    logs[j : j + 1, s * 128 : (s + 1) * 128],
                    logs[j + 1 : j + 2, s * 128 : (s + 1) * 128],
                    jnp.zeros((1, 128), F32),
                ],
                1,
            )
            send[2 * s + j, 128:144, :] = jnp.broadcast_to(line, (16, 384)).astype(BF16)


def project(x_all, w1r, bias, wo):
    def fixed(*dims):
        return pl.BlockSpec(dims, lambda i: (0,) * len(dims))

    return pl.pallas_call(
        proj_kernel,
        grid=(2,),
        out_shape=(
            shape(1024, 1536),
            shape(16, 144, 384),
            shape(8, 1024, dtype=F32),
            shape(8, 1536, dtype=F32),
            shape(1536, 896),
            shape(768, 128),
            shape(192, 1536),
        ),
        in_specs=[
            pl.BlockSpec((512, 1536), lambda i: (i, 0)),
            fixed(8, 208, 896),
            fixed(8, 1),
            fixed(192, 1536),
        ],
        out_specs=(
            pl.BlockSpec((512, 1536), lambda i: (i, 0)),
            pl.BlockSpec((8, 144, 384), lambda i: (i, 0, 0)),
            pl.BlockSpec((8, 512), lambda i: (0, i)),
            fixed(8, 1536),
            fixed(1536, 896),
            fixed(768, 128),
            fixed(192, 1536),
        ),
        compiler_params=pltpu.CompilerParams(vmem_limit_bytes=60 * MIB),
        cost_estimate=pl.CostEstimate(
            flops=2 * 10**9, bytes_accessed=10**7, transcendentals=0
        ),
        name="project",
    )(x_all, w1r, bias, wo)


def score_cols(hs, b, q_s, k_s, fc_s, fr):
    n = (b + 1) * QB
    q0 = b * QB
    qq = q_s[hs, q0 : q0 + QB, :]
    cols = dot(k_s[hs, 0:n, :], qq, NT)
    bias = fr[hs, :, q0 : q0 + 1] - fc_s[hs, 0:n, :]
    cols = cols + bias
    keep = lax.broadcasted_iota(jnp.int32, (QB, QB), 0) <= lax.broadcasted_iota(
        jnp.int32, (QB, QB), 1
    )
    tail = jnp.where(keep, cols[n - QB : n], NEG)
    if b:
        cols = jnp.concatenate([cols[: n - QB], tail], 0)
    else:
        cols = tail
    return cols, qq, n, q0


def run_units(j, unit):
    for b in range(SPAN // QB):
        unit(j, b)
    for half in range(2):

        @pl.when(j == half)
        def _():
            for b in SHARED[half]:
                unit(1 - half, b)


def load_heads(bm_ref, r1, q_s, k_s, v_s):
    for blk in range(32):
        at = pl.multiple_of(bm_ref[blk] * 64, 64)
        c, r = divmod(blk, 2)
        for hs in range(2):
            part = r1[c, r * 64 : (r + 1) * 64, hs * 192 : (hs + 1) * 192]
            q_s[hs, pl.ds(at, 64), :] = (part[:, 0:64].astype(F32) * 0.125).astype(BF16)
            k_s[hs, pl.ds(at, 64), :] = part[:, 64:128]
            v_s[hs, pl.ds(at, 64), :] = part[:, 128:192]


def column_decay(fr, fc_s):
    both = jnp.concatenate([fr[0], fr[1], jnp.zeros((6, SPAN), F32)], 0).T
    fc_s[0] = both[:, 0:1]
    fc_s[1] = both[:, 1:2]


def fwd_kernel(bm_ref, ids, r1, fr, _a, _b, _c, o_ref, attn_ref, l_ref, q_s, k_s, v_s, vt_s, fc_s, o_s):
    j = ids[3]
    load_heads(bm_ref, r1, q_s, k_s, v_s)
    column_decay(fr, fc_s)
    for hs in range(2):
        vt_s[hs, 0:64, :] = v_s[hs].astype(F32).T.astype(BF16)
        vt_s[hs, 64:80, :] = jnp.ones((16, SPAN), BF16)
        o_s[hs] = jnp.zeros((SPAN, HD), BF16)

    def unit(hs, b):
        cols, _, n, q0 = score_cols(hs, b, q_s, k_s, fc_s, fr)
        top = jnp.max(cols, 0, keepdims=True)
        probs = jnp.exp(cols - top).astype(BF16)
        acc = dot(vt_s[hs, :, 0:n], probs)
        total = acc[64:65]
        rows = (acc[0:64] / total).T
        attn_ref[hs, q0 : q0 + QB, :] = rows
        l_ref[hs, :, q0 : q0 + QB] = top + jnp.log(total)
        o_s[hs, q0 : q0 + QB, :] = rows.astype(BF16)

    run_units(j, unit)
    for blk in range(32):
        at = pl.multiple_of(bm_ref[blk] * 64, 64)
        c, r = divmod(blk, 2)
        o_ref[c, r * 64 : (r + 1) * 64, :] = jnp.concatenate(
            [o_s[0, pl.ds(at, 64), :], o_s[1, pl.ds(at, 64), :]], 1
        )


def suffix_sums(row, dl_s, hs):
    grid = jnp.concatenate([row[:, b * 64 : (b + 1) * 64] for b in range(32)], 0)
    tri = lax.broadcasted_iota(jnp.int32, (64, 64), 0) >= lax.broadcasted_iota(
        jnp.int32, (64, 64), 1
    )
    within = jnp.dot(grid, tri.astype(F32), precision=HIGH, preferred_element_type=F32)
    total = jnp.broadcast_to(within[:, 0:1], (32, 64))
    later = lax.broadcasted_iota(jnp.int32, (32, 32), 0) < lax.broadcasted_iota(
        jnp.int32, (32, 32), 1
    )
    dl_s[hs] = within + jnp.dot(
        later.astype(F32), total, precision=HIGH, preferred_element_type=F32
    )


def bwd_kernel(
    bm_ref, ids, r1, da_r, attn_ref, l_ref, fr, go,
    ds_ref,
    q_s, k_s, v_s, da_s, kt_s, fc_s, dk_s, dv_s, out_s, rs_ref, dl_s,
):
    j = ids[3]
    for c in range(16):
        ds_ref[c, 144:192, :] = go[c]
    load_heads(bm_ref, r1, q_s, k_s, v_s)
    column_decay(fr, fc_s)
    for blk in range(32):
        at = pl.multiple_of(bm_ref[blk] * 64, 64)
        c, r = divmod(blk, 2)
        part = da_r[c, r * 64 : (r + 1) * 64, :]
        for hs in range(2):
            da_s[hs, pl.ds(at, 64), :] = part[:, hs * 64 : (hs + 1) * 64]
    for hs in range(2):
        kt_s[hs, 0:64, :] = k_s[hs].astype(F32).T.astype(BF16)
        kt_s[hs, 64:80, :] = jnp.ones((16, SPAN), BF16)
        dk_s[hs] = jnp.zeros((SPAN, 128), F32)
        dv_s[hs] = jnp.zeros((SPAN, HD), F32)
        out_s[hs] = jnp.zeros((SPAN, 192), BF16)
        rs_ref[hs] = jnp.zeros((1, SPAN), F32)

    def unit(hs, b):
        cols, qq, n, q0 = score_cols(hs, b, q_s, k_s, fc_s, fr)
        datt = da_s[hs, q0 : q0 + QB, :]
        attn = attn_ref[hs, q0 : q0 + QB, :]
        delta = jnp.sum((datt.astype(F32) * attn).T, 0, keepdims=True)
        probs = jnp.exp(cols - l_ref[hs, :, q0 : q0 + QB])
        dv_s[hs, 0:n, :] += dot(probs.astype(BF16), datt)
        back = dot(v_s[hs, 0:n, :], datt, NT)
        dscore = (probs * (back - delta)).astype(BF16)
        wide = jnp.concatenate([qq, jnp.ones((QB, HD), BF16)], 1)
        dk_s[hs, 0:n, :] += dot(dscore, wide)
        dq = dot(kt_s[hs, :, 0:n], dscore)
        rs_ref[hs, :, q0 : q0 + QB] = dq[64:65]
        out_s[hs, q0 : q0 + QB, 0:64] = (dq[0:64].T * 0.125).astype(BF16)

    run_units(j, unit)
    for hs in range(2):
        both = dk_s[hs]
        suffix_sums(rs_ref[hs] - both.T[64:65], dl_s, hs)
        out_s[hs, :, 64:128] = both[:, 0:64].astype(BF16)
        out_s[hs, :, 128:192] = dv_s[hs].astype(BF16)
    for blk in range(32):
        at = pl.multiple_of(bm_ref[blk] * 64, 64)
        c, r = divmod(blk, 2)
        ds_ref[c, r * 64 : (r + 1) * 64, :] = jnp.concatenate(
            [out_s[0, pl.ds(at, 64), :], out_s[1, pl.ds(at, 64), :]], 1
        )
    for c in range(16):
        lines = [
            dl_s[hs, pl.ds(bm_ref[2 * c + r], 1), :] for hs in range(2) for r in range(2)
        ]
        line = jnp.concatenate(lines + [jnp.zeros((1, 128), F32)], 1)
        ds_ref[c, 128:144, :] = jnp.broadcast_to(line, (16, 384)).astype(BF16)


HEADS = [pltpu.VMEM((2, SPAN, HD), BF16)] * 3


def attend(block_map, ids, r1, decay, after):
    return call(
        fwd_kernel,
        (shape(16, 128, 128), shape(2, SPAN, HD, dtype=F32), shape(2, 1, SPAN, dtype=F32)),
        "attend",
        (block_map, ids, r1, decay, *after),
        HEADS
        + [
            pltpu.VMEM((2, 80, SPAN), BF16),
            pltpu.VMEM((2, SPAN, 1), F32),
            pltpu.VMEM((2, SPAN, HD), BF16),
        ],
        [SMEM, SMEM, VMEM, VMEM, ANY, ANY, ANY],
        flops=4 * 10**9,
    )


def attend_back(block_map, ids, r1, upstream, attn, logs, decay, go):
    return call(
        bwd_kernel,
        shape(16, 192, 384),
        "attend_back",
        (block_map, ids, r1, upstream, attn, logs, decay, go),
        HEADS
        + [
            pltpu.VMEM((2, SPAN, HD), BF16),
            pltpu.VMEM((2, 80, SPAN), BF16),
            pltpu.VMEM((2, SPAN, 1), F32),
            pltpu.VMEM((2, SPAN, 128), F32),
            pltpu.VMEM((2, SPAN, HD), F32),
            pltpu.VMEM((2, SPAN, 192), BF16),
            pltpu.VMEM((2, 1, SPAN), F32),
            pltpu.VMEM((2, 32, 64), F32),
        ],
        [SMEM, SMEM] + [VMEM] * 6,
        flops=10**10,
    )


def mid_kernel(o_r, wo, x, gains, h_ref, n2_ref, r2_ref):
    acc = x[...].astype(F32)
    for f in range(8):
        at = f * 192
        acc += dot(o_r[f, :, 0:128], wo[at : at + 128, :])
        acc += dot(o_r[f, :, 128:256], wo[at + 64 : at + 192, :])
    h_ref[...] = acc
    r2 = lax.rsqrt(jnp.mean(acc * acc, -1, keepdims=True) + EPS)
    r2_ref[...] = jnp.broadcast_to(r2, (128, 128))
    n2_ref[...] = (acc * r2 * gains[4:5]).astype(BF16)


def mid_back_kernel(
    dn2_r, h_ref, r2_ref, c_ref, gains, wo, _after,
    dh_ref, da_ref, do_ref, g2_ref,
):
    h = h_ref[...]
    r2 = r2_ref[:, 0:1]
    dn2 = dn2_r[...].astype(F32)
    g2_ref[...] = jnp.sum(dn2 * h * r2, 0, keepdims=True)
    scaled = dn2 * gains[4:5]
    dh = (
        c_ref[...].astype(F32)
        + r2 * scaled
        - h * (r2 * r2 * r2) * jnp.mean(scaled * h, -1, keepdims=True)
    )
    dh_ref[...] = dh
    da = dh.astype(BF16)
    da_ref[...] = da
    for f in range(8):
        at = f * 192
        do_ref[f, :, 0:128] = dot(da, wo[at : at + 128, :], NT).astype(BF16)
        do_ref[f, :, 128:256] = dot(da, wo[at + 64 : at + 192, :], NT).astype(BF16)


def ready_kernel(ids, w2g, *refs):
    parts, w2, c_all = refs[:8], refs[8], refs[9]
    for k in range(8):
        first = ids[2] if k < 4 else ids[2] + 1 - 2 * lax.rem(ids[2], 2)
        slot = lax.rem(first + 8 - 2 * (k % 4), 8)
        c_all[pl.ds(pl.multiple_of(slot * 128, 128), 128), :] = parts[k][...]
    for p in range(16):
        cr, cc = divmod(p, 4)
        for f in range(8):
            for lt in range(2):
                row, col = f * 192 + cr * 48, cc * 256 + lt * 128
                at = f * 96 + lt * 48
                w2[row : row + 48, col : col + 128] = w2g[p, at : at + 48, :]


def ffn_kernel(n2, c, w2, wd, dn2_ref, ffo_ref, u_ref, dpre_ref):
    pre = dot(n2[...], w2[...])
    gate, up = pre[:, 0:512], pre[:, 512:1024]
    sig = jax.nn.sigmoid(gate)
    act = gate * sig
    u = (act * up).astype(BF16)
    u_ref[...] = u
    du = dot(c[...], wd[...], NT)
    dgate = (du * up * (sig * (1.0 + gate * (1.0 - sig)))).astype(BF16)
    dup = (du * act).astype(BF16)
    dpre = jnp.concatenate([dgate, dup], 1)
    dpre_ref[...] = dpre
    dn2_ref[...] = dot(dpre, w2[...], NT).astype(BF16)
    ffo_ref[...] = dot(u, wd[...]).astype(BF16)


def feed_forward(n2, c_all, w2, wd):
    rows = 256
    return pl.pallas_call(
        ffn_kernel,
        grid=(1024 // rows,),
        out_shape=(
            shape(1024, 1536),
            shape(1024, 1536),
            shape(1024, 512),
            shape(1024, 1024),
        ),
        in_specs=[
            pl.BlockSpec((rows, 1536), lambda i: (i, 0)),
            pl.BlockSpec((rows, 1536), lambda i: (i, 0)),
            pl.BlockSpec((1536, 1024), lambda i: (0, 0)),
            pl.BlockSpec((512, 1536), lambda i: (0, 0)),
        ],
        out_specs=(
            pl.BlockSpec((rows, 1536), lambda i: (i, 0)),
            pl.BlockSpec((rows, 1536), lambda i: (i, 0)),
            pl.BlockSpec((rows, 512), lambda i: (i, 0)),
            pl.BlockSpec((rows, 1024), lambda i: (i, 0)),
        ),
        compiler_params=pltpu.CompilerParams(vmem_limit_bytes=56 * MIB),
        cost_estimate=pl.CostEstimate(
            flops=10**10, bytes_accessed=2 * 10**7, transcendentals=0
        ),
        name="feed_forward",
    )(n2, c_all, w2, wd)


def ffn_grad_kernel(n2, dpre, u, c, out):
    for part in range(4):
        g = dot(n2[:, part * 384 : (part + 1) * 384], dpre[...], TN).astype(BF16)
        for sub in range(2):
            f = 2 * part + sub
            for cr in range(4):
                for col in range(8):
                    cc, half = divmod(col, 2)
                    at = f * 96 + half * 48
                    out[cr * 4 + cc, at : at + 48, :] = g[
                        sub * 192 + cr * 48 : sub * 192 + cr * 48 + 48,
                        col * 128 : (col + 1) * 128,
                    ]
    for part in range(4):
        g = dot(u[:, part * 128 : (part + 1) * 128], c[...], TN).astype(BF16)
        for sub in range(4):
            for col in range(12):
                at = 768 + col * 32
                out[4 * part + sub, at : at + 32, :] = g[
                    sub * 32 : sub * 32 + 32, col * 128 : (col + 1) * 128
                ]


def split_kernel(ids, r, _after, *outs):
    for k in range(8):
        at = pl.multiple_of(lax.rem(ids[2] + k, 8) * 96, 16)
        outs[k][...] = r[pl.ds(at, 96), :]


def out_grad_kernel(o, da, out):
    t = dot(o[...], da[...], TN)
    t = jnp.concatenate([t[0:64], t[64:128] + t[128:192], t[192:256]], 0).astype(BF16)
    for c in range(16):
        cr, cc = divmod(c, 4)
        out[c] = t[cr * 48 : (cr + 1) * 48, cc * 384 : (cc + 1) * 384]


def head_grad_kernel(n1, dback, dlog2, out, dproj):
    for s in range(8):
        d0, d1 = dback[2 * s], dback[2 * s + 1]
        dproj[s * 128 : (s + 1) * 128, :] = jnp.concatenate(
            [d0[0:128, 0:192], d0[0:128, 192:384] + d1[0:128, 0:192], d1[0:128, 192:384]], 1
        )
    for c in (3, 7, 11, 15):
        out[c] = jnp.zeros((8, 80, 128), BF16)
    for part in range(2):
        left = n1[:, part * 768 : (part + 1) * 768]
        heads = dot(left, dproj[...], TN)
        gate = dot(left, dlog2[...], TN)
        mid = gate[:, 64:128] + gate[:, 128:192]
        g = jnp.concatenate([heads, gate[:, 0:64], mid, gate[:, 192:256]], 1).astype(BF16)
        for sub in range(4):
            f = 4 * part + sub
            for t in range(72):
                rt, lt = divmod(t, 6)
                c, slot = divmod((rt % 3) * 6 + lt, 5)
                c += rt // 3 * 4
                row = sub * 192 + rt * 16
                out[c, f, slot * 16 : (slot + 1) * 16, :] = g[
                    row : row + 16, lt * 128 : (lt + 1) * 128
                ]


def input_grad_kernel(
    ids, dproj, dlog2, dl, fpre, w1, gains, n1, gain2, ffo, out
):
    fi = ids[2]
    rows = [[], [], []]
    for s in range(8):
        d0 = dl[2 * s : 2 * s + 1].astype(F32)
        d1 = dl[2 * s + 1 : 2 * s + 2].astype(F32)
        rows[0].append(d0[:, 0:128])
        rows[1].append(d0[:, 128:256] + d1[:, 0:128])
        rows[2].append(d1[:, 128:256])
    dlf = jnp.concatenate(
        [jnp.concatenate(r, 1) for r in rows] + [jnp.zeros((5, 1024), F32)], 0
    )
    is_head = lax.broadcasted_iota(jnp.int32, (8, 1024), 0) < 3
    dfpre = jnp.where(is_head, dlf * jax.nn.sigmoid(-fpre[...]), 0.0).astype(BF16)
    w_forget = gains[...].astype(BF16)
    gain1 = jnp.zeros((1, 1536), F32)
    for p in range(4):
        at = p * 256
        part = (
            dot(dproj[at : at + 256, :], w1[:, 0:576], NT)
            + dot(dlog2[at : at + 256, :], w1[:, 640:896], NT)
            + dot(dfpre[:, at : at + 256], w_forget, TN)
        )
        gain1 += jnp.sum(part * n1[at : at + 256, :].astype(F32), 0, keepdims=True)
        out[2 * p : 2 * p + 2, 0:128, :] = part.astype(BF16).reshape(2, 128, 1536)
    gain1 = gain1 / gains[3:4]
    forget = dot(dfpre, n1[...])
    bias = jnp.sum(dfpre.astype(F32), 1, keepdims=True)
    lane = lax.broadcasted_iota(jnp.int32, (8, 1536), 1)
    mine = (lane >= fi * 192) & (lane < fi * 192 + 192)
    for d in range(8):
        at = d * 192
        top = jnp.concatenate([forget[:, at : at + 192]] * 8, 1)
        top = jnp.where(mine, top, 0.0)
        own = jnp.broadcast_to(bias[0:3], (3, 1536)) * (fi == d).astype(F32)
        low = jnp.concatenate(
            [
                jnp.concatenate([gain1[:, at : at + 192]] * 8, 1),
                jnp.concatenate([gain2[:, at : at + 192]] * 8, 1),
                own,
                jnp.zeros((3, 1536), F32),
            ],
            0,
        )
        out[d, 128:144, :] = jnp.concatenate([top, low], 0).astype(BF16)
        out[d, 144:272, :] = ffo[d * 128 : (d + 1) * 128, :]


def head_sum_kernel(r, go, mine, *refs):
    cols, out = refs[:8], refs[8]
    for k in range(8):
        out[k * 96 : (k + 1) * 96, :] = cols[k][...]
    out[768:1152, :] = mine[768:1152, :]
    for f in range(8):
        acc = r[0, f].astype(F32)
        for c in range(1, 16):
            acc += r[c, f].astype(F32)
        at = 1152 + f * 80
        out[at : at + 80, :] = acc.astype(BF16)
    acc = go[0].astype(F32)
    for c in range(1, 16):
        acc += go[c].astype(F32)
    for lt in range(3):
        at = 1792 + lt * 48
        out[at : at + 48, :] = acc[:, lt * 128 : (lt + 1) * 128].astype(BF16)


def small_sum_kernel(r, out):
    acc = r[0].astype(F32)
    for c in range(1, 16):
        acc += r[c].astype(F32)
    out[...] = acc


def finish_kernel(dn1, dh, x, gains, out):
    x32 = x[...].astype(F32)
    r1 = lax.rsqrt(jnp.mean(x32 * x32, -1, keepdims=True) + EPS)
    scaled = dn1[0:128, :].astype(F32) * gains[3:4]
    out[...] = (
        dh[...]
        + r1 * scaled
        - x32 * (r1 * r1 * r1) * jnp.mean(scaled * x32, -1, keepdims=True)
    ).astype(BF16)


def unpack_kernel(ids, r, q, k, v, g, o, gate, up, down):
    for cc in range(4):
        to = gate if cc < 2 else up
        for d in range(8):
            f = lax.rem(ids[2] + 8 - d, 8)
            for half in range(2):
                at = d * 96 + half * 48
                col = pl.multiple_of(f * 512 + ((cc % 2) * 256 + half * 128), 128)
                to[:, pl.ds(col, 128)] = r[cc, at : at + 48, :].astype(F32)
        for col in range(12):
            at = 768 + col * 32
            down[cc * 32 : (cc + 1) * 32, col * 128 : (col + 1) * 128] = r[
                cc, at : at + 32, :
            ].astype(F32)
        for lt in range(3):
            col = cc * 384 + lt * 128
            o[:, col : col + 128] = r[cc, 1792 + lt * 48 : 1840 + lt * 48, :].astype(F32)
    for rt in range(3):
        rows = [[], [], [], []]
        for f in range(8):
            tiles = []
            for lt in range(6):
                c, slot = divmod(rt * 6 + lt, 5)
                at = 1152 + f * 80 + slot * 16
                tiles.append(r[c, at : at + 16, :].astype(F32))
            line = jnp.concatenate(tiles, 1)
            for h in range(3):
                for w in range(3):
                    at = h * 192 + w * 64
                    rows[w].append(line[:, at : at + 64])
            rows[3].append(line[:, 576:768])
        for w, to in enumerate((q, k, v, g)):
            to[rt * 16 : (rt + 1) * 16, :] = jnp.concatenate(rows[w], 1)


def unpack(ids, total):
    def rows(n, width):
        return shape(4 * n, width, dtype=F32), pl.BlockSpec((n, width), lambda i: (i, 0))

    outs = [rows(48, 1536)] * 5 + [rows(48, 4096)] * 2 + [rows(128, 1536)]
    return pl.pallas_call(
        unpack_kernel,
        grid=(4,),
        out_shape=tuple(a for a, _ in outs),
        in_specs=[SMEM, pl.BlockSpec((4, 1936, 128), lambda i: (i, 0, 0))],
        out_specs=tuple(b for _, b in outs),
        compiler_params=pltpu.CompilerParams(vmem_limit_bytes=60 * MIB),
        cost_estimate=pl.CostEstimate(
            flops=6 * 10**10, bytes_accessed=3 * 10**7, transcendentals=0
        ),
        name="unpack",
    )(ids, total)


def after(array, *others):
    return pl.pallas_call(
        lambda *refs: None,
        out_shape=jax.ShapeDtypeStruct(array.shape, array.dtype),
        in_specs=[ANY] * (1 + len(others)),
        out_specs=ANY,
        input_output_aliases={0: 0},
        name="after",
    )(array, *others)


def swap(array, axis):
    return lax.all_to_all(array, axis, 0, 0, tiled=True)


def gather(array, axis):
    return lax.all_gather(array, axis, axis=0, tiled=True)


def tie(*arrays):
    return lax.optimization_barrier(arrays)


def per_device(
    tokens, cotangent, lengths, block_map, norm_gain, w_query, w_key, w_value, w_forget,
    forget_bias, w_outgate, w_output, ffn_gain, w_gate, w_up, w_down,
):
    ci = lax.axis_index("ctx").astype(jnp.int32)
    fi = lax.axis_index("fsdp").astype(jnp.int32)
    ids = jnp.stack([ci // 4, lax.rem(ci, 4), fi, lax.rem(ci, 2), ci])
    offsets = jnp.arange(64, dtype=jnp.int32)
    x_own = tokens[0]

    w1r, x_send, c_own = call(
        pack_kernel,
        (shape(8, 208, 896), shape(128, 1536), shape(128, 1536)),
        "pack",
        (
            ids, block_map, lengths, x_own, cotangent[0], w_query, w_key, w_value, w_forget.T,
            jnp.stack([norm_gain, ffn_gain]), w_outgate, w_gate, w_up,
        ),
        ins=[SMEM] * 3 + [VMEM] * 10,
    )
    x_all = gather(x_send, "fsdp")
    near = [c_own] + [
        lax.ppermute(c_own, "fsdp", [(f, (f + 2 * k) % 8) for f in range(8)]) for k in range(1, 4)
    ]
    c_parts = near + [lax.ppermute(p, "fsdp", [(f, f ^ 1) for f in range(8)]) for p in near]
    w1r = swap(w1r, "fsdp")
    bias = jnp.pad(forget_bias.astype(F32), (0, 5))[:, None]
    n1, send, fpre, gains, w1, w2p, wo_own = project(x_all, w1r, bias, w_output)
    wo_all = gather(wo_own, "fsdp")
    w2g = gather(w2p, "ctx").reshape(16, 768, 128)
    recv = swap(send, "ctx")
    sig2 = call(open_kernel, shape(1024, 256, dtype=F32), "open", (n1, w1, near[3]), ins=[VMEM] * 2 + [ANY])

    tri = (offsets[:, None] <= offsets[None, :]).astype(BF16)
    blocks = jnp.arange(32, dtype=jnp.int32)
    pick = (block_map[None, :] == blocks[:, None]).astype(BF16)
    logs = recv[:, 128, 0:256].reshape(16, 2, 2, 64).transpose(0, 2, 1, 3).reshape(32, 128)
    logs = dot(pick, logs).astype(BF16).reshape(32, 2, 64)
    within = jnp.einsum("bht,tu->hbu", logs, tri, preferred_element_type=F32)
    before = (blocks[None, :] < blocks[:, None]).astype(F32)
    starts = jnp.sum(before[None, :, :] * within[:, None, :, 63], -1)
    decay = (within + starts[:, :, None]).reshape(2, 1, SPAN)

    attn_own, attn, log_total = attend(block_map, ids, recv, decay, [wo_all, *near[1:3]])
    attn2 = swap(attn_own, "ctx").reshape(8, 2, 128, 128).transpose(0, 2, 1, 3)
    attn2 = attn2.reshape(1024, 256)
    o2 = (attn2.astype(F32) * sig2).astype(BF16)
    o_own = swap(o2.reshape(8, 128, 256), "fsdp")
    h, n2_own, inv2 = call(
        mid_kernel,
        (shape(128, 1536, dtype=F32), shape(128, 1536), shape(128, 128, dtype=F32)),
        "mid",
        (o_own, wo_all, x_own, gains),
    )
    n2 = gather(n2_own, "fsdp")
    w2, c_all = call(
        ready_kernel,
        (shape(1536, 1024), shape(1024, 1536)),
        "ready",
        (ids, w2g, *c_parts),
        ins=[SMEM] + [VMEM] * 9,
    )
    dn2, ffo, u, dpre = feed_forward(n2, c_all, w2, w_down)
    dn2 = lax.psum_scatter(dn2, "fsdp", scatter_dimension=0, tiled=True)

    fg = call(
        ffn_grad_kernel,
        shape(16, 1152, 128),
        "ffn_grad",
        (n2, dpre, u, c_all),
        flops=5 * 10**9,
    )
    dh, da_own, do_own, gain2_part = call(
        mid_back_kernel,
        (
            shape(128, 1536, dtype=F32),
            shape(128, 1536),
            shape(8, 128, 256),
            shape(1, 1536, dtype=F32),
        ),
        "mid_back",
        (dn2, h, inv2, c_own, gains, wo_all, fg),
        ins=[VMEM] * 6 + [ANY],
    )
    do2 = swap(do_own, "fsdp").reshape(1024, 256)
    da = gather(da_own, "fsdp")
    do2 = do2.astype(F32)
    datt2 = (do2 * sig2).astype(BF16)
    dlog2 = (do2 * attn2.astype(F32) * sig2 * (1.0 - sig2)).astype(BF16)
    datt_send = datt2.reshape(8, 128, 2, 128).transpose(0, 2, 1, 3).reshape(16, 128, 128)
    datt = swap(datt_send, "ctx")
    fg = after(fg, da_own)
    fg_rows = lax.psum_scatter(
        fg.reshape(16 * 1152, 128), "ctx", scatter_dimension=0, tiled=True
    )
    go = call(out_grad_kernel, shape(16, 48, 384), "out_grad", (o2, da))
    dheads = attend_back(block_map, ids, recv, datt, attn, log_total, decay, go)
    dback = swap(dheads, "ctx")
    g1, dproj = call(
        head_grad_kernel,
        (shape(16, 8, 80, 128), shape(1024, 576)),
        "head_grad",
        (n1, dback, dlog2),
        flops=3 * 10**9,
    )
    g1 = swap(g1.reshape(128, 80, 128), BOTH).reshape(16, 8, 80, 128)

    dn1 = call(
        input_grad_kernel,
        shape(8, 272, 1536),
        "input_grad",
        (ids, dproj, dlog2, dback[:, 128, 0:256], fpre, w1, gains, n1, gain2_part, ffo),
        ins=[SMEM] + [VMEM] * 9,
        flops=3 * 10**9,
    )
    cols_g = call(
        split_kernel, (shape(96, 128),) * 8, "split", (ids, fg_rows, dn1), ins=[SMEM, VMEM, ANY]
    )
    cols_g = [cols_g[0]] + [
        lax.ppermute(cols_g[k], "fsdp", [(f, (f + k) % 8) for f in range(8)]) for k in range(1, 8)
    ]
    dn1 = lax.psum_scatter(
        dn1.reshape(8 * 272, 1536), "fsdp", scatter_dimension=0, tiled=True
    )
    total = call(
        head_sum_kernel,
        shape(1936, 128),
        "head_sum",
        (g1, dback[:, 144:192], fg_rows, *cols_g),
        flops=3 * 10**9,
    )
    total, dn1 = tie(total, dn1)
    total = gather(total, "ctx").reshape(16, 1936, 128)

    small = jnp.concatenate([dn1[128:131], dn1[136:141]], 0)
    small = swap(jnp.broadcast_to(small[None], (16, 8, 1536)), "ctx")
    small = call(
        small_sum_kernel, shape(8, 1536, dtype=F32), "small_sum", (small,)
    )
    forget_g = small[0:3].reshape(3, 8, 192).transpose(2, 1, 0).reshape(192, 24)
    tokens_grad = call(finish_kernel, shape(128, 1536), "finish", (dn1, dh, x_own, gains))

    live = (
        lax.dynamic_slice_in_dim(block_map, 2 * ci, 2)[:, None] * 64 + offsets[None, :]
    ).reshape(128) < lengths[0]
    mixed = jnp.where(live[:, None], h + dn1[144:272].astype(F32), 0.0).astype(BF16)
    query_g, key_g, value_g, outgate_g, output_g, gate_g, up_g, down_g = unpack(ids, total)
    return (
        mixed[None], tokens_grad[None], small[3, 0:192], query_g, key_g, value_g, forget_g,
        small[5:8, 0], outgate_g, output_g, small[4, 0:192], gate_g, up_g, down_g,
    )


def solution(mesh):
    act = P("fsdp", "ctx", None)
    vec, mat = P("fsdp"), P("fsdp", None)
    return jax.shard_map(
        per_device,
        mesh=mesh,
        in_specs=(act, act, vec, P(), vec, mat, mat, mat, mat, vec, mat, mat, vec, mat, mat, mat),
        out_specs=(act, act, vec, mat, mat, mat, mat, vec, mat, mat, vec, mat, mat, mat),
        check_vma=False,
    )
```

```python
import jax
import jax.numpy as jnp
from jax import lax
from jax.experimental import pallas as pl
from jax.experimental.pallas import tpu as pltpu
from jax.sharding import PartitionSpec as P

EPS = 1e-06
NEG = -1e30
HD = 64
QB = 256
SPAN = 2048
SHARED = ((0, 3, 4, 7), (1, 2, 5, 6))
F32 = jnp.float32
BF16 = jnp.bfloat16
HIGH = lax.Precision.HIGHEST
NN = (((1,), (0,)), ((), ()))
NT = (((1,), (1,)), ((), ()))
TN = (((0,), (0,)), ((), ()))
MIB = 2**20
SMEM = pl.BlockSpec(memory_space=pltpu.SMEM)
VMEM = pl.BlockSpec(memory_space=pltpu.VMEM)
ANY = pl.BlockSpec(memory_space=pl.ANY)
BOTH = ("ctx", "fsdp")


def dot(a, b, dims=NN):
    return lax.dot_general(a, b, dims, preferred_element_type=F32)


def shape(*dims, dtype=BF16):
    return jax.ShapeDtypeStruct(dims, dtype)


def call(kernel, outs, name, args, scratch=(), ins=None, flops=10**9, moved=10**7, limit=60):
    return pl.pallas_call(
        kernel,
        grid=(1,),
        out_shape=outs,
        in_specs=ins or [VMEM] * len(args),
        out_specs=jax.tree.map(lambda _: VMEM, outs),
        scratch_shapes=list(scratch),
        compiler_params=pltpu.CompilerParams(vmem_limit_bytes=limit * MIB),
        cost_estimate=pl.CostEstimate(flops=flops, bytes_accessed=moved, transcendentals=0),
        name=name,
    )(*args)


def pack_kernel(ids, bm_ref, len_ref, x, cot, wq, wk, wv, wf, gain, wo, wg, wu, out, x_out, c_out):
    row = lax.broadcasted_iota(jnp.int32, (128, 128), 0)
    first, second = bm_ref[2 * ids[4]] * 64, bm_ref[2 * ids[4] + 1] * 64
    pos = row + jnp.where(row < 64, first, second - 64)
    live = jnp.where(pos < len_ref[0], 1.0, 0.0)[:, 0:1]
    x_out[...] = x[...]
    c_out[...] = jnp.where(live > 0.5, cot[...].astype(F32), 0.0).astype(BF16)
    lane = lax.broadcasted_iota(jnp.int32, (192, 64), 1)
    rows = jnp.concatenate(
        [wf[...].astype(F32), gain[...].astype(F32), jnp.zeros((6, 192), F32)], 0
    ).T
    base = jnp.where(lane == 3, rows[:, 24:25], jnp.where(lane == 4, rows[:, 25:26], 0.0))
    for d in range(8):
        parts = []
        for h in range(3):
            at = d * 192 + h * 64
            parts += [wq[:, at : at + 64], wk[:, at : at + 64], wv[:, at : at + 64]]
        ext = base
        for h in range(3):
            ext = jnp.where(lane == h, rows[:, 3 * d + h : 3 * d + h + 1], ext)
        parts.append(ext.astype(BF16))
        heads = [wo[:, d * 192 + h * 64 : d * 192 + h * 64 + 64] for h in range(3)]
        parts += [heads[0], heads[1], heads[1], heads[2]]
        for m in range(7):
            out[d, 0:192, m * 128 : (m + 1) * 128] = jnp.concatenate(
                [parts[2 * m], parts[2 * m + 1]], 1
            )
        out[d, 192:208, 768:896] = jnp.zeros((16, 128), BF16)
    for half in range(2):

        @pl.when(ids[1] // 2 == half)
        def _():
            w = (wg, wu)[half]
            for d in range(8):
                for b in range(6):
                    lt, part = divmod(b, 3)
                    at = pl.multiple_of(ids[0] * 48 + part * 16, 16)
                    col = pl.multiple_of(lax.rem(ids[1], 2) * 256 + (d * 512 + lt * 128), 128)
                    out[d, 192:208, b * 128 : (b + 1) * 128] = w[pl.ds(at, 16), pl.ds(col, 128)]


def open_kernel(n1, w1, _a, sig):
    sig[...] = jax.nn.sigmoid(dot(n1[...], w1[:, 640:896]))


def proj_kernel(x, w1r, bias, wo, n1, send, fpre, gains, w1, w2, wo_out):
    @pl.when(pl.program_id(0) == 0)
    def _():
        for f in range(8):
            w1[f * 192 : (f + 1) * 192, :] = w1r[f, 0:192, :]
            for b in range(6):
                at = f * 96 + b * 16
                w2[at : at + 16, :] = w1r[f, 192:208, b * 128 : (b + 1) * 128]
        wo_out[...] = wo[...]
        gains[...] = w1[:, 512:640].astype(F32).T[64:72]

    x32 = x[...].astype(F32)
    r1 = lax.rsqrt(jnp.mean(x32 * x32, -1, keepdims=True) + EPS)
    normed = (x32 * r1 * gains[3:4]).astype(BF16)
    n1[...] = normed
    proj = dot(normed, w1[:, 0:640])
    rows = proj[:, 512:640].T[64:72] + bias[...]
    fpre[...] = rows
    logs = jnp.minimum(rows, 0.0) - jnp.log1p(jnp.exp(-jnp.abs(rows)))
    low = proj[:, 0:576].astype(BF16)
    for s in range(4):
        for j in range(2):
            send[2 * s + j, 0:128, :] = low[s * 128 : (s + 1) * 128, j * 192 : j * 192 + 384]
            line = jnp.concatenate(
                [
                    logs[j : j + 1, s * 128 : (s + 1) * 128],
                    logs[j + 1 : j + 2, s * 128 : (s + 1) * 128],
                    jnp.zeros((1, 128), F32),
                ],
                1,
            )
            send[2 * s + j, 128:144, :] = jnp.broadcast_to(line, (16, 384)).astype(BF16)


def project(x_all, w1r, bias, wo):
    def fixed(*dims):
        return pl.BlockSpec(dims, lambda i: (0,) * len(dims))

    return pl.pallas_call(
        proj_kernel,
        grid=(2,),
        out_shape=(
            shape(1024, 1536),
            shape(16, 144, 384),
            shape(8, 1024, dtype=F32),
            shape(8, 1536, dtype=F32),
            shape(1536, 896),
            shape(768, 128),
            shape(192, 1536),
        ),
        in_specs=[
            pl.BlockSpec((512, 1536), lambda i: (i, 0)),
            fixed(8, 208, 896),
            fixed(8, 1),
            fixed(192, 1536),
        ],
        out_specs=(
            pl.BlockSpec((512, 1536), lambda i: (i, 0)),
            pl.BlockSpec((8, 144, 384), lambda i: (i, 0, 0)),
            pl.BlockSpec((8, 512), lambda i: (0, i)),
            fixed(8, 1536),
            fixed(1536, 896),
            fixed(768, 128),
            fixed(192, 1536),
        ),
        compiler_params=pltpu.CompilerParams(vmem_limit_bytes=60 * MIB),
        cost_estimate=pl.CostEstimate(
            flops=2 * 10**9, bytes_accessed=10**7, transcendentals=0
        ),
        name="project",
    )(x_all, w1r, bias, wo)


def score_cols(hs, b, q_s, k_s, fc_s, fr):
    n = (b + 1) * QB
    q0 = b * QB
    qq = q_s[hs, q0 : q0 + QB, :]
    cols = dot(k_s[hs, 0:n, :], qq, NT)
    bias = fr[hs, :, q0 : q0 + 1] - fc_s[hs, 0:n, :]
    cols = cols + bias
    keep = lax.broadcasted_iota(jnp.int32, (QB, QB), 0) <= lax.broadcasted_iota(
        jnp.int32, (QB, QB), 1
    )
    tail = jnp.where(keep, cols[n - QB : n], NEG)
    if b:
        cols = jnp.concatenate([cols[: n - QB], tail], 0)
    else:
        cols = tail
    return cols, qq, n, q0


def run_units(j, unit):
    for b in range(SPAN // QB):
        unit(j, b)
    for half in range(2):

        @pl.when(j == half)
        def _():
            for b in SHARED[half]:
                unit(1 - half, b)


def load_heads(bm_ref, r1, q_s, k_s, v_s):
    for blk in range(32):
        at = pl.multiple_of(bm_ref[blk] * 64, 64)
        c, r = divmod(blk, 2)
        for hs in range(2):
            part = r1[c, r * 64 : (r + 1) * 64, hs * 192 : (hs + 1) * 192]
            q_s[hs, pl.ds(at, 64), :] = (part[:, 0:64].astype(F32) * 0.125).astype(BF16)
            k_s[hs, pl.ds(at, 64), :] = part[:, 64:128]
            v_s[hs, pl.ds(at, 64), :] = part[:, 128:192]


def column_decay(fr, fc_s):
    both = jnp.concatenate([fr[0], fr[1], jnp.zeros((6, SPAN), F32)], 0).T
    fc_s[0] = both[:, 0:1]
    fc_s[1] = both[:, 1:2]


def fwd_kernel(bm_ref, ids, r1, fr, _a, o_ref, attn_ref, l_ref, q_s, k_s, v_s, vt_s, fc_s, o_s):
    j = ids[3]
    load_heads(bm_ref, r1, q_s, k_s, v_s)
    column_decay(fr, fc_s)
    for hs in range(2):
        vt_s[hs, 0:64, :] = v_s[hs].astype(F32).T.astype(BF16)
        vt_s[hs, 64:80, :] = jnp.ones((16, SPAN), BF16)
        o_s[hs] = jnp.zeros((SPAN, HD), BF16)

    def unit(hs, b):
        cols, _, n, q0 = score_cols(hs, b, q_s, k_s, fc_s, fr)
        top = jnp.max(cols, 0, keepdims=True)
        probs = jnp.exp(cols - top).astype(BF16)
        acc = dot(vt_s[hs, :, 0:n], probs)
        total = acc[64:65]
        rows = (acc[0:64] / total).T
        attn_ref[hs, q0 : q0 + QB, :] = rows
        l_ref[hs, :, q0 : q0 + QB] = top + jnp.log(total)
        o_s[hs, q0 : q0 + QB, :] = rows.astype(BF16)

    run_units(j, unit)
    for blk in range(32):
        at = pl.multiple_of(bm_ref[blk] * 64, 64)
        c, r = divmod(blk, 2)
        o_ref[c, r * 64 : (r + 1) * 64, :] = jnp.concatenate(
            [o_s[0, pl.ds(at, 64), :], o_s[1, pl.ds(at, 64), :]], 1
        )


def suffix_sums(row, dl_s, hs):
    grid = jnp.concatenate([row[:, b * 64 : (b + 1) * 64] for b in range(32)], 0)
    tri = lax.broadcasted_iota(jnp.int32, (64, 64), 0) >= lax.broadcasted_iota(
        jnp.int32, (64, 64), 1
    )
    within = jnp.dot(grid, tri.astype(F32), precision=HIGH, preferred_element_type=F32)
    total = jnp.broadcast_to(within[:, 0:1], (32, 64))
    later = lax.broadcasted_iota(jnp.int32, (32, 32), 0) < lax.broadcasted_iota(
        jnp.int32, (32, 32), 1
    )
    dl_s[hs] = within + jnp.dot(
        later.astype(F32), total, precision=HIGH, preferred_element_type=F32
    )


def bwd_kernel(
    bm_ref, ids, r1, da_r, attn_ref, l_ref, fr, go,
    ds_ref,
    q_s, k_s, v_s, da_s, kt_s, fc_s, dk_s, dv_s, out_s, rs_ref, dl_s,
):
    j = ids[3]
    for c in range(16):
        ds_ref[c, 144:192, :] = go[c]
    load_heads(bm_ref, r1, q_s, k_s, v_s)
    column_decay(fr, fc_s)
    for blk in range(32):
        at = pl.multiple_of(bm_ref[blk] * 64, 64)
        c, r = divmod(blk, 2)
        part = da_r[c, r * 64 : (r + 1) * 64, :]
        for hs in range(2):
            da_s[hs, pl.ds(at, 64), :] = part[:, hs * 64 : (hs + 1) * 64]
    for hs in range(2):
        kt_s[hs, 0:64, :] = k_s[hs].astype(F32).T.astype(BF16)
        kt_s[hs, 64:80, :] = jnp.ones((16, SPAN), BF16)
        dk_s[hs] = jnp.zeros((SPAN, 128), F32)
        dv_s[hs] = jnp.zeros((SPAN, HD), F32)
        out_s[hs] = jnp.zeros((SPAN, 192), BF16)
        rs_ref[hs] = jnp.zeros((1, SPAN), F32)

    def unit(hs, b):
        cols, qq, n, q0 = score_cols(hs, b, q_s, k_s, fc_s, fr)
        datt = da_s[hs, q0 : q0 + QB, :]
        attn = attn_ref[hs, q0 : q0 + QB, :]
        delta = jnp.sum((datt.astype(F32) * attn).T, 0, keepdims=True)
        probs = jnp.exp(cols - l_ref[hs, :, q0 : q0 + QB])
        dv_s[hs, 0:n, :] += dot(probs.astype(BF16), datt)
        back = dot(v_s[hs, 0:n, :], datt, NT)
        dscore = (probs * (back - delta)).astype(BF16)
        wide = jnp.concatenate([qq, jnp.ones((QB, HD), BF16)], 1)
        dk_s[hs, 0:n, :] += dot(dscore, wide)
        dq = dot(kt_s[hs, :, 0:n], dscore)
        rs_ref[hs, :, q0 : q0 + QB] = dq[64:65]
        out_s[hs, q0 : q0 + QB, 0:64] = (dq[0:64].T * 0.125).astype(BF16)

    run_units(j, unit)
    for hs in range(2):
        both = dk_s[hs]
        suffix_sums(rs_ref[hs] - both.T[64:65], dl_s, hs)
        out_s[hs, :, 64:128] = both[:, 0:64].astype(BF16)
        out_s[hs, :, 128:192] = dv_s[hs].astype(BF16)
    for blk in range(32):
        at = pl.multiple_of(bm_ref[blk] * 64, 64)
        c, r = divmod(blk, 2)
        ds_ref[c, r * 64 : (r + 1) * 64, :] = jnp.concatenate(
            [out_s[0, pl.ds(at, 64), :], out_s[1, pl.ds(at, 64), :]], 1
        )
    for c in range(16):
        lines = [
            dl_s[hs, pl.ds(bm_ref[2 * c + r], 1), :] for hs in range(2) for r in range(2)
        ]
        line = jnp.concatenate(lines + [jnp.zeros((1, 128), F32)], 1)
        ds_ref[c, 128:144, :] = jnp.broadcast_to(line, (16, 384)).astype(BF16)


HEADS = [pltpu.VMEM((2, SPAN, HD), BF16)] * 3


def attend(block_map, ids, r1, decay, after):
    return call(
        fwd_kernel,
        (shape(16, 128, 128), shape(2, SPAN, HD, dtype=F32), shape(2, 1, SPAN, dtype=F32)),
        "attend",
        (block_map, ids, r1, decay, *after),
        HEADS
        + [
            pltpu.VMEM((2, 80, SPAN), BF16),
            pltpu.VMEM((2, SPAN, 1), F32),
            pltpu.VMEM((2, SPAN, HD), BF16),
        ],
        [SMEM, SMEM, VMEM, VMEM, ANY],
        flops=4 * 10**9,
    )


def attend_back(block_map, ids, r1, upstream, attn, logs, decay, go):
    return call(
        bwd_kernel,
        shape(16, 192, 384),
        "attend_back",
        (block_map, ids, r1, upstream, attn, logs, decay, go),
        HEADS
        + [
            pltpu.VMEM((2, SPAN, HD), BF16),
            pltpu.VMEM((2, 80, SPAN), BF16),
            pltpu.VMEM((2, SPAN, 1), F32),
            pltpu.VMEM((2, SPAN, 128), F32),
            pltpu.VMEM((2, SPAN, HD), F32),
            pltpu.VMEM((2, SPAN, 192), BF16),
            pltpu.VMEM((2, 1, SPAN), F32),
            pltpu.VMEM((2, 32, 64), F32),
        ],
        [SMEM, SMEM] + [VMEM] * 6,
        flops=10**10,
    )


def mid_kernel(o_r, wo, x, gains, h_ref, n2_ref, r2_ref):
    acc = x[...].astype(F32)
    for f in range(8):
        at = f * 192
        acc += dot(o_r[f, :, 0:128], wo[at : at + 128, :])
        acc += dot(o_r[f, :, 128:256], wo[at + 64 : at + 192, :])
    h_ref[...] = acc
    r2 = lax.rsqrt(jnp.mean(acc * acc, -1, keepdims=True) + EPS)
    r2_ref[...] = jnp.broadcast_to(r2, (128, 128))
    n2_ref[...] = (acc * r2 * gains[4:5]).astype(BF16)


def mid_back_kernel(
    dn2_r, h_ref, r2_ref, c_ref, gains, wo, _after,
    dh_ref, da_ref, do_ref, g2_ref,
):
    h = h_ref[...]
    r2 = r2_ref[:, 0:1]
    dn2 = dn2_r[:, 0:1536].astype(F32)
    g2_ref[...] = jnp.sum(dn2 * h * r2, 0, keepdims=True)
    scaled = dn2 * gains[4:5]
    dh = (
        c_ref[...].astype(F32)
        + r2 * scaled
        - h * (r2 * r2 * r2) * jnp.mean(scaled * h, -1, keepdims=True)
    )
    dh_ref[...] = dh
    da = dh.astype(BF16)
    da_ref[...] = da
    for f in range(8):
        at = f * 192
        do_ref[f, :, 0:128] = dot(da, wo[at : at + 128, :], NT).astype(BF16)
        do_ref[f, :, 128:256] = dot(da, wo[at + 64 : at + 192, :], NT).astype(BF16)


def ready_kernel(ids, w2g, *refs):
    parts, w2, c_all = refs[:8], refs[8], refs[9]
    for k in range(8):
        first = ids[2] if k < 4 else ids[2] + 1 - 2 * lax.rem(ids[2], 2)
        slot = lax.rem(first + 8 - 2 * (k % 4), 8)
        c_all[pl.ds(pl.multiple_of(slot * 128, 128), 128), :] = parts[k][...]
    for p in range(16):
        cr, cc = divmod(p, 4)
        for f in range(8):
            for lt in range(2):
                row, col = f * 192 + cr * 48, cc * 256 + lt * 128
                at = f * 96 + lt * 48
                w2[row : row + 48, col : col + 128] = w2g[p, at : at + 48, :]


def ffn_kernel(n2, c, w2, wd, both, u_ref, dpre_ref):
    pre = dot(n2[...], w2[...])
    gate, up = pre[:, 0:512], pre[:, 512:1024]
    sig = jax.nn.sigmoid(gate)
    act = gate * sig
    u = (act * up).astype(BF16)
    u_ref[...] = u
    du = dot(c[...], wd[...], NT)
    dgate = (du * up * (sig * (1.0 + gate * (1.0 - sig)))).astype(BF16)
    dup = (du * act).astype(BF16)
    dpre = jnp.concatenate([dgate, dup], 1)
    dpre_ref[...] = dpre
    both[:, 0:1536] = dot(dpre, w2[...], NT).astype(BF16)
    both[:, 1536:3072] = dot(u, wd[...]).astype(BF16)


def feed_forward(n2, c_all, w2, wd):
    rows = 256
    return pl.pallas_call(
        ffn_kernel,
        grid=(1024 // rows,),
        out_shape=(
            shape(1024, 3072),
            shape(1024, 512),
            shape(1024, 1024),
        ),
        in_specs=[
            pl.BlockSpec((rows, 1536), lambda i: (i, 0)),
            pl.BlockSpec((rows, 1536), lambda i: (i, 0)),
            pl.BlockSpec((1536, 1024), lambda i: (0, 0)),
            pl.BlockSpec((512, 1536), lambda i: (0, 0)),
        ],
        out_specs=(
            pl.BlockSpec((rows, 3072), lambda i: (i, 0)),
            pl.BlockSpec((rows, 512), lambda i: (i, 0)),
            pl.BlockSpec((rows, 1024), lambda i: (i, 0)),
        ),
        compiler_params=pltpu.CompilerParams(vmem_limit_bytes=56 * MIB),
        cost_estimate=pl.CostEstimate(
            flops=10**10, bytes_accessed=2 * 10**7, transcendentals=0
        ),
        name="feed_forward",
    )(n2, c_all, w2, wd)


def ffn_grad_kernel(n2, dpre, u, c, out):
    for part in range(4):
        g = dot(n2[:, part * 384 : (part + 1) * 384], dpre[...], TN).astype(BF16)
        for sub in range(2):
            f = 2 * part + sub
            for cr in range(4):
                for col in range(8):
                    cc, half = divmod(col, 2)
                    at = f * 96 + half * 48
                    out[cr * 4 + cc, at : at + 48, :] = g[
                        sub * 192 + cr * 48 : sub * 192 + cr * 48 + 48,
                        col * 128 : (col + 1) * 128,
                    ]
    for part in range(4):
        g = dot(u[:, part * 128 : (part + 1) * 128], c[...], TN).astype(BF16)
        for sub in range(4):
            for col in range(12):
                at = 768 + col * 32
                out[4 * part + sub, at : at + 32, :] = g[
                    sub * 32 : sub * 32 + 32, col * 128 : (col + 1) * 128
                ]


def split_kernel(ids, r, *outs):
    for k in range(8):
        at = pl.multiple_of(lax.rem(ids[2] + k, 8) * 96, 16)
        outs[k][...] = r[pl.ds(at, 96), :]


def out_grad_kernel(ids, o, *refs):
    pieces, out, o_s, da_s = refs[:8], refs[8], refs[9], refs[10]
    for k in range(8):
        first = ids[2] if k < 4 else ids[2] + 1 - 2 * lax.rem(ids[2], 2)
        slot = lax.rem(first + 8 - 2 * (k % 4), 8)
        at = pl.multiple_of(slot * 128, 128)
        o_s[k * 128 : (k + 1) * 128, :] = o[pl.ds(at, 128), :]
        da_s[k * 128 : (k + 1) * 128, :] = pieces[k][...]
    t = dot(o_s[...], da_s[...], TN)
    t = jnp.concatenate([t[0:64], t[64:128] + t[128:192], t[192:256]], 0).astype(BF16)
    for c in range(16):
        cr, cc = divmod(c, 4)
        out[c] = t[cr * 48 : (cr + 1) * 48, cc * 384 : (cc + 1) * 384]


def head_grad_kernel(n1, dback, dlog2, *refs):
    out, dproj = refs[-2:]
    for s in range(8):
        d0, d1 = dback[2 * s], dback[2 * s + 1]
        dproj[s * 128 : (s + 1) * 128, :] = jnp.concatenate(
            [d0[0:128, 0:192], d0[0:128, 192:384] + d1[0:128, 0:192], d1[0:128, 192:384]], 1
        )
    for c in (3, 7, 11, 15):
        out[c] = jnp.zeros((8, 80, 128), BF16)
    for part in range(2):
        left = n1[:, part * 768 : (part + 1) * 768]
        heads = dot(left, dproj[...], TN)
        gate = dot(left, dlog2[...], TN)
        mid = gate[:, 64:128] + gate[:, 128:192]
        g = jnp.concatenate([heads, gate[:, 0:64], mid, gate[:, 192:256]], 1).astype(BF16)
        for sub in range(4):
            f = 4 * part + sub
            for t in range(72):
                rt, lt = divmod(t, 6)
                c, slot = divmod((rt % 3) * 6 + lt, 5)
                c += rt // 3 * 4
                row = sub * 192 + rt * 16
                out[c, f, slot * 16 : (slot + 1) * 16, :] = g[
                    row : row + 16, lt * 128 : (lt + 1) * 128
                ]


def input_grad_kernel(
    ids, dproj, dlog2, dl, fpre, w1, gains, n1, gain2, out
):
    fi = ids[2]
    rows = [[], [], []]
    for s in range(8):
        d0 = dl[2 * s : 2 * s + 1].astype(F32)
        d1 = dl[2 * s + 1 : 2 * s + 2].astype(F32)
        rows[0].append(d0[:, 0:128])
        rows[1].append(d0[:, 128:256] + d1[:, 0:128])
        rows[2].append(d1[:, 128:256])
    dlf = jnp.concatenate(
        [jnp.concatenate(r, 1) for r in rows] + [jnp.zeros((5, 1024), F32)], 0
    )
    is_head = lax.broadcasted_iota(jnp.int32, (8, 1024), 0) < 3
    dfpre = jnp.where(is_head, dlf * jax.nn.sigmoid(-fpre[...]), 0.0).astype(BF16)
    w_forget = gains[...].astype(BF16)
    gain1 = jnp.zeros((1, 1536), F32)
    for p in range(4):
        at = p * 256
        part = (
            dot(dproj[at : at + 256, :], w1[:, 0:576], NT)
            + dot(dlog2[at : at + 256, :], w1[:, 640:896], NT)
            + dot(dfpre[:, at : at + 256], w_forget, TN)
        )
        gain1 += jnp.sum(part * n1[at : at + 256, :].astype(F32), 0, keepdims=True)
        out[2 * p : 2 * p + 2, 0:128, :] = part.astype(BF16).reshape(2, 128, 1536)
    gain1 = gain1 / gains[3:4]
    forget = dot(dfpre, n1[...])
    bias = jnp.sum(dfpre.astype(F32), 1, keepdims=True)
    lane = lax.broadcasted_iota(jnp.int32, (8, 1536), 1)
    mine = (lane >= fi * 192) & (lane < fi * 192 + 192)
    for d in range(8):
        at = d * 192
        top = jnp.concatenate([forget[:, at : at + 192]] * 8, 1)
        top = jnp.where(mine, top, 0.0)
        own = jnp.broadcast_to(bias[0:3], (3, 1536)) * (fi == d).astype(F32)
        low = jnp.concatenate(
            [
                jnp.concatenate([gain1[:, at : at + 192]] * 8, 1),
                jnp.concatenate([gain2[:, at : at + 192]] * 8, 1),
                own,
                jnp.zeros((3, 1536), F32),
            ],
            0,
        )
        out[d, 128:144, :] = jnp.concatenate([top, low], 0).astype(BF16)


def head_sum_kernel(r, go, mine, *refs):
    cols, out = refs[:8], refs[8]
    for k in range(8):
        out[k * 96 : (k + 1) * 96, :] = cols[k][...]
    out[768:1152, :] = mine[768:1152, :]
    for f in range(8):
        acc = r[0, f].astype(F32)
        for c in range(1, 16):
            acc += r[c, f].astype(F32)
        at = 1152 + f * 80
        out[at : at + 80, :] = acc.astype(BF16)
    acc = go[0].astype(F32)
    for c in range(1, 16):
        acc += go[c].astype(F32)
    for lt in range(3):
        at = 1792 + lt * 48
        out[at : at + 48, :] = acc[:, lt * 128 : (lt + 1) * 128].astype(BF16)


def small_sum_kernel(r, out):
    acc = r[0].astype(F32)
    for c in range(1, 16):
        acc += r[c].astype(F32)
    out[...] = acc


def finish_kernel(dn1, dh, x, gains, out):
    x32 = x[...].astype(F32)
    r1 = lax.rsqrt(jnp.mean(x32 * x32, -1, keepdims=True) + EPS)
    scaled = dn1[0:128, :].astype(F32) * gains[3:4]
    out[...] = (
        dh[...]
        + r1 * scaled
        - x32 * (r1 * r1 * r1) * jnp.mean(scaled * x32, -1, keepdims=True)
    ).astype(BF16)


def unpack_kernel(ids, r, q, k, v, g, o, gate, up, down):
    for cc in range(4):
        to = gate if cc < 2 else up
        for d in range(8):
            f = lax.rem(ids[2] + 8 - d, 8)
            for half in range(2):
                at = d * 96 + half * 48
                col = pl.multiple_of(f * 512 + ((cc % 2) * 256 + half * 128), 128)
                to[:, pl.ds(col, 128)] = r[cc, at : at + 48, :].astype(F32)
        for col in range(12):
            at = 768 + col * 32
            down[cc * 32 : (cc + 1) * 32, col * 128 : (col + 1) * 128] = r[
                cc, at : at + 32, :
            ].astype(F32)
        for lt in range(3):
            col = cc * 384 + lt * 128
            o[:, col : col + 128] = r[cc, 1792 + lt * 48 : 1840 + lt * 48, :].astype(F32)
    for rt in range(3):
        rows = [[], [], [], []]
        for f in range(8):
            tiles = []
            for lt in range(6):
                c, slot = divmod(rt * 6 + lt, 5)
                at = 1152 + f * 80 + slot * 16
                tiles.append(r[c, at : at + 16, :].astype(F32))
            line = jnp.concatenate(tiles, 1)
            for h in range(3):
                for w in range(3):
                    at = h * 192 + w * 64
                    rows[w].append(line[:, at : at + 64])
            rows[3].append(line[:, 576:768])
        for w, to in enumerate((q, k, v, g)):
            to[rt * 16 : (rt + 1) * 16, :] = jnp.concatenate(rows[w], 1)


def unpack(ids, total):
    def rows(n, width):
        return shape(4 * n, width, dtype=F32), pl.BlockSpec((n, width), lambda i: (i, 0))

    outs = [rows(48, 1536)] * 5 + [rows(48, 4096)] * 2 + [rows(128, 1536)]
    return pl.pallas_call(
        unpack_kernel,
        grid=(4,),
        out_shape=tuple(a for a, _ in outs),
        in_specs=[SMEM, pl.BlockSpec((4, 1936, 128), lambda i: (i, 0, 0))],
        out_specs=tuple(b for _, b in outs),
        compiler_params=pltpu.CompilerParams(vmem_limit_bytes=60 * MIB),
        cost_estimate=pl.CostEstimate(
            flops=6 * 10**10, bytes_accessed=3 * 10**7, transcendentals=0
        ),
        name="unpack",
    )(ids, total)


def after(array, *others):
    return pl.pallas_call(
        lambda *refs: None,
        out_shape=jax.ShapeDtypeStruct(array.shape, array.dtype),
        in_specs=[ANY] * (1 + len(others)),
        out_specs=ANY,
        input_output_aliases={0: 0},
        name="after",
    )(array, *others)


def swap(array, axis):
    return lax.all_to_all(array, axis, 0, 0, tiled=True)


def gather(array, axis):
    return lax.all_gather(array, axis, axis=0, tiled=True)


def tie(*arrays):
    return lax.optimization_barrier(arrays)


def per_device(
    tokens, cotangent, lengths, block_map, norm_gain, w_query, w_key, w_value, w_forget,
    forget_bias, w_outgate, w_output, ffn_gain, w_gate, w_up, w_down,
):
    ci = lax.axis_index("ctx").astype(jnp.int32)
    fi = lax.axis_index("fsdp").astype(jnp.int32)
    ids = jnp.stack([ci // 4, lax.rem(ci, 4), fi, lax.rem(ci, 2), ci])
    offsets = jnp.arange(64, dtype=jnp.int32)
    x_own = tokens[0]

    w1r, x_send, c_own = call(
        pack_kernel,
        (shape(8, 208, 896), shape(128, 1536), shape(128, 1536)),
        "pack",
        (
            ids, block_map, lengths, x_own, cotangent[0], w_query, w_key, w_value, w_forget.T,
            jnp.stack([norm_gain, ffn_gain]), w_outgate, w_gate, w_up,
        ),
        ins=[SMEM] * 3 + [VMEM] * 10,
    )
    x_all = gather(x_send, "fsdp")
    near = [c_own] + [
        lax.ppermute(c_own, "fsdp", [(f, (f + 2 * k) % 8) for f in range(8)]) for k in range(1, 4)
    ]
    c_parts = near + [lax.ppermute(p, "fsdp", [(f, f ^ 1) for f in range(8)]) for p in near]
    w1r = swap(w1r, "fsdp")
    bias = jnp.pad(forget_bias.astype(F32), (0, 5))[:, None]
    n1, send, fpre, gains, w1, w2p, wo_own = project(x_all, w1r, bias, w_output)
    wo_all = gather(wo_own, "fsdp")
    w2g = gather(w2p, "ctx").reshape(16, 768, 128)
    recv = swap(send, "ctx")
    sig2 = call(open_kernel, shape(1024, 256, dtype=F32), "open", (n1, w1, near[2]), ins=[VMEM] * 2 + [ANY])

    tri = (offsets[:, None] <= offsets[None, :]).astype(BF16)
    blocks = jnp.arange(32, dtype=jnp.int32)
    pick = (block_map[None, :] == blocks[:, None]).astype(BF16)
    logs = recv[:, 128, 0:256].reshape(16, 2, 2, 64).transpose(0, 2, 1, 3).reshape(32, 128)
    logs = dot(pick, logs).astype(BF16).reshape(32, 2, 64)
    within = jnp.einsum("bht,tu->hbu", logs, tri, preferred_element_type=F32)
    before = (blocks[None, :] < blocks[:, None]).astype(F32)
    starts = jnp.sum(before[None, :, :] * within[:, None, :, 63], -1)
    decay = (within + starts[:, :, None]).reshape(2, 1, SPAN)

    attn_own, attn, log_total = attend(block_map, ids, recv, decay, [near[1]])
    attn2 = swap(attn_own, "ctx").reshape(8, 2, 128, 128).transpose(0, 2, 1, 3)
    attn2 = attn2.reshape(1024, 256)
    o2 = (attn2.astype(F32) * sig2).astype(BF16)
    o_own = swap(o2.reshape(8, 128, 256), "fsdp")
    h, n2_own, inv2 = call(
        mid_kernel,
        (shape(128, 1536, dtype=F32), shape(128, 1536), shape(128, 128, dtype=F32)),
        "mid",
        (o_own, wo_all, x_own, gains),
    )
    n2 = gather(n2_own, "fsdp")
    w2, c_all = call(
        ready_kernel,
        (shape(1536, 1024), shape(1024, 1536)),
        "ready",
        (ids, w2g, *c_parts),
        ins=[SMEM] + [VMEM] * 9,
    )
    both, u, dpre = feed_forward(n2, c_all, w2, w_down)
    both = lax.psum_scatter(both, "fsdp", scatter_dimension=0, tiled=True)

    fg = call(
        ffn_grad_kernel,
        shape(16, 1152, 128),
        "ffn_grad",
        (n2, dpre, u, c_all),
        flops=5 * 10**9,
    )
    dh, da_own, do_own, gain2_part = call(
        mid_back_kernel,
        (
            shape(128, 1536, dtype=F32),
            shape(128, 1536),
            shape(8, 128, 256),
            shape(1, 1536, dtype=F32),
        ),
        "mid_back",
        (both, h, inv2, c_own, gains, wo_all, fg),
        ins=[VMEM] * 6 + [ANY],
    )
    do2 = swap(do_own, "fsdp").reshape(1024, 256)
    da_near = [da_own] + [
        lax.ppermute(da_own, "fsdp", [(f, (f + 2 * k) % 8) for f in range(8)])
        for k in range(1, 4)
    ]
    do2 = do2.astype(F32)
    datt2 = (do2 * sig2).astype(BF16)
    dlog2 = (do2 * attn2.astype(F32) * sig2 * (1.0 - sig2)).astype(BF16)
    datt_send = datt2.reshape(8, 128, 2, 128).transpose(0, 2, 1, 3).reshape(16, 128, 128)
    datt = swap(datt_send, "ctx")
    fg = after(fg, da_own)
    fg_rows = lax.psum_scatter(
        fg.reshape(16 * 1152, 128), "ctx", scatter_dimension=0, tiled=True
    )
    da_near = [after(piece, datt_send) for piece in da_near]
    da_far = [lax.ppermute(p, "fsdp", [(f, f ^ 1) for f in range(8)]) for p in da_near]
    go = call(
        out_grad_kernel,
        shape(16, 48, 384),
        "out_grad",
        (ids, o2, *da_near, *da_far),
        [pltpu.VMEM((1024, 256), BF16), pltpu.VMEM((1024, 1536), BF16)],
        [SMEM] + [VMEM] * 9,
    )
    dheads = attend_back(block_map, ids, recv, datt, attn, log_total, decay, go)
    dback = swap(dheads, "ctx")
    cols_g = call(
        split_kernel, (shape(96, 128),) * 8, "split", (ids, fg_rows), ins=[SMEM, VMEM]
    )
    cols_g = [cols_g[0]] + [
        lax.ppermute(cols_g[k], "fsdp", [(f, (f + k) % 8) for f in range(8)]) for k in range(1, 8)
    ]
    g1, dproj = call(
        head_grad_kernel,
        (shape(16, 8, 80, 128), shape(1024, 576)),
        "head_grad",
        (n1, dback, dlog2, *cols_g[1:]),
        ins=[VMEM] * 3 + [ANY] * 7,
        flops=3 * 10**9,
    )
    g1 = swap(g1.reshape(128, 80, 128), BOTH).reshape(16, 8, 80, 128)

    dn1 = call(
        input_grad_kernel,
        shape(8, 144, 1536),
        "input_grad",
        (ids, dproj, dlog2, dback[:, 128, 0:256], fpre, w1, gains, n1, gain2_part),
        ins=[SMEM] + [VMEM] * 8,
        flops=3 * 10**9,
    )
    dn1 = lax.psum_scatter(
        dn1.reshape(8 * 144, 1536), "fsdp", scatter_dimension=0, tiled=True
    )
    total = call(
        head_sum_kernel,
        shape(1936, 128),
        "head_sum",
        (g1, dback[:, 144:192], fg_rows, *cols_g),
        flops=3 * 10**9,
    )
    total, dn1 = tie(total, dn1)
    total = gather(total, "ctx").reshape(16, 1936, 128)

    small = jnp.concatenate([dn1[128:131], dn1[136:141]], 0)
    small = swap(jnp.broadcast_to(small[None], (16, 8, 1536)), "ctx")
    small = call(
        small_sum_kernel, shape(8, 1536, dtype=F32), "small_sum", (small,)
    )
    forget_g = small[0:3].reshape(3, 8, 192).transpose(2, 1, 0).reshape(192, 24)
    tokens_grad = call(finish_kernel, shape(128, 1536), "finish", (dn1, dh, x_own, gains))

    live = (
        lax.dynamic_slice_in_dim(block_map, 2 * ci, 2)[:, None] * 64 + offsets[None, :]
    ).reshape(128) < lengths[0]
    mixed = jnp.where(live[:, None], h + both[:, 1536:3072].astype(F32), 0.0).astype(BF16)
    query_g, key_g, value_g, outgate_g, output_g, gate_g, up_g, down_g = unpack(ids, total)
    return (
        mixed[None], tokens_grad[None], small[3, 0:192], query_g, key_g, value_g, forget_g,
        small[5:8, 0], outgate_g, output_g, small[4, 0:192], gate_g, up_g, down_g,
    )


def solution(mesh):
    act = P("fsdp", "ctx", None)
    vec, mat = P("fsdp"), P("fsdp", None)
    return jax.shard_map(
        per_device,
        mesh=mesh,
        in_specs=(act, act, vec, P(), vec, mat, mat, mat, mat, vec, mat, mat, vec, mat, mat, mat),
        out_specs=(act, act, vec, mat, mat, mat, mat, vec, mat, mat, vec, mat, mat, mat),
        check_vma=False,
    )
```

```python
import jax
import jax.numpy as jnp
from jax import lax
from jax.experimental import pallas as pl
from jax.experimental.pallas import tpu as pltpu
from jax.sharding import PartitionSpec as P

EPS = 1e-06
NEG = -1e30
HD = 64
QB = 256
SPAN = 2048
SHARED = ((0, 3, 4, 7), (1, 2, 5, 6))
F32 = jnp.float32
BF16 = jnp.bfloat16
HIGH = lax.Precision.HIGHEST
NN = (((1,), (0,)), ((), ()))
NT = (((1,), (1,)), ((), ()))
TN = (((0,), (0,)), ((), ()))
MIB = 2**20
SMEM = pl.BlockSpec(memory_space=pltpu.SMEM)
VMEM = pl.BlockSpec(memory_space=pltpu.VMEM)
ANY = pl.BlockSpec(memory_space=pl.ANY)
BOTH = ("ctx", "fsdp")


def dot(a, b, dims=NN):
    return lax.dot_general(a, b, dims, preferred_element_type=F32)


def shape(*dims, dtype=BF16):
    return jax.ShapeDtypeStruct(dims, dtype)


def call(kernel, outs, name, args, scratch=(), ins=None, flops=10**9, moved=10**7, limit=60):
    return pl.pallas_call(
        kernel,
        grid=(1,),
        out_shape=outs,
        in_specs=ins or [VMEM] * len(args),
        out_specs=jax.tree.map(lambda _: VMEM, outs),
        scratch_shapes=list(scratch),
        compiler_params=pltpu.CompilerParams(vmem_limit_bytes=limit * MIB),
        cost_estimate=pl.CostEstimate(flops=flops, bytes_accessed=moved, transcendentals=0),
        name=name,
    )(*args)


def pack_kernel(ids, bm_ref, len_ref, x, cot, wq, wk, wv, wf, gain, wo, wg, wu, out, x_out, c_out):
    row = lax.broadcasted_iota(jnp.int32, (128, 128), 0)
    first, second = bm_ref[2 * ids[4]] * 64, bm_ref[2 * ids[4] + 1] * 64
    pos = row + jnp.where(row < 64, first, second - 64)
    live = jnp.where(pos < len_ref[0], 1.0, 0.0)[:, 0:1]
    x_out[...] = x[...]
    c_out[...] = jnp.where(live > 0.5, cot[...].astype(F32), 0.0).astype(BF16)
    lane = lax.broadcasted_iota(jnp.int32, (192, 64), 1)
    rows = jnp.concatenate(
        [wf[...].astype(F32), gain[...].astype(F32), jnp.zeros((6, 192), F32)], 0
    ).T
    base = jnp.where(lane == 3, rows[:, 24:25], jnp.where(lane == 4, rows[:, 25:26], 0.0))
    for d in range(8):
        parts = []
        for h in range(3):
            at = d * 192 + h * 64
            parts += [wq[:, at : at + 64], wk[:, at : at + 64], wv[:, at : at + 64]]
        ext = base
        for h in range(3):
            ext = jnp.where(lane == h, rows[:, 3 * d + h : 3 * d + h + 1], ext)
        parts.append(ext.astype(BF16))
        heads = [wo[:, d * 192 + h * 64 : d * 192 + h * 64 + 64] for h in range(3)]
        parts += [heads[0], heads[1], heads[1], heads[2]]
        for m in range(7):
            out[d, 0:192, m * 128 : (m + 1) * 128] = jnp.concatenate(
                [parts[2 * m], parts[2 * m + 1]], 1
            )
        out[d, 192:208, 768:896] = jnp.zeros((16, 128), BF16)
    for half in range(2):

        @pl.when(ids[1] // 2 == half)
        def _():
            w = (wg, wu)[half]
            for d in range(8):
                for b in range(6):
                    lt, part = divmod(b, 3)
                    at = pl.multiple_of(ids[0] * 48 + part * 16, 16)
                    col = pl.multiple_of(lax.rem(ids[1], 2) * 256 + (d * 512 + lt * 128), 128)
                    out[d, 192:208, b * 128 : (b + 1) * 128] = w[pl.ds(at, 16), pl.ds(col, 128)]


def open_kernel(n1, w1, sig):
    sig[...] = jax.nn.sigmoid(dot(n1[...], w1[:, 640:896]))


def proj_kernel(x, w1r, bias, wo, n1, send, fpre, gains, w1, w2, wo_out):
    @pl.when(pl.program_id(0) == 0)
    def _():
        for f in range(8):
            w1[f * 192 : (f + 1) * 192, :] = w1r[f, 0:192, :]
            for b in range(6):
                at = f * 96 + b * 16
                w2[at : at + 16, :] = w1r[f, 192:208, b * 128 : (b + 1) * 128]
        wo_out[...] = wo[...]
        gains[...] = w1[:, 512:640].astype(F32).T[64:72]

    x32 = x[...].astype(F32)
    r1 = lax.rsqrt(jnp.mean(x32 * x32, -1, keepdims=True) + EPS)
    normed = (x32 * r1 * gains[3:4]).astype(BF16)
    n1[...] = normed
    proj = dot(normed, w1[:, 0:640])
    rows = proj[:, 512:640].T[64:72] + bias[...]
    fpre[...] = rows
    logs = jnp.minimum(rows, 0.0) - jnp.log1p(jnp.exp(-jnp.abs(rows)))
    low = proj[:, 0:576].astype(BF16)
    for s in range(4):
        for j in range(2):
            send[2 * s + j, 0:128, :] = low[s * 128 : (s + 1) * 128, j * 192 : j * 192 + 384]
            line = jnp.concatenate(
                [
                    logs[j : j + 1, s * 128 : (s + 1) * 128],
                    logs[j + 1 : j + 2, s * 128 : (s + 1) * 128],
                    jnp.zeros((1, 128), F32),
                ],
                1,
            )
            send[2 * s + j, 128:144, :] = jnp.broadcast_to(line, (16, 384)).astype(BF16)


def project(x_all, w1r, bias, wo):
    def fixed(*dims):
        return pl.BlockSpec(dims, lambda i: (0,) * len(dims))

    return pl.pallas_call(
        proj_kernel,
        grid=(2,),
        out_shape=(
            shape(1024, 1536),
            shape(16, 144, 384),
            shape(8, 1024, dtype=F32),
            shape(8, 1536, dtype=F32),
            shape(1536, 896),
            shape(768, 128),
            shape(192, 1536),
        ),
        in_specs=[
            pl.BlockSpec((512, 1536), lambda i: (i, 0)),
            fixed(8, 208, 896),
            fixed(8, 1),
            fixed(192, 1536),
        ],
        out_specs=(
            pl.BlockSpec((512, 1536), lambda i: (i, 0)),
            pl.BlockSpec((8, 144, 384), lambda i: (i, 0, 0)),
            pl.BlockSpec((8, 512), lambda i: (0, i)),
            fixed(8, 1536),
            fixed(1536, 896),
            fixed(768, 128),
            fixed(192, 1536),
        ),
        compiler_params=pltpu.CompilerParams(vmem_limit_bytes=60 * MIB),
        cost_estimate=pl.CostEstimate(
            flops=2 * 10**9, bytes_accessed=10**7, transcendentals=0
        ),
        name="project",
    )(x_all, w1r, bias, wo)


def score_cols(hs, b, q_s, k_s, fc_s, fr):
    n = (b + 1) * QB
    q0 = b * QB
    qq = q_s[hs, q0 : q0 + QB, :]
    cols = dot(k_s[hs, 0:n, :], qq, NT)
    bias = fr[hs, :, q0 : q0 + 1] - fc_s[hs, 0:n, :]
    cols = cols + bias
    keep = lax.broadcasted_iota(jnp.int32, (QB, QB), 0) <= lax.broadcasted_iota(
        jnp.int32, (QB, QB), 1
    )
    tail = jnp.where(keep, cols[n - QB : n], NEG)
    if b:
        cols = jnp.concatenate([cols[: n - QB], tail], 0)
    else:
        cols = tail
    return cols, qq, n, q0


def run_units(j, unit):
    for b in range(SPAN // QB):
        unit(j, b)
    for half in range(2):

        @pl.when(j == half)
        def _():
            for b in SHARED[half]:
                unit(1 - half, b)


def load_heads(bm_ref, r1, q_s, k_s, v_s):
    for blk in range(32):
        at = pl.multiple_of(bm_ref[blk] * 64, 64)
        c, r = divmod(blk, 2)
        for hs in range(2):
            part = r1[c, r * 64 : (r + 1) * 64, hs * 192 : (hs + 1) * 192]
            q_s[hs, pl.ds(at, 64), :] = (part[:, 0:64].astype(F32) * 0.125).astype(BF16)
            k_s[hs, pl.ds(at, 64), :] = part[:, 64:128]
            v_s[hs, pl.ds(at, 64), :] = part[:, 128:192]


def column_decay(fr, fc_s):
    both = jnp.concatenate([fr[0], fr[1], jnp.zeros((6, SPAN), F32)], 0).T
    fc_s[0] = both[:, 0:1]
    fc_s[1] = both[:, 1:2]


def fwd_kernel(bm_ref, ids, r1, fr, _a, o_ref, attn_ref, l_ref, q_s, k_s, v_s, vt_s, fc_s, o_s):
    j = ids[3]
    load_heads(bm_ref, r1, q_s, k_s, v_s)
    column_decay(fr, fc_s)
    for hs in range(2):
        vt_s[hs, 0:64, :] = v_s[hs].astype(F32).T.astype(BF16)
        vt_s[hs, 64:80, :] = jnp.ones((16, SPAN), BF16)
        o_s[hs] = jnp.zeros((SPAN, HD), BF16)

    def unit(hs, b):
        cols, _, n, q0 = score_cols(hs, b, q_s, k_s, fc_s, fr)
        top = jnp.max(cols, 0, keepdims=True)
        probs = jnp.exp(cols - top).astype(BF16)
        acc = dot(vt_s[hs, :, 0:n], probs)
        total = acc[64:65]
        rows = (acc[0:64] / total).T
        attn_ref[hs, q0 : q0 + QB, :] = rows
        l_ref[hs, :, q0 : q0 + QB] = top + jnp.log(total)
        o_s[hs, q0 : q0 + QB, :] = rows.astype(BF16)

    run_units(j, unit)
    for blk in range(32):
        at = pl.multiple_of(bm_ref[blk] * 64, 64)
        c, r = divmod(blk, 2)
        o_ref[c, r * 64 : (r + 1) * 64, :] = jnp.concatenate(
            [o_s[0, pl.ds(at, 64), :], o_s[1, pl.ds(at, 64), :]], 1
        )


def suffix_sums(row, dl_s, hs):
    grid = jnp.concatenate([row[:, b * 64 : (b + 1) * 64] for b in range(32)], 0)
    tri = lax.broadcasted_iota(jnp.int32, (64, 64), 0) >= lax.broadcasted_iota(
        jnp.int32, (64, 64), 1
    )
    within = jnp.dot(grid, tri.astype(F32), precision=HIGH, preferred_element_type=F32)
    total = jnp.broadcast_to(within[:, 0:1], (32, 64))
    later = lax.broadcasted_iota(jnp.int32, (32, 32), 0) < lax.broadcasted_iota(
        jnp.int32, (32, 32), 1
    )
    dl_s[hs] = within + jnp.dot(
        later.astype(F32), total, precision=HIGH, preferred_element_type=F32
    )


def bwd_kernel(
    bm_ref, ids, r1, da_r, attn_ref, l_ref, fr, go,
    ds_ref,
    q_s, k_s, v_s, da_s, kt_s, fc_s, dk_s, dv_s, out_s, rs_ref, dl_s,
):
    j = ids[3]
    for c in range(16):
        ds_ref[c, 144:192, :] = go[c]
    load_heads(bm_ref, r1, q_s, k_s, v_s)
    column_decay(fr, fc_s)
    for blk in range(32):
        at = pl.multiple_of(bm_ref[blk] * 64, 64)
        c, r = divmod(blk, 2)
        part = da_r[c, r * 64 : (r + 1) * 64, :]
        for hs in range(2):
            da_s[hs, pl.ds(at, 64), :] = part[:, hs * 64 : (hs + 1) * 64]
    for hs in range(2):
        kt_s[hs, 0:64, :] = k_s[hs].astype(F32).T.astype(BF16)
        kt_s[hs, 64:80, :] = jnp.ones((16, SPAN), BF16)
        dk_s[hs] = jnp.zeros((SPAN, 128), F32)
        dv_s[hs] = jnp.zeros((SPAN, HD), F32)
        out_s[hs] = jnp.zeros((SPAN, 192), BF16)
        rs_ref[hs] = jnp.zeros((1, SPAN), F32)

    def unit(hs, b):
        cols, qq, n, q0 = score_cols(hs, b, q_s, k_s, fc_s, fr)
        datt = da_s[hs, q0 : q0 + QB, :]
        attn = attn_ref[hs, q0 : q0 + QB, :]
        delta = jnp.sum((datt.astype(F32) * attn).T, 0, keepdims=True)
        probs = jnp.exp(cols - l_ref[hs, :, q0 : q0 + QB])
        dv_s[hs, 0:n, :] += dot(probs.astype(BF16), datt)
        back = dot(v_s[hs, 0:n, :], datt, NT)
        dscore = (probs * (back - delta)).astype(BF16)
        wide = jnp.concatenate([qq, jnp.ones((QB, HD), BF16)], 1)
        dk_s[hs, 0:n, :] += dot(dscore, wide)
        dq = dot(kt_s[hs, :, 0:n], dscore)
        rs_ref[hs, :, q0 : q0 + QB] = dq[64:65]
        out_s[hs, q0 : q0 + QB, 0:64] = (dq[0:64].T * 0.125).astype(BF16)

    run_units(j, unit)
    for hs in range(2):
        both = dk_s[hs]
        suffix_sums(rs_ref[hs] - both.T[64:65], dl_s, hs)
        out_s[hs, :, 64:128] = both[:, 0:64].astype(BF16)
        out_s[hs, :, 128:192] = dv_s[hs].astype(BF16)
    for blk in range(32):
        at = pl.multiple_of(bm_ref[blk] * 64, 64)
        c, r = divmod(blk, 2)
        ds_ref[c, r * 64 : (r + 1) * 64, :] = jnp.concatenate(
            [out_s[0, pl.ds(at, 64), :], out_s[1, pl.ds(at, 64), :]], 1
        )
    for c in range(16):
        lines = [
            dl_s[hs, pl.ds(bm_ref[2 * c + r], 1), :] for hs in range(2) for r in range(2)
        ]
        line = jnp.concatenate(lines + [jnp.zeros((1, 128), F32)], 1)
        ds_ref[c, 128:144, :] = jnp.broadcast_to(line, (16, 384)).astype(BF16)


HEADS = [pltpu.VMEM((2, SPAN, HD), BF16)] * 3


def attend(block_map, ids, r1, decay, after):
    return call(
        fwd_kernel,
        (shape(16, 128, 128), shape(2, SPAN, HD, dtype=F32), shape(2, 1, SPAN, dtype=F32)),
        "attend",
        (block_map, ids, r1, decay, *after),
        HEADS
        + [
            pltpu.VMEM((2, 80, SPAN), BF16),
            pltpu.VMEM((2, SPAN, 1), F32),
            pltpu.VMEM((2, SPAN, HD), BF16),
        ],
        [SMEM, SMEM, VMEM, VMEM, ANY],
        flops=4 * 10**9,
    )


def attend_back(block_map, ids, r1, upstream, attn, logs, decay, go):
    return call(
        bwd_kernel,
        shape(16, 192, 384),
        "attend_back",
        (block_map, ids, r1, upstream, attn, logs, decay, go),
        HEADS
        + [
            pltpu.VMEM((2, SPAN, HD), BF16),
            pltpu.VMEM((2, 80, SPAN), BF16),
            pltpu.VMEM((2, SPAN, 1), F32),
            pltpu.VMEM((2, SPAN, 128), F32),
            pltpu.VMEM((2, SPAN, HD), F32),
            pltpu.VMEM((2, SPAN, 192), BF16),
            pltpu.VMEM((2, 1, SPAN), F32),
            pltpu.VMEM((2, 32, 64), F32),
        ],
        [SMEM, SMEM] + [VMEM] * 6,
        flops=10**10,
    )


def mid_kernel(o_r, wo, x, gains, h_ref, n2_ref, r2_ref):
    acc = x[...].astype(F32)
    for f in range(8):
        at = f * 192
        acc += dot(o_r[f, :, 0:128], wo[at : at + 128, :])
        acc += dot(o_r[f, :, 128:256], wo[at + 64 : at + 192, :])
    h_ref[...] = acc
    r2 = lax.rsqrt(jnp.mean(acc * acc, -1, keepdims=True) + EPS)
    r2_ref[...] = jnp.broadcast_to(r2, (128, 128))
    n2_ref[...] = (acc * r2 * gains[4:5]).astype(BF16)


def mid_back_kernel(
    dn2_r, h_ref, r2_ref, c_ref, gains, wo, _after,
    dh_ref, da_ref, do_ref, g2_ref,
):
    h = h_ref[...]
    r2 = r2_ref[:, 0:1]
    dn2 = dn2_r[:, 0:1536].astype(F32)
    g2_ref[...] = jnp.sum(dn2 * h * r2, 0, keepdims=True)
    scaled = dn2 * gains[4:5]
    dh = (
        c_ref[...].astype(F32)
        + r2 * scaled
        - h * (r2 * r2 * r2) * jnp.mean(scaled * h, -1, keepdims=True)
    )
    dh_ref[...] = dh
    da = dh.astype(BF16)
    da_ref[...] = da
    for f in range(8):
        at = f * 192
        do_ref[f, :, 0:128] = dot(da, wo[at : at + 128, :], NT).astype(BF16)
        do_ref[f, :, 128:256] = dot(da, wo[at + 64 : at + 192, :], NT).astype(BF16)


def ready_kernel(ids, w2g, *refs):
    parts, w2, c_all = refs[:8], refs[8], refs[9]
    for k in range(8):
        first = ids[2] if k < 4 else ids[2] + 1 - 2 * lax.rem(ids[2], 2)
        slot = lax.rem(first + 8 - 2 * (k % 4), 8)
        c_all[pl.ds(pl.multiple_of(slot * 128, 128), 128), :] = parts[k][...]
    for p in range(16):
        cr, cc = divmod(p, 4)
        for f in range(8):
            for lt in range(2):
                row, col = f * 192 + cr * 48, cc * 256 + lt * 128
                at = f * 96 + lt * 48
                w2[row : row + 48, col : col + 128] = w2g[p, at : at + 48, :]


def ffn_kernel(n2, c, w2, wd, both, u_ref, dpre_ref):
    pre = dot(n2[...], w2[...])
    gate, up = pre[:, 0:512], pre[:, 512:1024]
    sig = jax.nn.sigmoid(gate)
    act = gate * sig
    u = (act * up).astype(BF16)
    u_ref[...] = u
    du = dot(c[...], wd[...], NT)
    dgate = (du * up * (sig * (1.0 + gate * (1.0 - sig)))).astype(BF16)
    dup = (du * act).astype(BF16)
    dpre = jnp.concatenate([dgate, dup], 1)
    dpre_ref[...] = dpre
    both[:, 0:1536] = dot(dpre, w2[...], NT).astype(BF16)
    both[:, 1536:3072] = dot(u, wd[...]).astype(BF16)


def feed_forward(n2, c_all, w2, wd):
    rows = 256
    return pl.pallas_call(
        ffn_kernel,
        grid=(1024 // rows,),
        out_shape=(
            shape(1024, 3072),
            shape(1024, 512),
            shape(1024, 1024),
        ),
        in_specs=[
            pl.BlockSpec((rows, 1536), lambda i: (i, 0)),
            pl.BlockSpec((rows, 1536), lambda i: (i, 0)),
            pl.BlockSpec((1536, 1024), lambda i: (0, 0)),
            pl.BlockSpec((512, 1536), lambda i: (0, 0)),
        ],
        out_specs=(
            pl.BlockSpec((rows, 3072), lambda i: (i, 0)),
            pl.BlockSpec((rows, 512), lambda i: (i, 0)),
            pl.BlockSpec((rows, 1024), lambda i: (i, 0)),
        ),
        compiler_params=pltpu.CompilerParams(vmem_limit_bytes=56 * MIB),
        cost_estimate=pl.CostEstimate(
            flops=10**10, bytes_accessed=2 * 10**7, transcendentals=0
        ),
        name="feed_forward",
    )(n2, c_all, w2, wd)


def ffn_grad_kernel(n2, dpre, u, c, out):
    for part in range(4):
        g = dot(n2[:, part * 384 : (part + 1) * 384], dpre[...], TN).astype(BF16)
        for sub in range(2):
            f = 2 * part + sub
            for cr in range(4):
                for col in range(8):
                    cc, half = divmod(col, 2)
                    at = f * 96 + half * 48
                    out[cr * 4 + cc, at : at + 48, :] = g[
                        sub * 192 + cr * 48 : sub * 192 + cr * 48 + 48,
                        col * 128 : (col + 1) * 128,
                    ]
    for part in range(4):
        g = dot(u[:, part * 128 : (part + 1) * 128], c[...], TN).astype(BF16)
        for sub in range(4):
            for col in range(12):
                at = 768 + col * 32
                out[4 * part + sub, at : at + 32, :] = g[
                    sub * 32 : sub * 32 + 32, col * 128 : (col + 1) * 128
                ]


def split_kernel(ids, r, _after, *outs):
    for k in range(8):
        at = pl.multiple_of(lax.rem(ids[2] + k, 8) * 96, 16)
        outs[k][...] = r[pl.ds(at, 96), :]


def out_grad_kernel(ids, o, *refs):
    pieces, out, o_s, da_s = refs[:8], refs[8], refs[9], refs[10]
    for k in range(8):
        first = ids[2] if k < 4 else ids[2] + 1 - 2 * lax.rem(ids[2], 2)
        slot = lax.rem(first + 8 - 2 * (k % 4), 8)
        at = pl.multiple_of(slot * 128, 128)
        o_s[k * 128 : (k + 1) * 128, :] = o[pl.ds(at, 128), :]
        da_s[k * 128 : (k + 1) * 128, :] = pieces[k][...]
    t = dot(o_s[...], da_s[...], TN)
    t = jnp.concatenate([t[0:64], t[64:128] + t[128:192], t[192:256]], 0).astype(BF16)
    for c in range(16):
        cr, cc = divmod(c, 4)
        out[c] = t[cr * 48 : (cr + 1) * 48, cc * 384 : (cc + 1) * 384]


def head_grad_kernel(n1, dback, dlog2, out, dproj):
    for s in range(8):
        d0, d1 = dback[2 * s], dback[2 * s + 1]
        dproj[s * 128 : (s + 1) * 128, :] = jnp.concatenate(
            [d0[0:128, 0:192], d0[0:128, 192:384] + d1[0:128, 0:192], d1[0:128, 192:384]], 1
        )
    for c in (3, 7, 11, 15):
        out[c] = jnp.zeros((8, 80, 128), BF16)
    for part in range(2):
        left = n1[:, part * 768 : (part + 1) * 768]
        heads = dot(left, dproj[...], TN)
        gate = dot(left, dlog2[...], TN)
        mid = gate[:, 64:128] + gate[:, 128:192]
        g = jnp.concatenate([heads, gate[:, 0:64], mid, gate[:, 192:256]], 1).astype(BF16)
        for sub in range(4):
            f = 4 * part + sub
            for t in range(72):
                rt, lt = divmod(t, 6)
                c, slot = divmod((rt % 3) * 6 + lt, 5)
                c += rt // 3 * 4
                row = sub * 192 + rt * 16
                out[c, f, slot * 16 : (slot + 1) * 16, :] = g[
                    row : row + 16, lt * 128 : (lt + 1) * 128
                ]


def input_grad_kernel(
    ids, dproj, dlog2, dl, fpre, w1, gains, n1, gain2, out
):
    fi = ids[2]
    rows = [[], [], []]
    for s in range(8):
        d0 = dl[2 * s : 2 * s + 1].astype(F32)
        d1 = dl[2 * s + 1 : 2 * s + 2].astype(F32)
        rows[0].append(d0[:, 0:128])
        rows[1].append(d0[:, 128:256] + d1[:, 0:128])
        rows[2].append(d1[:, 128:256])
    dlf = jnp.concatenate(
        [jnp.concatenate(r, 1) for r in rows] + [jnp.zeros((5, 1024), F32)], 0
    )
    is_head = lax.broadcasted_iota(jnp.int32, (8, 1024), 0) < 3
    dfpre = jnp.where(is_head, dlf * jax.nn.sigmoid(-fpre[...]), 0.0).astype(BF16)
    w_forget = gains[...].astype(BF16)
    gain1 = jnp.zeros((1, 1536), F32)
    for p in range(4):
        at = p * 256
        part = (
            dot(dproj[at : at + 256, :], w1[:, 0:576], NT)
            + dot(dlog2[at : at + 256, :], w1[:, 640:896], NT)
            + dot(dfpre[:, at : at + 256], w_forget, TN)
        )
        gain1 += jnp.sum(part * n1[at : at + 256, :].astype(F32), 0, keepdims=True)
        out[2 * p : 2 * p + 2, 0:128, :] = part.astype(BF16).reshape(2, 128, 1536)
    gain1 = gain1 / gains[3:4]
    forget = dot(dfpre, n1[...])
    bias = jnp.sum(dfpre.astype(F32), 1, keepdims=True)
    lane = lax.broadcasted_iota(jnp.int32, (8, 1536), 1)
    mine = (lane >= fi * 192) & (lane < fi * 192 + 192)
    for d in range(8):
        at = d * 192
        top = jnp.concatenate([forget[:, at : at + 192]] * 8, 1)
        top = jnp.where(mine, top, 0.0)
        own = jnp.broadcast_to(bias[0:3], (3, 1536)) * (fi == d).astype(F32)
        low = jnp.concatenate(
            [
                jnp.concatenate([gain1[:, at : at + 192]] * 8, 1),
                jnp.concatenate([gain2[:, at : at + 192]] * 8, 1),
                own,
                jnp.zeros((3, 1536), F32),
            ],
            0,
        )
        out[d, 128:144, :] = jnp.concatenate([top, low], 0).astype(BF16)


def head_sum_kernel(r, go, mine, *refs):
    cols, out = refs[:8], refs[8]
    for k in range(8):
        out[k * 96 : (k + 1) * 96, :] = cols[k][...]
    out[768:1152, :] = mine[768:1152, :]
    for f in range(8):
        acc = r[0, f].astype(F32)
        for c in range(1, 16):
            acc += r[c, f].astype(F32)
        at = 1152 + f * 80
        out[at : at + 80, :] = acc.astype(BF16)
    acc = go[0].astype(F32)
    for c in range(1, 16):
        acc += go[c].astype(F32)
    for lt in range(3):
        at = 1792 + lt * 48
        out[at : at + 48, :] = acc[:, lt * 128 : (lt + 1) * 128].astype(BF16)


def small_sum_kernel(r, out):
    acc = r[0].astype(F32)
    for c in range(1, 16):
        acc += r[c].astype(F32)
    out[...] = acc


def finish_kernel(dn1, dh, x, gains, out):
    x32 = x[...].astype(F32)
    r1 = lax.rsqrt(jnp.mean(x32 * x32, -1, keepdims=True) + EPS)
    scaled = dn1[0:128, :].astype(F32) * gains[3:4]
    out[...] = (
        dh[...]
        + r1 * scaled
        - x32 * (r1 * r1 * r1) * jnp.mean(scaled * x32, -1, keepdims=True)
    ).astype(BF16)


def unpack_kernel(ids, r, q, k, v, g, o, gate, up, down):
    for cc in range(4):
        to = gate if cc < 2 else up
        for d in range(8):
            f = lax.rem(ids[2] + 8 - d, 8)
            for half in range(2):
                at = d * 96 + half * 48
                col = pl.multiple_of(f * 512 + ((cc % 2) * 256 + half * 128), 128)
                to[:, pl.ds(col, 128)] = r[cc, at : at + 48, :].astype(F32)
        for col in range(12):
            at = 768 + col * 32
            down[cc * 32 : (cc + 1) * 32, col * 128 : (col + 1) * 128] = r[
                cc, at : at + 32, :
            ].astype(F32)
        for lt in range(3):
            col = cc * 384 + lt * 128
            o[:, col : col + 128] = r[cc, 1792 + lt * 48 : 1840 + lt * 48, :].astype(F32)
    for rt in range(3):
        rows = [[], [], [], []]
        for f in range(8):
            tiles = []
            for lt in range(6):
                c, slot = divmod(rt * 6 + lt, 5)
                at = 1152 + f * 80 + slot * 16
                tiles.append(r[c, at : at + 16, :].astype(F32))
            line = jnp.concatenate(tiles, 1)
            for h in range(3):
                for w in range(3):
                    at = h * 192 + w * 64
                    rows[w].append(line[:, at : at + 64])
            rows[3].append(line[:, 576:768])
        for w, to in enumerate((q, k, v, g)):
            to[rt * 16 : (rt + 1) * 16, :] = jnp.concatenate(rows[w], 1)


def unpack(ids, total):
    def rows(n, width):
        return shape(4 * n, width, dtype=F32), pl.BlockSpec((n, width), lambda i: (i, 0))

    outs = [rows(48, 1536)] * 5 + [rows(48, 4096)] * 2 + [rows(128, 1536)]
    return pl.pallas_call(
        unpack_kernel,
        grid=(4,),
        out_shape=tuple(a for a, _ in outs),
        in_specs=[SMEM, pl.BlockSpec((4, 1936, 128), lambda i: (i, 0, 0))],
        out_specs=tuple(b for _, b in outs),
        compiler_params=pltpu.CompilerParams(vmem_limit_bytes=60 * MIB),
        cost_estimate=pl.CostEstimate(
            flops=6 * 10**10, bytes_accessed=3 * 10**7, transcendentals=0
        ),
        name="unpack",
    )(ids, total)


def after(array, *others):
    return pl.pallas_call(
        lambda *refs: None,
        out_shape=jax.ShapeDtypeStruct(array.shape, array.dtype),
        in_specs=[ANY] * (1 + len(others)),
        out_specs=ANY,
        input_output_aliases={0: 0},
        name="after",
    )(array, *others)


def swap(array, axis):
    return lax.all_to_all(array, axis, 0, 0, tiled=True)


def gather(array, axis):
    return lax.all_gather(array, axis, axis=0, tiled=True)


def tie(*arrays):
    return lax.optimization_barrier(arrays)


def per_device(
    tokens, cotangent, lengths, block_map, norm_gain, w_query, w_key, w_value, w_forget,
    forget_bias, w_outgate, w_output, ffn_gain, w_gate, w_up, w_down,
):
    ci = lax.axis_index("ctx").astype(jnp.int32)
    fi = lax.axis_index("fsdp").astype(jnp.int32)
    ids = jnp.stack([ci // 4, lax.rem(ci, 4), fi, lax.rem(ci, 2), ci])
    offsets = jnp.arange(64, dtype=jnp.int32)
    x_own = tokens[0]

    w1r, x_send, c_own = call(
        pack_kernel,
        (shape(8, 208, 896), shape(128, 1536), shape(128, 1536)),
        "pack",
        (
            ids, block_map, lengths, x_own, cotangent[0], w_query, w_key, w_value, w_forget.T,
            jnp.stack([norm_gain, ffn_gain]), w_outgate, w_gate, w_up,
        ),
        ins=[SMEM] * 3 + [VMEM] * 10,
    )
    x_all = gather(x_send, "fsdp")
    near = [c_own] + [
        lax.ppermute(c_own, "fsdp", [(f, (f + 2 * k) % 8) for f in range(8)]) for k in range(1, 4)
    ]
    c_parts = near + [lax.ppermute(p, "fsdp", [(f, f ^ 1) for f in range(8)]) for p in near]
    w1r = swap(w1r, "fsdp")
    bias = jnp.pad(forget_bias.astype(F32), (0, 5))[:, None]
    n1, send, fpre, gains, w1, w2p, wo_own = project(x_all, w1r, bias, w_output)
    wo_all = gather(wo_own, "fsdp")
    w2g = gather(w2p, "ctx").reshape(16, 768, 128)
    recv = swap(send, "ctx")
    sig2 = call(open_kernel, shape(1024, 256, dtype=F32), "open", (n1, w1))

    tri = (offsets[:, None] <= offsets[None, :]).astype(BF16)
    blocks = jnp.arange(32, dtype=jnp.int32)
    pick = (block_map[None, :] == blocks[:, None]).astype(BF16)
    logs = recv[:, 128, 0:256].reshape(16, 2, 2, 64).transpose(0, 2, 1, 3).reshape(32, 128)
    logs = dot(pick, logs).astype(BF16).reshape(32, 2, 64)
    within = jnp.einsum("bht,tu->hbu", logs, tri, preferred_element_type=F32)
    before = (blocks[None, :] < blocks[:, None]).astype(F32)
    starts = jnp.sum(before[None, :, :] * within[:, None, :, 63], -1)
    decay = (within + starts[:, :, None]).reshape(2, 1, SPAN)

    attn_own, attn, log_total = attend(block_map, ids, recv, decay, [near[1]])
    attn2 = swap(attn_own, "ctx").reshape(8, 2, 128, 128).transpose(0, 2, 1, 3)
    attn2 = attn2.reshape(1024, 256)
    o2 = (attn2.astype(F32) * sig2).astype(BF16)
    o_own = swap(o2.reshape(8, 128, 256), "fsdp")
    h, n2_own, inv2 = call(
        mid_kernel,
        (shape(128, 1536, dtype=F32), shape(128, 1536), shape(128, 128, dtype=F32)),
        "mid",
        (o_own, wo_all, x_own, gains),
    )
    n2 = gather(n2_own, "fsdp")
    w2, c_all = call(
        ready_kernel,
        (shape(1536, 1024), shape(1024, 1536)),
        "ready",
        (ids, w2g, *c_parts),
        ins=[SMEM] + [VMEM] * 9,
    )
    both, u, dpre = feed_forward(n2, c_all, w2, w_down)
    both = lax.psum_scatter(both, "fsdp", scatter_dimension=0, tiled=True)

    fg = call(
        ffn_grad_kernel,
        shape(16, 1152, 128),
        "ffn_grad",
        (n2, dpre, u, c_all),
        flops=5 * 10**9,
    )
    dh, da_own, do_own, gain2_part = call(
        mid_back_kernel,
        (
            shape(128, 1536, dtype=F32),
            shape(128, 1536),
            shape(8, 128, 256),
            shape(1, 1536, dtype=F32),
        ),
        "mid_back",
        (both, h, inv2, c_own, gains, wo_all, fg),
        ins=[VMEM] * 6 + [ANY],
    )
    do2 = swap(do_own, "fsdp").reshape(1024, 256)
    da_near = [da_own] + [
        lax.ppermute(da_own, "fsdp", [(f, (f + 2 * k) % 8) for f in range(8)])
        for k in range(1, 4)
    ]
    do2 = do2.astype(F32)
    datt2 = (do2 * sig2).astype(BF16)
    dlog2 = (do2 * attn2.astype(F32) * sig2 * (1.0 - sig2)).astype(BF16)
    datt_send = datt2.reshape(8, 128, 2, 128).transpose(0, 2, 1, 3).reshape(16, 128, 128)
    datt = swap(datt_send, "ctx")
    fg = after(fg, da_own)
    fg_rows = lax.psum_scatter(
        fg.reshape(16 * 1152, 128), "ctx", scatter_dimension=0, tiled=True
    )
    da_near = [after(piece, datt_send) for piece in da_near]
    da_far = [lax.ppermute(p, "fsdp", [(f, f ^ 1) for f in range(8)]) for p in da_near]
    go = call(
        out_grad_kernel,
        shape(16, 48, 384),
        "out_grad",
        (ids, o2, *da_near, *da_far),
        [pltpu.VMEM((1024, 256), BF16), pltpu.VMEM((1024, 1536), BF16)],
        [SMEM] + [VMEM] * 9,
    )
    dheads = attend_back(block_map, ids, recv, datt, attn, log_total, decay, go)
    dback = swap(dheads, "ctx")
    g1, dproj = call(
        head_grad_kernel,
        (shape(16, 8, 80, 128), shape(1024, 576)),
        "head_grad",
        (n1, dback, dlog2),
        flops=3 * 10**9,
    )
    g1 = swap(g1.reshape(128, 80, 128), BOTH).reshape(16, 8, 80, 128)

    dn1 = call(
        input_grad_kernel,
        shape(8, 144, 1536),
        "input_grad",
        (ids, dproj, dlog2, dback[:, 128, 0:256], fpre, w1, gains, n1, gain2_part),
        ins=[SMEM] + [VMEM] * 8,
        flops=3 * 10**9,
    )
    cols_g = call(
        split_kernel, (shape(96, 128),) * 8, "split", (ids, fg_rows, dn1), ins=[SMEM, VMEM, ANY]
    )
    cols_g = [cols_g[0]] + [
        lax.ppermute(cols_g[k], "fsdp", [(f, (f + k) % 8) for f in range(8)]) for k in range(1, 8)
    ]
    dn1 = lax.psum_scatter(
        dn1.reshape(8 * 144, 1536), "fsdp", scatter_dimension=0, tiled=True
    )
    total = call(
        head_sum_kernel,
        shape(1936, 128),
        "head_sum",
        (g1, dback[:, 144:192], fg_rows, *cols_g),
        flops=int(6 * 10**10),
    )
    total, dn1 = tie(total, dn1)
    total = gather(total, "ctx").reshape(16, 1936, 128)

    small = jnp.concatenate([dn1[128:131], dn1[136:141]], 0)
    small = swap(jnp.broadcast_to(small[None], (16, 8, 1536)), "ctx")
    small = call(
        small_sum_kernel, shape(8, 1536, dtype=F32), "small_sum", (small,)
    )
    forget_g = small[0:3].reshape(3, 8, 192).transpose(2, 1, 0).reshape(192, 24)
    tokens_grad = call(finish_kernel, shape(128, 1536), "finish", (dn1, dh, x_own, gains))

    live = (
        lax.dynamic_slice_in_dim(block_map, 2 * ci, 2)[:, None] * 64 + offsets[None, :]
    ).reshape(128) < lengths[0]
    mixed = jnp.where(live[:, None], h + both[:, 1536:3072].astype(F32), 0.0).astype(BF16)
    query_g, key_g, value_g, outgate_g, output_g, gate_g, up_g, down_g = unpack(ids, total)
    return (
        mixed[None], tokens_grad[None], small[3, 0:192], query_g, key_g, value_g, forget_g,
        small[5:8, 0], outgate_g, output_g, small[4, 0:192], gate_g, up_g, down_g,
    )


def solution(mesh):
    act = P("fsdp", "ctx", None)
    vec, mat = P("fsdp"), P("fsdp", None)
    return jax.shard_map(
        per_device,
        mesh=mesh,
        in_specs=(act, act, vec, P(), vec, mat, mat, mat, mat, vec, mat, mat, vec, mat, mat, mat),
        out_specs=(act, act, vec, mat, mat, mat, mat, vec, mat, mat, vec, mat, mat, mat),
        check_vma=False,
    )
```

```python
import jax
import jax.numpy as jnp
from jax import lax
from jax.experimental import pallas as pl
from jax.experimental.pallas import tpu as pltpu
from jax.sharding import PartitionSpec as P

EPS = 1e-06
NEG = -1e30
HD = 64
QB = 256
SPAN = 2048
SHARED = ((0, 3, 4, 7), (1, 2, 5, 6))
F32 = jnp.float32
BF16 = jnp.bfloat16
HIGH = lax.Precision.HIGHEST
NN = (((1,), (0,)), ((), ()))
NT = (((1,), (1,)), ((), ()))
TN = (((0,), (0,)), ((), ()))
MIB = 2**20
SMEM = pl.BlockSpec(memory_space=pltpu.SMEM)
VMEM = pl.BlockSpec(memory_space=pltpu.VMEM)
ANY = pl.BlockSpec(memory_space=pl.ANY)
BOTH = ("ctx", "fsdp")


def dot(a, b, dims=NN):
    return lax.dot_general(a, b, dims, preferred_element_type=F32)


def shape(*dims, dtype=BF16):
    return jax.ShapeDtypeStruct(dims, dtype)


def call(kernel, outs, name, args, scratch=(), ins=None, flops=10**9, moved=10**7, limit=60):
    return pl.pallas_call(
        kernel,
        grid=(1,),
        out_shape=outs,
        in_specs=ins or [VMEM] * len(args),
        out_specs=jax.tree.map(lambda _: VMEM, outs),
        scratch_shapes=list(scratch),
        compiler_params=pltpu.CompilerParams(vmem_limit_bytes=limit * MIB),
        cost_estimate=pl.CostEstimate(flops=flops, bytes_accessed=moved, transcendentals=0),
        name=name,
    )(*args)


def pack_kernel(ids, bm_ref, len_ref, x, cot, wq, wk, wv, wf, gain, wo, wg, wu, out, x_out, c_out):
    row = lax.broadcasted_iota(jnp.int32, (128, 128), 0)
    first, second = bm_ref[2 * ids[4]] * 64, bm_ref[2 * ids[4] + 1] * 64
    pos = row + jnp.where(row < 64, first, second - 64)
    live = jnp.where(pos < len_ref[0], 1.0, 0.0)[:, 0:1]
    x_out[...] = x[...]
    c_out[...] = jnp.where(live > 0.5, cot[...].astype(F32), 0.0).astype(BF16)
    lane = lax.broadcasted_iota(jnp.int32, (192, 64), 1)
    rows = jnp.concatenate(
        [wf[...].astype(F32), gain[...].astype(F32), jnp.zeros((6, 192), F32)], 0
    ).T
    base = jnp.where(lane == 3, rows[:, 24:25], jnp.where(lane == 4, rows[:, 25:26], 0.0))
    for d in range(8):
        parts = []
        for h in range(3):
            at = d * 192 + h * 64
            parts += [wq[:, at : at + 64], wk[:, at : at + 64], wv[:, at : at + 64]]
        ext = base
        for h in range(3):
            ext = jnp.where(lane == h, rows[:, 3 * d + h : 3 * d + h + 1], ext)
        parts.append(ext.astype(BF16))
        heads = [wo[:, d * 192 + h * 64 : d * 192 + h * 64 + 64] for h in range(3)]
        parts += [heads[0], heads[1], heads[1], heads[2]]
        for m in range(7):
            out[d, 0:192, m * 128 : (m + 1) * 128] = jnp.concatenate(
                [parts[2 * m], parts[2 * m + 1]], 1
            )
        out[d, 192:208, 768:896] = jnp.zeros((16, 128), BF16)
    for half in range(2):

        @pl.when(ids[1] // 2 == half)
        def _():
            w = (wg, wu)[half]
            for d in range(8):
                for b in range(6):
                    lt, part = divmod(b, 3)
                    at = pl.multiple_of(ids[0] * 48 + part * 16, 16)
                    col = pl.multiple_of(lax.rem(ids[1], 2) * 256 + (d * 512 + lt * 128), 128)
                    out[d, 192:208, b * 128 : (b + 1) * 128] = w[pl.ds(at, 16), pl.ds(col, 128)]


def open_kernel(n1, w1, sig):
    sig[...] = jax.nn.sigmoid(dot(n1[...], w1[:, 640:896]))


def proj_kernel(x, w1r, bias, wo, n1, send, fpre, gains, w1, w2, wo_out):
    @pl.when(pl.program_id(0) == 0)
    def _():
        for f in range(8):
            w1[f * 192 : (f + 1) * 192, :] = w1r[f, 0:192, :]
            for b in range(6):
                at = f * 96 + b * 16
                w2[at : at + 16, :] = w1r[f, 192:208, b * 128 : (b + 1) * 128]
        wo_out[...] = wo[...]
        gains[...] = w1[:, 512:640].astype(F32).T[64:72]

    x32 = x[...].astype(F32)
    r1 = lax.rsqrt(jnp.mean(x32 * x32, -1, keepdims=True) + EPS)
    normed = (x32 * r1 * gains[3:4]).astype(BF16)
    n1[...] = normed
    proj = dot(normed, w1[:, 0:640])
    rows = proj[:, 512:640].T[64:72] + bias[...]
    fpre[...] = rows
    logs = jnp.minimum(rows, 0.0) - jnp.log1p(jnp.exp(-jnp.abs(rows)))
    low = proj[:, 0:576].astype(BF16)
    for s in range(4):
        for j in range(2):
            send[2 * s + j, 0:128, :] = low[s * 128 : (s + 1) * 128, j * 192 : j * 192 + 384]
            line = jnp.concatenate(
                [
                    logs[j : j + 1, s * 128 : (s + 1) * 128],
                    logs[j + 1 : j + 2, s * 128 : (s + 1) * 128],
                    jnp.zeros((1, 128), F32),
                ],
                1,
            )
            send[2 * s + j, 128:144, :] = jnp.broadcast_to(line, (16, 384)).astype(BF16)


def project(x_all, w1r, bias, wo):
    def fixed(*dims):
        return pl.BlockSpec(dims, lambda i: (0,) * len(dims))

    return pl.pallas_call(
        proj_kernel,
        grid=(2,),
        out_shape=(
            shape(1024, 1536),
            shape(16, 144, 384),
            shape(8, 1024, dtype=F32),
            shape(8, 1536, dtype=F32),
            shape(1536, 896),
            shape(768, 128),
            shape(192, 1536),
        ),
        in_specs=[
            pl.BlockSpec((512, 1536), lambda i: (i, 0)),
            fixed(8, 208, 896),
            fixed(8, 1),
            fixed(192, 1536),
        ],
        out_specs=(
            pl.BlockSpec((512, 1536), lambda i: (i, 0)),
            pl.BlockSpec((8, 144, 384), lambda i: (i, 0, 0)),
            pl.BlockSpec((8, 512), lambda i: (0, i)),
            fixed(8, 1536),
            fixed(1536, 896),
            fixed(768, 128),
            fixed(192, 1536),
        ),
        compiler_params=pltpu.CompilerParams(vmem_limit_bytes=60 * MIB),
        cost_estimate=pl.CostEstimate(
            flops=2 * 10**9, bytes_accessed=10**7, transcendentals=0
        ),
        name="project",
    )(x_all, w1r, bias, wo)


def score_cols(hs, b, q_s, k_s, fc_s, fr):
    n = (b + 1) * QB
    q0 = b * QB
    qq = q_s[hs, q0 : q0 + QB, :]
    cols = dot(k_s[hs, 0:n, :], qq, NT)
    bias = fr[hs, :, q0 : q0 + 1] - fc_s[hs, 0:n, :]
    cols = cols + bias
    keep = lax.broadcasted_iota(jnp.int32, (QB, QB), 0) <= lax.broadcasted_iota(
        jnp.int32, (QB, QB), 1
    )
    tail = jnp.where(keep, cols[n - QB : n], NEG)
    if b:
        cols = jnp.concatenate([cols[: n - QB], tail], 0)
    else:
        cols = tail
    return cols, qq, n, q0


def run_units(j, unit):
    for b in range(SPAN // QB):
        unit(j, b)
    for half in range(2):

        @pl.when(j == half)
        def _():
            for b in SHARED[half]:
                unit(1 - half, b)


def load_heads(bm_ref, r1, q_s, k_s, v_s):
    for blk in range(32):
        at = pl.multiple_of(bm_ref[blk] * 64, 64)
        c, r = divmod(blk, 2)
        for hs in range(2):
            part = r1[c, r * 64 : (r + 1) * 64, hs * 192 : (hs + 1) * 192]
            q_s[hs, pl.ds(at, 64), :] = (part[:, 0:64].astype(F32) * 0.125).astype(BF16)
            k_s[hs, pl.ds(at, 64), :] = part[:, 64:128]
            v_s[hs, pl.ds(at, 64), :] = part[:, 128:192]


def column_decay(fr, fc_s):
    both = jnp.concatenate([fr[0], fr[1], jnp.zeros((6, SPAN), F32)], 0).T
    fc_s[0] = both[:, 0:1]
    fc_s[1] = both[:, 1:2]


def fwd_kernel(bm_ref, ids, r1, fr, _a, o_ref, attn_ref, l_ref, q_s, k_s, v_s, vt_s, fc_s, o_s):
    j = ids[3]
    load_heads(bm_ref, r1, q_s, k_s, v_s)
    column_decay(fr, fc_s)
    for hs in range(2):
        vt_s[hs, 0:64, :] = v_s[hs].astype(F32).T.astype(BF16)
        vt_s[hs, 64:80, :] = jnp.ones((16, SPAN), BF16)
        o_s[hs] = jnp.zeros((SPAN, HD), BF16)

    def unit(hs, b):
        cols, _, n, q0 = score_cols(hs, b, q_s, k_s, fc_s, fr)
        top = jnp.max(cols, 0, keepdims=True)
        probs = jnp.exp(cols - top).astype(BF16)
        acc = dot(vt_s[hs, :, 0:n], probs)
        total = acc[64:65]
        rows = (acc[0:64] / total).T
        attn_ref[hs, q0 : q0 + QB, :] = rows
        l_ref[hs, :, q0 : q0 + QB] = top + jnp.log(total)
        o_s[hs, q0 : q0 + QB, :] = rows.astype(BF16)

    run_units(j, unit)
    for blk in range(32):
        at = pl.multiple_of(bm_ref[blk] * 64, 64)
        c, r = divmod(blk, 2)
        o_ref[c, r * 64 : (r + 1) * 64, :] = jnp.concatenate(
            [o_s[0, pl.ds(at, 64), :], o_s[1, pl.ds(at, 64), :]], 1
        )


def suffix_sums(row, dl_s, hs):
    grid = jnp.concatenate([row[:, b * 64 : (b + 1) * 64] for b in range(32)], 0)
    tri = lax.broadcasted_iota(jnp.int32, (64, 64), 0) >= lax.broadcasted_iota(
        jnp.int32, (64, 64), 1
    )
    within = jnp.dot(grid, tri.astype(F32), precision=HIGH, preferred_element_type=F32)
    total = jnp.broadcast_to(within[:, 0:1], (32, 64))
    later = lax.broadcasted_iota(jnp.int32, (32, 32), 0) < lax.broadcasted_iota(
        jnp.int32, (32, 32), 1
    )
    dl_s[hs] = within + jnp.dot(
        later.astype(F32), total, precision=HIGH, preferred_element_type=F32
    )


def bwd_kernel(
    bm_ref, ids, r1, da_r, attn_ref, l_ref, fr,
    ds_ref,
    q_s, k_s, v_s, da_s, kt_s, fc_s, dk_s, dv_s, out_s, rs_ref, dl_s,
):
    j = ids[3]
    load_heads(bm_ref, r1, q_s, k_s, v_s)
    column_decay(fr, fc_s)
    for blk in range(32):
        at = pl.multiple_of(bm_ref[blk] * 64, 64)
        c, r = divmod(blk, 2)
        part = da_r[c, r * 64 : (r + 1) * 64, :]
        for hs in range(2):
            da_s[hs, pl.ds(at, 64), :] = part[:, hs * 64 : (hs + 1) * 64]
    for hs in range(2):
        kt_s[hs, 0:64, :] = k_s[hs].astype(F32).T.astype(BF16)
        kt_s[hs, 64:80, :] = jnp.ones((16, SPAN), BF16)
        dk_s[hs] = jnp.zeros((SPAN, 128), F32)
        dv_s[hs] = jnp.zeros((SPAN, HD), F32)
        out_s[hs] = jnp.zeros((SPAN, 192), BF16)
        rs_ref[hs] = jnp.zeros((1, SPAN), F32)

    def unit(hs, b):
        cols, qq, n, q0 = score_cols(hs, b, q_s, k_s, fc_s, fr)
        datt = da_s[hs, q0 : q0 + QB, :]
        attn = attn_ref[hs, q0 : q0 + QB, :]
        delta = jnp.sum((datt.astype(F32) * attn).T, 0, keepdims=True)
        probs = jnp.exp(cols - l_ref[hs, :, q0 : q0 + QB])
        dv_s[hs, 0:n, :] += dot(probs.astype(BF16), datt)
        back = dot(v_s[hs, 0:n, :], datt, NT)
        dscore = (probs * (back - delta)).astype(BF16)
        wide = jnp.concatenate([qq, jnp.ones((QB, HD), BF16)], 1)
        dk_s[hs, 0:n, :] += dot(dscore, wide)
        dq = dot(kt_s[hs, :, 0:n], dscore)
        rs_ref[hs, :, q0 : q0 + QB] = dq[64:65]
        out_s[hs, q0 : q0 + QB, 0:64] = (dq[0:64].T * 0.125).astype(BF16)

    run_units(j, unit)
    for hs in range(2):
        both = dk_s[hs]
        suffix_sums(rs_ref[hs] - both.T[64:65], dl_s, hs)
        out_s[hs, :, 64:128] = both[:, 0:64].astype(BF16)
        out_s[hs, :, 128:192] = dv_s[hs].astype(BF16)
    for blk in range(32):
        at = pl.multiple_of(bm_ref[blk] * 64, 64)
        c, r = divmod(blk, 2)
        ds_ref[c, r * 64 : (r + 1) * 64, :] = jnp.concatenate(
            [out_s[0, pl.ds(at, 64), :], out_s[1, pl.ds(at, 64), :]], 1
        )
    for c in range(16):
        lines = [
            dl_s[hs, pl.ds(bm_ref[2 * c + r], 1), :] for hs in range(2) for r in range(2)
        ]
        line = jnp.concatenate(lines + [jnp.zeros((1, 128), F32)], 1)
        ds_ref[c, 128:144, :] = jnp.broadcast_to(line, (16, 384)).astype(BF16)


HEADS = [pltpu.VMEM((2, SPAN, HD), BF16)] * 3


def attend(block_map, ids, r1, decay, after):
    return call(
        fwd_kernel,
        (shape(16, 128, 128), shape(2, SPAN, HD, dtype=F32), shape(2, 1, SPAN, dtype=F32)),
        "attend",
        (block_map, ids, r1, decay, *after),
        HEADS
        + [
            pltpu.VMEM((2, 80, SPAN), BF16),
            pltpu.VMEM((2, SPAN, 1), F32),
            pltpu.VMEM((2, SPAN, HD), BF16),
        ],
        [SMEM, SMEM, VMEM, VMEM, ANY],
        flops=4 * 10**9,
    )


def attend_back(block_map, ids, r1, upstream, attn, logs, decay):
    return call(
        bwd_kernel,
        shape(16, 144, 384),
        "attend_back",
        (block_map, ids, r1, upstream, attn, logs, decay),
        HEADS
        + [
            pltpu.VMEM((2, SPAN, HD), BF16),
            pltpu.VMEM((2, 80, SPAN), BF16),
            pltpu.VMEM((2, SPAN, 1), F32),
            pltpu.VMEM((2, SPAN, 128), F32),
            pltpu.VMEM((2, SPAN, HD), F32),
            pltpu.VMEM((2, SPAN, 192), BF16),
            pltpu.VMEM((2, 1, SPAN), F32),
            pltpu.VMEM((2, 32, 64), F32),
        ],
        [SMEM, SMEM] + [VMEM] * 5,
        flops=10**10,
    )


def mid_kernel(o_r, wo, x, gains, h_ref, n2_ref, r2_ref):
    acc = x[...].astype(F32)
    for f in range(8):
        at = f * 192
        acc += dot(o_r[f, :, 0:128], wo[at : at + 128, :])
        acc += dot(o_r[f, :, 128:256], wo[at + 64 : at + 192, :])
    h_ref[...] = acc
    r2 = lax.rsqrt(jnp.mean(acc * acc, -1, keepdims=True) + EPS)
    r2_ref[...] = jnp.broadcast_to(r2, (128, 128))
    n2_ref[...] = (acc * r2 * gains[4:5]).astype(BF16)


def mid_back_kernel(
    dn2_r, h_ref, r2_ref, c_ref, gains, wo, _after,
    dh_ref, da_ref, do_ref, g2_ref,
):
    h = h_ref[...]
    r2 = r2_ref[:, 0:1]
    dn2 = dn2_r[:, 0:1536].astype(F32)
    g2_ref[...] = jnp.sum(dn2 * h * r2, 0, keepdims=True)
    scaled = dn2 * gains[4:5]
    dh = (
        c_ref[...].astype(F32)
        + r2 * scaled
        - h * (r2 * r2 * r2) * jnp.mean(scaled * h, -1, keepdims=True)
    )
    dh_ref[...] = dh
    da = dh.astype(BF16)
    da_ref[...] = da
    for f in range(8):
        at = f * 192
        do_ref[f, :, 0:128] = dot(da, wo[at : at + 128, :], NT).astype(BF16)
        do_ref[f, :, 128:256] = dot(da, wo[at + 64 : at + 192, :], NT).astype(BF16)


def ready_kernel(ids, w2g, *refs):
    parts, w2, c_all = refs[:8], refs[8], refs[9]
    for k in range(8):
        first = ids[2] if k < 4 else ids[2] + 1 - 2 * lax.rem(ids[2], 2)
        slot = lax.rem(first + 8 - 2 * (k % 4), 8)
        c_all[pl.ds(pl.multiple_of(slot * 128, 128), 128), :] = parts[k][...]
    for p in range(16):
        cr, cc = divmod(p, 4)
        for f in range(8):
            for lt in range(2):
                row, col = f * 192 + cr * 48, cc * 256 + lt * 128
                at = f * 96 + lt * 48
                w2[row : row + 48, col : col + 128] = w2g[p, at : at + 48, :]


def ffn_kernel(n2, c, w2, wd, both, u_ref, dpre_ref):
    pre = dot(n2[...], w2[...])
    gate, up = pre[:, 0:512], pre[:, 512:1024]
    sig = jax.nn.sigmoid(gate)
    act = gate * sig
    u = (act * up).astype(BF16)
    u_ref[...] = u
    du = dot(c[...], wd[...], NT)
    dgate = (du * up * (sig * (1.0 + gate * (1.0 - sig)))).astype(BF16)
    dup = (du * act).astype(BF16)
    dpre = jnp.concatenate([dgate, dup], 1)
    dpre_ref[...] = dpre
    both[:, 0:1536] = dot(dpre, w2[...], NT).astype(BF16)
    both[:, 1536:3072] = dot(u, wd[...]).astype(BF16)


def feed_forward(n2, c_all, w2, wd):
    rows = 256
    return pl.pallas_call(
        ffn_kernel,
        grid=(1024 // rows,),
        out_shape=(
            shape(1024, 3072),
            shape(1024, 512),
            shape(1024, 1024),
        ),
        in_specs=[
            pl.BlockSpec((rows, 1536), lambda i: (i, 0)),
            pl.BlockSpec((rows, 1536), lambda i: (i, 0)),
            pl.BlockSpec((1536, 1024), lambda i: (0, 0)),
            pl.BlockSpec((512, 1536), lambda i: (0, 0)),
        ],
        out_specs=(
            pl.BlockSpec((rows, 3072), lambda i: (i, 0)),
            pl.BlockSpec((rows, 512), lambda i: (i, 0)),
            pl.BlockSpec((rows, 1024), lambda i: (i, 0)),
        ),
        compiler_params=pltpu.CompilerParams(vmem_limit_bytes=56 * MIB),
        cost_estimate=pl.CostEstimate(
            flops=10**10, bytes_accessed=2 * 10**7, transcendentals=0
        ),
        name="feed_forward",
    )(n2, c_all, w2, wd)


def ffn_grad_kernel(n2, dpre, u, c, out):
    for part in range(4):
        g = dot(n2[:, part * 384 : (part + 1) * 384], dpre[...], TN).astype(BF16)
        for sub in range(2):
            f = 2 * part + sub
            for cr in range(4):
                for col in range(8):
                    cc, half = divmod(col, 2)
                    at = f * 96 + half * 48
                    out[cr * 4 + cc, at : at + 48, :] = g[
                        sub * 192 + cr * 48 : sub * 192 + cr * 48 + 48,
                        col * 128 : (col + 1) * 128,
                    ]
    for part in range(4):
        g = dot(u[:, part * 128 : (part + 1) * 128], c[...], TN).astype(BF16)
        for sub in range(4):
            for col in range(12):
                at = 768 + col * 32
                out[4 * part + sub, at : at + 32, :] = g[
                    sub * 32 : sub * 32 + 32, col * 128 : (col + 1) * 128
                ]


def split_kernel(ids, r, _after, *outs):
    for k in range(8):
        at = pl.multiple_of(lax.rem(ids[2] + k, 8) * 96, 16)
        outs[k][...] = r[pl.ds(at, 96), :]


def out_grad_kernel(ids, _after, o, *refs):
    pieces, out, o_s, da_s = refs[:8], refs[8], refs[9], refs[10]
    for k in range(8):
        first = ids[2] if k < 4 else ids[2] + 1 - 2 * lax.rem(ids[2], 2)
        slot = lax.rem(first + 8 - 2 * (k % 4), 8)
        at = pl.multiple_of(slot * 128, 128)
        o_s[k * 128 : (k + 1) * 128, :] = o[pl.ds(at, 128), :]
        da_s[k * 128 : (k + 1) * 128, :] = pieces[k][...]
    t = dot(o_s[...], da_s[...], TN)
    t = jnp.concatenate([t[0:64], t[64:128] + t[128:192], t[192:256]], 0).astype(BF16)
    for c in range(16):
        cr, cc = divmod(c, 4)
        out[c] = t[cr * 48 : (cr + 1) * 48, cc * 384 : (cc + 1) * 384]


def head_grad_kernel(n1, dback, dlog2, out, dproj):
    for s in range(8):
        d0, d1 = dback[2 * s], dback[2 * s + 1]
        dproj[s * 128 : (s + 1) * 128, :] = jnp.concatenate(
            [d0[0:128, 0:192], d0[0:128, 192:384] + d1[0:128, 0:192], d1[0:128, 192:384]], 1
        )
    for c in (3, 7, 11, 15):
        out[c] = jnp.zeros((8, 80, 128), BF16)
    for part in range(2):
        left = n1[:, part * 768 : (part + 1) * 768]
        heads = dot(left, dproj[...], TN)
        gate = dot(left, dlog2[...], TN)
        mid = gate[:, 64:128] + gate[:, 128:192]
        g = jnp.concatenate([heads, gate[:, 0:64], mid, gate[:, 192:256]], 1).astype(BF16)
        for sub in range(4):
            f = 4 * part + sub
            for t in range(72):
                rt, lt = divmod(t, 6)
                c, slot = divmod((rt % 3) * 6 + lt, 5)
                c += rt // 3 * 4
                row = sub * 192 + rt * 16
                out[c, f, slot * 16 : (slot + 1) * 16, :] = g[
                    row : row + 16, lt * 128 : (lt + 1) * 128
                ]


def input_grad_kernel(
    ids, dproj, dlog2, dl, fpre, w1, gains, n1, gain2, out
):
    fi = ids[2]
    rows = [[], [], []]
    for s in range(8):
        d0 = dl[2 * s : 2 * s + 1].astype(F32)
        d1 = dl[2 * s + 1 : 2 * s + 2].astype(F32)
        rows[0].append(d0[:, 0:128])
        rows[1].append(d0[:, 128:256] + d1[:, 0:128])
        rows[2].append(d1[:, 128:256])
    dlf = jnp.concatenate(
        [jnp.concatenate(r, 1) for r in rows] + [jnp.zeros((5, 1024), F32)], 0
    )
    is_head = lax.broadcasted_iota(jnp.int32, (8, 1024), 0) < 3
    dfpre = jnp.where(is_head, dlf * jax.nn.sigmoid(-fpre[...]), 0.0).astype(BF16)
    w_forget = gains[...].astype(BF16)
    gain1 = jnp.zeros((1, 1536), F32)
    for p in range(4):
        at = p * 256
        part = (
            dot(dproj[at : at + 256, :], w1[:, 0:576], NT)
            + dot(dlog2[at : at + 256, :], w1[:, 640:896], NT)
            + dot(dfpre[:, at : at + 256], w_forget, TN)
        )
        gain1 += jnp.sum(part * n1[at : at + 256, :].astype(F32), 0, keepdims=True)
        out[2 * p : 2 * p + 2, 0:128, :] = part.astype(BF16).reshape(2, 128, 1536)
    gain1 = gain1 / gains[3:4]
    forget = dot(dfpre, n1[...])
    bias = jnp.sum(dfpre.astype(F32), 1, keepdims=True)
    lane = lax.broadcasted_iota(jnp.int32, (8, 1536), 1)
    mine = (lane >= fi * 192) & (lane < fi * 192 + 192)
    for d in range(8):
        at = d * 192
        top = jnp.concatenate([forget[:, at : at + 192]] * 8, 1)
        top = jnp.where(mine, top, 0.0)
        own = jnp.broadcast_to(bias[0:3], (3, 1536)) * (fi == d).astype(F32)
        low = jnp.concatenate(
            [
                jnp.concatenate([gain1[:, at : at + 192]] * 8, 1),
                jnp.concatenate([gain2[:, at : at + 192]] * 8, 1),
                own,
                jnp.zeros((3, 1536), F32),
            ],
            0,
        )
        out[d, 128:144, :] = jnp.concatenate([top, low], 0).astype(BF16)


def head_sum_kernel(r, go, mine, *refs):
    cols, out = refs[:8], refs[8]
    for k in range(8):
        out[k * 96 : (k + 1) * 96, :] = cols[k][...]
    out[768:1152, :] = mine[768:1152, :]
    for f in range(8):
        acc = r[0, f].astype(F32)
        for c in range(1, 16):
            acc += r[c, f].astype(F32)
        at = 1152 + f * 80
        out[at : at + 80, :] = acc.astype(BF16)
    acc = go[0].astype(F32)
    for c in range(1, 16):
        acc += go[c].astype(F32)
    for lt in range(3):
        at = 1792 + lt * 48
        out[at : at + 48, :] = acc[:, lt * 128 : (lt + 1) * 128].astype(BF16)


def small_sum_kernel(r, out):
    acc = r[0].astype(F32)
    for c in range(1, 16):
        acc += r[c].astype(F32)
    out[...] = acc


def finish_kernel(dn1, dh, x, gains, out):
    x32 = x[...].astype(F32)
    r1 = lax.rsqrt(jnp.mean(x32 * x32, -1, keepdims=True) + EPS)
    scaled = dn1[0:128, :].astype(F32) * gains[3:4]
    out[...] = (
        dh[...]
        + r1 * scaled
        - x32 * (r1 * r1 * r1) * jnp.mean(scaled * x32, -1, keepdims=True)
    ).astype(BF16)


def unpack_kernel(ids, r, q, k, v, g, o, gate, up, down):
    for cc in range(4):
        to = gate if cc < 2 else up
        for d in range(8):
            f = lax.rem(ids[2] + 8 - d, 8)
            for half in range(2):
                at = d * 96 + half * 48
                col = pl.multiple_of(f * 512 + ((cc % 2) * 256 + half * 128), 128)
                to[:, pl.ds(col, 128)] = r[cc, at : at + 48, :].astype(F32)
        for col in range(12):
            at = 768 + col * 32
            down[cc * 32 : (cc + 1) * 32, col * 128 : (col + 1) * 128] = r[
                cc, at : at + 32, :
            ].astype(F32)
        for lt in range(3):
            col = cc * 384 + lt * 128
            o[:, col : col + 128] = r[cc, 1792 + lt * 48 : 1840 + lt * 48, :].astype(F32)
    for rt in range(3):
        rows = [[], [], [], []]
        for f in range(8):
            tiles = []
            for lt in range(6):
                c, slot = divmod(rt * 6 + lt, 5)
                at = 1152 + f * 80 + slot * 16
                tiles.append(r[c, at : at + 16, :].astype(F32))
            line = jnp.concatenate(tiles, 1)
            for h in range(3):
                for w in range(3):
                    at = h * 192 + w * 64
                    rows[w].append(line[:, at : at + 64])
            rows[3].append(line[:, 576:768])
        for w, to in enumerate((q, k, v, g)):
            to[rt * 16 : (rt + 1) * 16, :] = jnp.concatenate(rows[w], 1)


def unpack(ids, total):
    def rows(n, width):
        return shape(4 * n, width, dtype=F32), pl.BlockSpec((n, width), lambda i: (i, 0))

    outs = [rows(48, 1536)] * 5 + [rows(48, 4096)] * 2 + [rows(128, 1536)]
    return pl.pallas_call(
        unpack_kernel,
        grid=(4,),
        out_shape=tuple(a for a, _ in outs),
        in_specs=[SMEM, pl.BlockSpec((4, 1936, 128), lambda i: (i, 0, 0))],
        out_specs=tuple(b for _, b in outs),
        compiler_params=pltpu.CompilerParams(vmem_limit_bytes=60 * MIB),
        cost_estimate=pl.CostEstimate(
            flops=6 * 10**10, bytes_accessed=3 * 10**7, transcendentals=0
        ),
        name="unpack",
    )(ids, total)


def after(array, *others):
    return pl.pallas_call(
        lambda *refs: None,
        out_shape=jax.ShapeDtypeStruct(array.shape, array.dtype),
        in_specs=[ANY] * (1 + len(others)),
        out_specs=ANY,
        input_output_aliases={0: 0},
        name="after",
    )(array, *others)


def swap(array, axis):
    return lax.all_to_all(array, axis, 0, 0, tiled=True)


def gather(array, axis):
    return lax.all_gather(array, axis, axis=0, tiled=True)


def tie(*arrays):
    return lax.optimization_barrier(arrays)


def per_device(
    tokens, cotangent, lengths, block_map, norm_gain, w_query, w_key, w_value, w_forget,
    forget_bias, w_outgate, w_output, ffn_gain, w_gate, w_up, w_down,
):
    ci = lax.axis_index("ctx").astype(jnp.int32)
    fi = lax.axis_index("fsdp").astype(jnp.int32)
    ids = jnp.stack([ci // 4, lax.rem(ci, 4), fi, lax.rem(ci, 2), ci])
    offsets = jnp.arange(64, dtype=jnp.int32)
    x_own = tokens[0]

    w1r, x_send, c_own = call(
        pack_kernel,
        (shape(8, 208, 896), shape(128, 1536), shape(128, 1536)),
        "pack",
        (
            ids, block_map, lengths, x_own, cotangent[0], w_query, w_key, w_value, w_forget.T,
            jnp.stack([norm_gain, ffn_gain]), w_outgate, w_gate, w_up,
        ),
        ins=[SMEM] * 3 + [VMEM] * 10,
    )
    x_all = gather(x_send, "fsdp")
    near = [c_own] + [
        lax.ppermute(c_own, "fsdp", [(f, (f + 2 * k) % 8) for f in range(8)]) for k in range(1, 4)
    ]
    c_parts = near + [lax.ppermute(p, "fsdp", [(f, f ^ 1) for f in range(8)]) for p in near]
    w1r = swap(w1r, "fsdp")
    bias = jnp.pad(forget_bias.astype(F32), (0, 5))[:, None]
    n1, send, fpre, gains, w1, w2p, wo_own = project(x_all, w1r, bias, w_output)
    wo_all = gather(wo_own, "fsdp")
    w2g = gather(w2p, "ctx").reshape(16, 768, 128)
    recv = swap(send, "ctx")
    sig2 = call(open_kernel, shape(1024, 256, dtype=F32), "open", (n1, w1))

    tri = (offsets[:, None] <= offsets[None, :]).astype(BF16)
    blocks = jnp.arange(32, dtype=jnp.int32)
    pick = (block_map[None, :] == blocks[:, None]).astype(BF16)
    logs = recv[:, 128, 0:256].reshape(16, 2, 2, 64).transpose(0, 2, 1, 3).reshape(32, 128)
    logs = dot(pick, logs).astype(BF16).reshape(32, 2, 64)
    within = jnp.einsum("bht,tu->hbu", logs, tri, preferred_element_type=F32)
    before = (blocks[None, :] < blocks[:, None]).astype(F32)
    starts = jnp.sum(before[None, :, :] * within[:, None, :, 63], -1)
    decay = (within + starts[:, :, None]).reshape(2, 1, SPAN)

    attn_own, attn, log_total = attend(block_map, ids, recv, decay, [near[1]])
    attn2 = swap(attn_own, "ctx").reshape(8, 2, 128, 128).transpose(0, 2, 1, 3)
    attn2 = attn2.reshape(1024, 256)
    o2 = (attn2.astype(F32) * sig2).astype(BF16)
    o_own = swap(o2.reshape(8, 128, 256), "fsdp")
    h, n2_own, inv2 = call(
        mid_kernel,
        (shape(128, 1536, dtype=F32), shape(128, 1536), shape(128, 128, dtype=F32)),
        "mid",
        (o_own, wo_all, x_own, gains),
    )
    n2 = gather(n2_own, "fsdp")
    w2, c_all = call(
        ready_kernel,
        (shape(1536, 1024), shape(1024, 1536)),
        "ready",
        (ids, w2g, *c_parts),
        ins=[SMEM] + [VMEM] * 9,
    )
    both, u, dpre = feed_forward(n2, c_all, w2, w_down)
    both = lax.psum_scatter(both, "fsdp", scatter_dimension=0, tiled=True)

    fg = call(
        ffn_grad_kernel,
        shape(16, 1152, 128),
        "ffn_grad",
        (n2, dpre, u, c_all),
        flops=5 * 10**9,
    )
    dh, da_own, do_own, gain2_part = call(
        mid_back_kernel,
        (
            shape(128, 1536, dtype=F32),
            shape(128, 1536),
            shape(8, 128, 256),
            shape(1, 1536, dtype=F32),
        ),
        "mid_back",
        (both, h, inv2, c_own, gains, wo_all, fg),
        ins=[VMEM] * 6 + [ANY],
    )
    do2 = swap(do_own, "fsdp").reshape(1024, 256)
    da_near = [da_own] + [
        lax.ppermute(da_own, "fsdp", [(f, (f + 2 * k) % 8) for f in range(8)])
        for k in range(1, 4)
    ]
    do2 = do2.astype(F32)
    datt2 = (do2 * sig2).astype(BF16)
    dlog2 = (do2 * attn2.astype(F32) * sig2 * (1.0 - sig2)).astype(BF16)
    datt_send = datt2.reshape(8, 128, 2, 128).transpose(0, 2, 1, 3).reshape(16, 128, 128)
    datt = swap(datt_send, "ctx")
    fg = after(fg, da_own)
    fg_rows = lax.psum_scatter(
        fg.reshape(16 * 1152, 128), "ctx", scatter_dimension=0, tiled=True
    )
    da_near = [after(piece, datt_send) for piece in da_near]
    da_far = [lax.ppermute(p, "fsdp", [(f, f ^ 1) for f in range(8)]) for p in da_near]
    dheads = attend_back(block_map, ids, recv, datt, attn, log_total, decay)
    dback = swap(dheads, "ctx")
    g1, dproj = call(
        head_grad_kernel,
        (shape(16, 8, 80, 128), shape(1024, 576)),
        "head_grad",
        (n1, dback, dlog2),
        flops=3 * 10**9,
    )
    g1 = swap(g1.reshape(128, 80, 128), BOTH).reshape(16, 8, 80, 128)

    dn1 = call(
        input_grad_kernel,
        shape(8, 144, 1536),
        "input_grad",
        (ids, dproj, dlog2, dback[:, 128, 0:256], fpre, w1, gains, n1, gain2_part),
        ins=[SMEM] + [VMEM] * 8,
        flops=3 * 10**9,
    )
    cols_g = call(
        split_kernel, (shape(96, 128),) * 8, "split", (ids, fg_rows, dn1), ins=[SMEM, VMEM, ANY]
    )
    cols_g = [cols_g[0]] + [
        lax.ppermute(cols_g[k], "fsdp", [(f, (f + k) % 8) for f in range(8)]) for k in range(1, 8)
    ]
    go = call(
        out_grad_kernel,
        shape(16, 48, 384),
        "out_grad",
        (ids, dn1, o2, *da_near, *da_far),
        [pltpu.VMEM((1024, 256), BF16), pltpu.VMEM((1024, 1536), BF16)],
        [SMEM, ANY] + [VMEM] * 9,
    )
    go = swap(after(go, g1), "ctx")
    dn1 = lax.psum_scatter(
        dn1.reshape(8 * 144, 1536), "fsdp", scatter_dimension=0, tiled=True
    )
    total = call(
        head_sum_kernel,
        shape(1936, 128),
        "head_sum",
        (g1, go, fg_rows, *cols_g),
        flops=int(6 * 10**10),
    )
    total, dn1 = tie(total, dn1)
    total = gather(total, "ctx").reshape(16, 1936, 128)

    small = jnp.concatenate([dn1[128:131], dn1[136:141]], 0)
    small = swap(jnp.broadcast_to(small[None], (16, 8, 1536)), "ctx")
    small = call(
        small_sum_kernel, shape(8, 1536, dtype=F32), "small_sum", (small,)
    )
    forget_g = small[0:3].reshape(3, 8, 192).transpose(2, 1, 0).reshape(192, 24)
    tokens_grad = call(finish_kernel, shape(128, 1536), "finish", (dn1, dh, x_own, gains))

    live = (
        lax.dynamic_slice_in_dim(block_map, 2 * ci, 2)[:, None] * 64 + offsets[None, :]
    ).reshape(128) < lengths[0]
    mixed = jnp.where(live[:, None], h + both[:, 1536:3072].astype(F32), 0.0).astype(BF16)
    query_g, key_g, value_g, outgate_g, output_g, gate_g, up_g, down_g = unpack(ids, total)
    return (
        mixed[None], tokens_grad[None], small[3, 0:192], query_g, key_g, value_g, forget_g,
        small[5:8, 0], outgate_g, output_g, small[4, 0:192], gate_g, up_g, down_g,
    )


def solution(mesh):
    act = P("fsdp", "ctx", None)
    vec, mat = P("fsdp"), P("fsdp", None)
    return jax.shard_map(
        per_device,
        mesh=mesh,
        in_specs=(act, act, vec, P(), vec, mat, mat, mat, mat, vec, mat, mat, vec, mat, mat, mat),
        out_specs=(act, act, vec, mat, mat, mat, mat, vec, mat, mat, vec, mat, mat, mat),
        check_vma=False,
    )
```
